32 devices in a mesh: batch: 4 (over y, x), seq: 8 (over z, core).
Axes of the slice: x: 2, y: 2, z: 4, core: 2. Of those that a mesh axis runs over, the one named last changes fastest.
Arguments:
- hidden_in: bfloat16 [16, 1024, 768], P('batch', 'seq'), may hold values from -6 to 6
- positions: int32 [16, 1024], P('batch', 'seq'), may hold values from 0 to 1534, as said below
- cotangent: bfloat16 [16, 1024, 768], P('batch', 'seq'), may hold values from -6 to 6
- norm_gains: float32 [2, 2, 768], replicated, may hold values from 0.5 to 1.5
- norm_biases: float32 [2, 2, 768], replicated, may hold values from -2 to 2
- w_qkv: bfloat16 [768, 896], replicated, may hold values from -0.21875 to 0.21875
- b_qkv: float32 [896], replicated, may hold values from -2 to 2
- w_q2: bfloat16 [768, 768], replicated, may hold values from -0.21875 to 0.21875
- b_q2: float32 [768], replicated, may hold values from -2 to 2
- w_out: bfloat16 [2, 768, 768], replicated, may hold values from -3 to 3
- w_up: bfloat16 [2, 768, 3072], replicated, may hold values from -0.21875 to 0.21875
- b_up: float32 [2, 3072], replicated, may hold values from -2 to 2
- w_down: bfloat16 [2, 3072, 768], replicated, may hold values from -0.109375 to 0.109375
- out_bias: float32 [2, 768], replicated, may hold values from -2 to 2
Outputs:
- hidden_out: bfloat16 [16, 1024, 768], P('batch', 'seq')
- grad_input: float32 [16, 1024, 768], P('batch', 'seq')
- grad_gains: float32 [2, 2, 768], replicated
- grad_biases: float32 [2, 2, 768], replicated
- grad_qkv: float32 [768, 896], replicated
- grad_qkv_bias: float32 [896], replicated
- grad_q2: float32 [768, 768], replicated
- grad_q2_bias: float32 [768], replicated
- grad_out: float32 [2, 768, 768], replicated
- grad_up: float32 [2, 768, 3072], replicated
- grad_up_bias: float32 [2, 3072], replicated
- grad_down: float32 [2, 3072, 768], replicated
- grad_out_bias: float32 [2, 768], replicated
The draws below stay inside these ranges and needn't reach their ends.
Inputs may be any that keep to these rules, and one draw needn't show every extreme that they name: `positions`: in each sequence the first position is 0 and each next one exceeds the one before by 1 or 2, by 2 exactly (1023) // 2 times.
All inputs are finite; a program needn't handle non-finite values.
Results may differ from the reference program's by a relative error of at most 0.025.
Values may be sent and summed in bfloat16 or wider, within the bound.
No kernel may reach another device: no remote copies, remote signals or barrier semaphores. Data moves between devices by JAX's collectives and lax.ppermute only.
A program may use at most 256 MiB of HBM per device.

```python
import jax
import jax.numpy as jnp
from jax import lax

D = 768
H = 12
FF = 3072
HD = 64
ROT = 16
LENGTH = 1024
SEQUENCES = 16


def draw_positions(key, part):
    key = jax.random.fold_in(key, 11)
    steps_count = LENGTH - 1
    doubled = steps_count // 2
    row_keys = jax.random.split(key, SEQUENCES)
    orders = jax.vmap(lambda row_key: jax.random.permutation(row_key, jnp.arange(steps_count, dtype=jnp.int32)))(row_keys)
    increments = 1 + (orders < doubled).astype(jnp.int32)
    starts = jnp.zeros((SEQUENCES, 1), jnp.int32)
    return jnp.concatenate([starts, jnp.cumsum(increments, axis=1)], axis=1).astype(jnp.int32)


def block_scale(stream_key, extent, shards, low, largest):
    gain, own = 1.0, jax.random.fold_in(stream_key, 6)
    for axis_at, blocks in shards:
        draws = jnp.exp(jax.random.uniform(jax.random.fold_in(own, axis_at), (blocks,), jnp.float32, low / len(shards), largest / len(shards)))
        gain = gain * jnp.repeat(draws, extent[axis_at] // blocks).reshape([-1 if axis == axis_at else 1 for axis in range(len(extent))])
    return gain


def normal_values(rng, shape, scale, limit, pieces=(), held_as=jnp.bfloat16):
    loudness = block_scale(rng, shape, pieces, -0.22, 0.18) if pieces else 1.0
    values = jax.random.normal(rng, shape, jnp.float32) * scale * loudness
    return jnp.minimum(jnp.maximum(values, -limit), limit).astype(held_as)


def setup_inputs(seed: int = 0) -> dict:
    seeds = jax.random.split(jax.random.key(seed), 15)
    return {
        "hidden_in": normal_values(seeds[0], (SEQUENCES, LENGTH, D), 1.0, 6.0, ((0, 4), (1, 8))),
        "positions": draw_positions(jax.random.fold_in(seeds[14], 71), 0),
        "cotangent": normal_values(seeds[2], (SEQUENCES, LENGTH, D), 1.0, 6.0, ((0, 4), (1, 8))),
        "norm_gains": jnp.clip(1.0 + 0.1 * jax.random.normal(seeds[3], (2, 2, D), jnp.float32), 0.5, 1.5),
        "norm_biases": normal_values(seeds[4], (2, 2, D), 0.3, 2.0, (), jnp.float32),
        "w_qkv": normal_values(seeds[5], (D, D + 2 * HD), D ** -0.5, 0.21875),
        "b_qkv": normal_values(seeds[6], (D + 2 * HD,), 0.3, 2.0, (), jnp.float32),
        "w_q2": normal_values(seeds[7], (D, D), D ** -0.5, 0.21875),
        "b_q2": normal_values(seeds[8], (D,), 0.3, 2.0, (), jnp.float32),
        "w_out": normal_values(seeds[9], (2, D, D), 4 ** -0.5, 3.0),
        "w_up": normal_values(seeds[10], (2, D, FF), D ** -0.5, 0.21875),
        "b_up": normal_values(seeds[11], (2, FF), 0.3, 2.0, (), jnp.float32),
        "w_down": normal_values(seeds[12], (2, FF, D), FF ** -0.5, 0.109375),
        "out_bias": normal_values(seeds[13], (2, D), 0.3, 2.0, (), jnp.float32),
    }


EPSILON = 1e-05
SCALE = 0.125
NEGATIVE = -1e+30
BASE = 10000.0
HIGHEST = lax.Precision.HIGHEST

@jax.custom_vjp
def low(v):
    return lax.optimization_barrier(v.astype(jnp.bfloat16)).astype(jnp.float32)

@jax.custom_vjp
def low_back(v):
    return v

def low_keep(v):
    return (low(v), None)

def low_pass(kept, grad):
    return (grad,)

def back_keep(v):
    return (v, None)

def back_low(kept, grad):
    return (low(grad),)
low.defvjp(low_keep, low_pass)
low_back.defvjp(back_keep, back_low)

def normalize(values, gain_row, offset):
    center = values - lax.optimization_barrier(jnp.mean(values, axis=-1, keepdims=True))
    spread = lax.optimization_barrier(jnp.mean(center * center, axis=-1, keepdims=True))
    return center * lax.rsqrt(spread + EPSILON) * gain_row + offset

def rotary_tables(positions):
    half_rot = ROT // 2
    inverse = BASE ** (-(jnp.arange(half_rot, dtype=jnp.float32) * 2.0 / ROT))
    angles = positions.astype(jnp.float32)[..., None] * inverse
    return (jnp.cos(angles), jnp.sin(angles))

def rotate(values, cosine_table, sine_table):
    half_rot = ROT // 2
    first_half = values[..., :half_rot]
    second_half = values[..., half_rot:ROT]
    return jnp.concatenate([first_half * cosine_table - second_half * sine_table, second_half * cosine_table + first_half * sine_table, values[..., ROT:]], axis=-1)

def matmul(left, right):
    return jnp.dot(left, right, preferred_element_type=jnp.float32, precision=HIGHEST)

def attention(queries, keys, values_in):
    length = queries.shape[0]
    key_block = min(512, length)
    blocks = queries.reshape(length // key_block, key_block, H, HD)
    starts = jnp.arange(length // key_block, dtype=jnp.int32) * key_block

    def one_block(item):
        query_block, block_start = item
        scores = jnp.einsum('qhd,kd->hqk', query_block, keys, precision=HIGHEST) * SCALE
        scores = low_back(scores)
        allowed = jnp.arange(length, dtype=jnp.int32)[None, :] <= (block_start + jnp.arange(key_block, dtype=jnp.int32))[:, None]
        scores = jnp.where(allowed, scores, NEGATIVE)
        row_top = lax.optimization_barrier(jnp.max(scores, axis=-1, keepdims=True))
        expo = jnp.exp(scores - row_top)
        probs = expo / lax.optimization_barrier(jnp.sum(expo, axis=-1, keepdims=True))
        return jnp.einsum('hqk,kd->qhd', low(probs), values_in, precision=HIGHEST)
    result = lax.map(jax.checkpoint(one_block), (blocks, starts))
    return result.reshape(length, H, HD)

def layer(inputs, cosine_table, sine_table, gains, offsets, w_in, b_in, w_o, w_u, b_u, w_d, bias_out, shared):
    width = inputs.shape[-1]
    norm_attn = low(normalize(inputs, gains[0], offsets[0]))
    norm_mlp = low(normalize(inputs, gains[1], offsets[1]))
    projected = low_back(matmul(norm_attn, w_in) + b_in)
    queries = low(rotate(projected[:, :width].reshape(-1, H, HD), cosine_table[:, None, :], sine_table[:, None, :]))
    if shared is None:
        keys = low(rotate(projected[:, width:width + HD], cosine_table, sine_table))
        values_in = low(projected[:, width + HD:])
        shared = (keys, values_in)
    attended = attention(queries, shared[0], shared[1]).reshape(-1, width)
    attended = low_back(low(attended))
    lifted = low_back(matmul(norm_mlp, w_u) + b_u)
    active = low(jax.nn.gelu(lifted, approximate=False))
    return (inputs + matmul(attended, w_o) + matmul(active, w_d) + bias_out, shared)

def two_layers(inputs, positions, params):
    gains, offsets, w_qkv, b_qkv, w_q2, b_q2, w_out, w_up, b_up, w_down, out_bias = params
    cosine_table, sine_table = rotary_tables(positions)
    first_out, shared = layer(inputs, cosine_table, sine_table, gains[0], offsets[0], w_qkv, b_qkv, w_out[0], w_up[0], b_up[0], w_down[0], out_bias[0], None)
    second_in = low_back(low(first_out))
    second_out, unused = layer(second_in, cosine_table, sine_table, gains[1], offsets[1], w_q2, b_q2, w_out[1], w_up[1], b_up[1], w_down[1], out_bias[1], shared)
    return second_out

def reference(hidden_in, positions, cotangent, norm_gains, norm_biases, w_qkv, b_qkv, w_q2, b_q2, w_out, w_up, b_up, w_down, out_bias):
    params = (norm_gains, norm_biases, w_qkv.astype(jnp.float32), b_qkv, w_q2.astype(jnp.float32), b_q2, w_out.astype(jnp.float32), w_up.astype(jnp.float32), b_up, w_down.astype(jnp.float32), out_bias)
    start_sums = jax.tree.map(jnp.zeros_like, params)

    def step(sums, item):
        seq_in, seq_pos, seq_ct = item
        result, pullback = jax.vjp(lambda given, weights: two_layers(given, seq_pos, weights), seq_in.astype(jnp.float32), params)
        grad_seq, grad_params = pullback(seq_ct.astype(jnp.float32))
        return (jax.tree.map(jnp.add, sums, grad_params), (result.astype(jnp.bfloat16), grad_seq))
    sums, outputs = lax.scan(step, start_sums, (hidden_in, positions, cotangent))
    hidden_out, grad_input = outputs
    return (hidden_out, grad_input, sums[0], sums[1], sums[2], sums[3], sums[4], sums[5], sums[6], sums[7], sums[8], sums[9], sums[10])
```

```python
from functools import partial

import jax
import jax.numpy as jnp
from jax import lax
from jax.experimental import pallas as pl
from jax.experimental.pallas import tpu as pltpu
from jax.sharding import PartitionSpec as P

ROT = 16
EPSILON = 1e-05
SCALE = 0.125
NEGATIVE = -1e30
BASE = 10000.0

B = ("b0", "b1")
Z = "z"
C = "c"
TILE = 768
UNIT = 96
KB = 256

f32 = jnp.float32
bf16 = jnp.bfloat16


def dot_nn(a, b):
    return lax.dot_general(a, b, (((1,), (0,)), ((), ())), preferred_element_type=f32)


def dot_nt(a, b):
    return lax.dot_general(a, b, (((1,), (1,)), ((), ())), preferred_element_type=f32)


def dot_tn(a, b):
    return lax.dot_general(a, b, (((0,), (0,)), ((), ())), preferred_element_type=f32)


def params(limit=50):
    return pltpu.CompilerParams(vmem_limit_bytes=limit << 20)


def cost(flops, moved, transcendentals=0):
    return pl.CostEstimate(
        flops=int(flops), bytes_accessed=int(moved), transcendentals=int(transcendentals)
    )


def vmem(count):
    return [pl.BlockSpec(memory_space=pltpu.VMEM)] * count


def unit_rows(values):
    center = values - jnp.mean(values, axis=-1, keepdims=True)
    spread = jnp.mean(center * center, axis=-1, keepdims=True)
    inverse = lax.rsqrt(spread + EPSILON)
    return center * inverse, inverse


def turn(values, cos_tab, sin_low, sin_high):
    return (
        values * cos_tab
        + pltpu.roll(values, 120, 1) * sin_low
        + pltpu.roll(values, 8, 1) * sin_high
    )


def pairs_down(values):
    return jnp.concatenate(
        [values[:, p * 128 : (p + 1) * 128] for p in range(values.shape[1] // 128)], axis=0
    )


def gelu_parts(lifted):
    cdf = 0.5 * (1.0 + lax.erf(lifted * 0.7071067811865476))
    slope = cdf + lifted * (0.3989422804014327 * jnp.exp(-0.5 * lifted * lifted))
    return lifted * cdf, slope


def first_kernel(x_ref, gain_ref, off_ref, w_ref, b_ref, tab_ref, na_ref, nm_ref, q_ref, kv_ref):
    tokens, width = x_ref.shape
    unit = unit_rows(x_ref[...].astype(f32))[0]
    norm_a = (unit * gain_ref[0:1] + off_ref[0:1]).astype(bf16)
    na_ref[...] = norm_a
    nm_ref[...] = (unit * gain_ref[1:2] + off_ref[1:2]).astype(bf16)
    cos_tab, sin_low, sin_high = tab_ref[0], tab_ref[1], tab_ref[2]
    kv = dot_nn(norm_a, w_ref[:, width:]) + b_ref[:, width:]
    low_half = lax.broadcasted_iota(jnp.int32, kv.shape, 1) < 64
    kv = jnp.where(low_half, turn(kv, cos_tab, sin_low, sin_high), kv).astype(bf16)
    group = kv_ref.shape[0]
    for s in range(tokens // group):
        kv_ref[:, s * 128 : (s + 1) * 128] = kv[s * group : (s + 1) * group]
    proj = dot_nn(norm_a, w_ref[:, :width]) + b_ref[:, :width]
    for p in range(width // 128):
        cols = slice(p * 128, (p + 1) * 128)
        q_ref[:, cols] = (turn(proj[:, cols], cos_tab, sin_low, sin_high) * SCALE).astype(bf16)


def first_call(x, gains, offs, w_qkv, b_qkv, tab, group):
    tokens, width = x.shape
    shape = lambda *s: jax.ShapeDtypeStruct(s, bf16)
    return pl.pallas_call(
        first_kernel,
        out_shape=[
            shape(tokens, width),
            shape(tokens, width),
            shape(tokens, width),
            shape(group, tokens // group * 128),
        ],
        in_specs=vmem(6),
        out_specs=vmem(4),
        compiler_params=params(),
        cost_estimate=cost(2 * tokens * width * (width + 128), 6 << 20),
        name="first",
    )(x, gains, offs, w_qkv, b_qkv.reshape(1, -1), tab)


def mlp_fwd_kernel(nm_ref, up_ref, bup_ref, down_ref, y_ref, act_ref, slope_ref):
    lifted = dot_nn(nm_ref[...], up_ref[0]) + bup_ref[...]
    active, slope = gelu_parts(lifted)
    active = active.astype(bf16)
    act_ref[...] = active
    slope_ref[...] = slope.astype(bf16)

    @pl.when(pl.program_id(0) == 0)
    def _():
        y_ref[...] = jnp.zeros_like(y_ref)

    y_ref[...] += dot_nn(active, down_ref[0])


def mlp_fwd_call(nm, w_up, b_up, w_down, layer):
    tokens, width = nm.shape
    hidden = w_up.shape[2]
    return pl.pallas_call(
        mlp_fwd_kernel,
        grid=(hidden // TILE,),
        in_specs=[
            pl.BlockSpec((tokens, width), lambda t: (0, 0)),
            pl.BlockSpec((1, width, TILE), lambda t: (layer, 0, t)),
            pl.BlockSpec((1, TILE), lambda t: (0, t)),
            pl.BlockSpec((1, TILE, width), lambda t: (layer, t, 0)),
        ],
        out_specs=[
            pl.BlockSpec((tokens, width), lambda t: (0, 0)),
            pl.BlockSpec((tokens, TILE), lambda t: (0, t)),
            pl.BlockSpec((tokens, TILE), lambda t: (0, t)),
        ],
        out_shape=[
            jax.ShapeDtypeStruct((tokens, width), f32),
            jax.ShapeDtypeStruct((tokens, hidden), bf16),
            jax.ShapeDtypeStruct((tokens, hidden), bf16),
        ],
        compiler_params=params(),
        cost_estimate=cost(4 * tokens * width * hidden, 20 << 20, tokens * hidden),
        name="mlp_fwd",
    )(nm, w_up, b_up[layer : layer + 1], w_down)


def mlp_grads(active, slope, nm, grad, up, down, refs, core):
    grad_norm_ref, send_ref, keep_ref, bias_ref = refs
    step = pl.program_id(0)
    half = pl.num_programs(0) // 2
    grad_active = dot_nt(grad, down)
    grad_lifted_wide = grad_active * slope
    grad_lifted = grad_lifted_wide.astype(bf16)
    bias_ref[...] = jnp.sum(grad_lifted.astype(f32), axis=0, keepdims=True)

    @pl.when(step == 0)
    def _():
        grad_norm_ref[...] = jnp.zeros_like(grad_norm_ref)

    grad_norm_ref[...] += dot_nt(grad_lifted, up)
    grad_down = dot_tn(active, grad).astype(bf16)
    grad_up = dot_tn(nm, grad_lifted).astype(bf16)

    def put(ref):
        for j in range(TILE // UNIT):
            rows = slice(j * UNIT, (j + 1) * UNIT)
            ref[0, 2 * j * UNIT : (2 * j + 1) * UNIT] = grad_down[rows]
            ref[0, (2 * j + 1) * UNIT : (2 * j + 2) * UNIT] = grad_up[rows]

    @pl.when(step < half)
    def _():
        put(send_ref)

    @pl.when(step >= half)
    def _():
        put(keep_ref)


def mlp_both_kernel(
    core_ref, nm_ref, g_ref, up_ref, bup_ref, down_ref, y_ref, grad_norm_ref, send_ref, keep_ref, bias_ref
):
    nm, up, down = nm_ref[...], up_ref[0], down_ref[0]
    lifted = dot_nn(nm, up) + bup_ref[...]
    active, slope = gelu_parts(lifted)
    active = active.astype(bf16)

    @pl.when(pl.program_id(0) == 0)
    def _():
        y_ref[...] = jnp.zeros_like(y_ref)

    y_ref[...] += dot_nn(active, down)
    mlp_grads(
        active, slope, nm, g_ref[...], up, down, (grad_norm_ref, send_ref, keep_ref, bias_ref), core_ref
    )


def mlp_back_kernel(
    core_ref, nm_ref, g_ref, up_ref, down_ref, act_ref, slope_ref, grad_norm_ref, send_ref, keep_ref, bias_ref
):
    mlp_grads(
        act_ref[...],
        slope_ref[...].astype(f32),
        nm_ref[...],
        g_ref[...],
        up_ref[0],
        down_ref[0],
        (grad_norm_ref, send_ref, keep_ref, bias_ref),
        core_ref,
    )


def mlp_back_call(core, nm, grad, w_up, w_down, layer, b_up=None, kept=None):
    tokens, width = nm.shape
    hidden = w_up.shape[2]
    tiles = hidden // TILE
    half = tiles // 2

    def tile(t, core_ref):
        c = core_ref[0]
        return jnp.where(t < half, (1 - c) * half + t, c * half + t - half)

    whole = pl.BlockSpec((tokens, width), lambda t, c: (0, 0))
    up_spec = pl.BlockSpec((1, width, TILE), lambda t, c: (layer, 0, tile(t, c)))
    down_spec = pl.BlockSpec((1, TILE, width), lambda t, c: (layer, tile(t, c), 0))
    bias_spec = pl.BlockSpec((1, TILE), lambda t, c: (0, tile(t, c)))
    cols_spec = pl.BlockSpec((tokens, TILE), lambda t, c: (0, tile(t, c)))
    out_specs = [
        whole,
        pl.BlockSpec((1, 2 * TILE, width), lambda t, c: (jnp.minimum(t, half - 1), 0, 0)),
        pl.BlockSpec((1, 2 * TILE, width), lambda t, c: (jnp.maximum(t - half, 0), 0, 0)),
        bias_spec,
    ]
    out_shape = [
        jax.ShapeDtypeStruct((tokens, width), f32),
        jax.ShapeDtypeStruct((half, 2 * TILE, width), bf16),
        jax.ShapeDtypeStruct((half, 2 * TILE, width), bf16),
        jax.ShapeDtypeStruct((1, hidden), f32),
    ]
    if kept is None:
        kernel = mlp_both_kernel
        in_specs = [whole, whole, up_spec, bias_spec, down_spec]
        operands = (nm, grad, w_up, b_up[layer : layer + 1], w_down)
        out_specs = [whole] + out_specs
        out_shape = [jax.ShapeDtypeStruct((tokens, width), f32)] + out_shape
    else:
        kernel = mlp_back_kernel
        in_specs = [whole, whole, up_spec, down_spec, cols_spec, cols_spec]
        operands = (nm, grad, w_up, w_down) + kept
    return pl.pallas_call(
        kernel,
        grid_spec=pltpu.PrefetchScalarGridSpec(
            num_scalar_prefetch=1, grid=(tiles,), in_specs=in_specs, out_specs=out_specs
        ),
        out_shape=out_shape,
        compiler_params=params(),
        cost_estimate=cost((12 if kept is None else 8) * tokens * width * hidden, 25 << 20),
        name="mlp_both" if kept is None else "mlp_back",
    )(core, *operands)


def spread_kv(kv_ref, k0, k1, v0, v1):
    kv = kv_ref[...].astype(f32)
    swapped = pltpu.roll(kv, 64, 1)
    low_half = lax.broadcasted_iota(jnp.int32, kv.shape, 1) < 64
    zero = jnp.zeros_like(kv)
    k0[...] = jnp.where(low_half, kv, zero).astype(bf16)
    k1[...] = jnp.where(low_half, zero, swapped).astype(bf16)
    v0[...] = jnp.where(low_half, swapped, zero).astype(bf16)
    v1[...] = jnp.where(low_half, zero, kv).astype(bf16)


def block_rows(index):
    return pl.ds(pl.multiple_of(index * KB, KB), KB)


def forward_part(first, q6, keys, vals, group):
    full = first // KB

    def scores_of(kb):
        return dot_nt(q6, keys[block_rows(kb), :])

    scores = scores_of(full)
    row = lax.broadcasted_iota(jnp.int32, scores.shape, 0) % group
    col = lax.broadcasted_iota(jnp.int32, scores.shape, 1)
    scores = jnp.where(col - row <= first - full * KB, scores, NEGATIVE)
    top = jnp.max(scores, axis=1, keepdims=True)
    weights = jnp.exp(scores - top)
    total = jnp.sum(weights, axis=1, keepdims=True)
    summed = dot_nn(weights.astype(bf16), vals[block_rows(full), :])

    def step(kb, carry):
        top, total, summed = carry
        scores = scores_of(kb)
        new_top = jnp.maximum(top, jnp.max(scores, axis=1, keepdims=True))
        weights = jnp.exp(scores - new_top)
        factor = jnp.exp(top - new_top)
        total = total * factor + jnp.sum(weights, axis=1, keepdims=True)
        summed = summed * factor + dot_nn(weights.astype(bf16), vals[block_rows(kb), :])
        return new_top, total, summed

    top, total, summed = lax.fori_loop(0, full, step, (top, total, summed))
    return summed / total, top + jnp.log(total)


def attend_kernel(first_ref, q_ref, kv_ref, o_ref, lse_ref, k0, k1, v0, v1):
    first = first_ref[0]
    group = q_ref.shape[0]
    spread_kv(kv_ref, k0, k1, v0, v1)
    q6 = pairs_down(q_ref[...])
    even, even_log = forward_part(first, q6, k0, v0, group)
    odd, odd_log = forward_part(first, q6, k1, v1, group)
    both = (even + odd).astype(bf16)
    for p in range(q_ref.shape[1] // 128):
        o_ref[:, p * 128 : (p + 1) * 128] = both[p * group : (p + 1) * group]
    low_half = lax.broadcasted_iota(jnp.int32, even.shape, 1) < 64
    logs = jnp.where(low_half, even_log, odd_log).T
    lse_ref[0, 0] = logs[0:8]
    lse_ref[0, 1] = logs[64:72]


def attend_call(first, q, kv):
    tokens, width = q.shape
    length = kv.shape[0]
    seqs = kv.shape[1] // 128
    group = tokens // seqs
    rows = group * width // 128
    return pl.pallas_call(
        attend_kernel,
        grid_spec=pltpu.PrefetchScalarGridSpec(
            num_scalar_prefetch=1,
            grid=(seqs,),
            in_specs=[
                pl.BlockSpec((group, width), lambda s, f: (s, 0)),
                pl.BlockSpec((length, 128), lambda s, f: (0, s)),
            ],
            out_specs=[
                pl.BlockSpec((group, width), lambda s, f: (s, 0)),
                pl.BlockSpec((1, 2, 8, rows), lambda s, f: (s, 0, 0, 0)),
            ],
            scratch_shapes=[pltpu.VMEM((length, 128), bf16)] * 4,
        ),
        out_shape=[
            jax.ShapeDtypeStruct((tokens, width), bf16),
            jax.ShapeDtypeStruct((seqs, 2, 8, rows), f32),
        ],
        compiler_params=params(),
        cost_estimate=cost(8 * tokens * width * length, 4 << 20, tokens * 12 * length),
        name="attend",
    )(first, q, kv)


def backward_part(first, high, q6, do6, keys, vals, lse, delta, dkv_ref, group, dq_ref):
    full = first // KB
    low_half = lax.broadcasted_iota(jnp.int32, (KB, 128), 1) < 64

    def block(kb, masked):
        rows = block_rows(kb)
        key = keys[rows, :]
        probs = jnp.exp(dot_nt(key, q6) - lse)
        if masked:
            row = lax.broadcasted_iota(jnp.int32, probs.shape, 0)
            col = lax.broadcasted_iota(jnp.int32, probs.shape, 1) % group
            probs = jnp.where(row - col <= first - full * KB, probs, 0.0)
        grad_probs = dot_nt(vals[rows, :], do6)
        grad_scores = (probs * (grad_probs - delta)).astype(bf16)
        grad_key = dot_nn(grad_scores, q6)
        grad_val = dot_nn(probs.astype(bf16), do6)
        if high:
            part = jnp.where(low_half, pltpu.roll(grad_key, 64, 1), grad_val)
        else:
            part = jnp.where(low_half, grad_key, pltpu.roll(grad_val, 64, 1))
        dkv_ref[rows, :] += part
        dq_ref[...] += dot_tn(grad_scores, key)

    block(full, True)

    def step(kb, carry):
        block(kb, False)
        return carry

    lax.fori_loop(0, full, step, 0)


def attend_back_kernel(has_start, first_ref, *refs):
    if has_start:
        q_ref, kv_ref, o_ref, do_ref, lse_ref, tab_ref, start_ref, dq_out, dkv_ref, k0, k1, v0, v1, dq_ref = refs
        dkv_ref[...] = start_ref[...]
    else:
        q_ref, kv_ref, o_ref, do_ref, lse_ref, tab_ref, dq_out, dkv_ref, k0, k1, v0, v1, dq_ref = refs
        dkv_ref[...] = jnp.zeros_like(dkv_ref)
    first = first_ref[0]
    group = q_ref.shape[0]
    spread_kv(kv_ref, k0, k1, v0, v1)
    q6 = pairs_down(q_ref[...])
    do6 = pairs_down(do_ref[...])
    deltas = (do6.astype(f32) * pairs_down(o_ref[...]).astype(f32)).T
    even_delta = jnp.sum(deltas[:64], axis=0, keepdims=True)
    odd_delta = jnp.sum(deltas[64:], axis=0, keepdims=True)
    dq_ref[...] = jnp.zeros_like(dq_ref)
    backward_part(first, False, q6, do6, k0, v0, lse_ref[0, 0, 0:1], even_delta, dkv_ref, group, dq_ref)
    backward_part(first, True, q6, do6, k1, v1, lse_ref[0, 1, 0:1], odd_delta, dkv_ref, group, dq_ref)
    cos_tab, sin_low, sin_high = tab_ref[0], -tab_ref[1], -tab_ref[2]
    for p in range(q_ref.shape[1] // 128):
        part = dq_ref[p * group : (p + 1) * group] * SCALE
        dq_out[:, p * 128 : (p + 1) * 128] = turn(part, cos_tab, sin_low, sin_high).astype(bf16)


def attend_back_call(first, q, kv, attended, grad, lse, tab, start=None):
    tokens, width = q.shape
    length = kv.shape[0]
    seqs = kv.shape[1] // 128
    group = tokens // seqs
    rows = group * width // 128
    tok_spec = pl.BlockSpec((group, width), lambda s, f: (s, 0))
    len_spec = pl.BlockSpec((length, 128), lambda s, f: (0, s))
    in_specs = [
        tok_spec,
        len_spec,
        tok_spec,
        tok_spec,
        pl.BlockSpec((1, 2, 8, rows), lambda s, f: (s, 0, 0, 0)),
        pl.BlockSpec((3, group, 128), lambda s, f: (0, s, 0)),
    ]
    operands = [q, kv, attended, grad, lse, tab]
    if start is not None:
        in_specs.append(len_spec)
        operands.append(start)
    return pl.pallas_call(
        partial(attend_back_kernel, start is not None),
        grid_spec=pltpu.PrefetchScalarGridSpec(
            num_scalar_prefetch=1,
            grid=(seqs,),
            in_specs=in_specs,
            out_specs=[tok_spec, len_spec],
            scratch_shapes=[pltpu.VMEM((length, 128), bf16)] * 4 + [pltpu.VMEM((rows, 128), f32)],
        ),
        out_shape=[
            jax.ShapeDtypeStruct((tokens, width), bf16),
            jax.ShapeDtypeStruct((length, seqs * 128), f32),
        ],
        compiler_params=params(),
        cost_estimate=cost(20 * tokens * width * length, 8 << 20, tokens * 12 * length),
        name="attend_back",
    )(first, *operands)


def middle_kernel(
    att_ref, x_ref, y_ref, wo_ref, bias_ref, gain_ref, off_ref, wq_ref, bq_ref, tab_ref,
    x2_ref, na_ref, nm_ref, q_ref,
):
    second = (
        x_ref[...].astype(f32) + dot_nn(att_ref[...], wo_ref[0]) + y_ref[...] + bias_ref[...]
    ).astype(bf16)
    x2_ref[...] = second
    unit = unit_rows(second.astype(f32))[0]
    norm_a = (unit * gain_ref[0:1] + off_ref[0:1]).astype(bf16)
    na_ref[...] = norm_a
    nm_ref[...] = (unit * gain_ref[1:2] + off_ref[1:2]).astype(bf16)
    proj = dot_nn(norm_a, wq_ref[...]) + bq_ref[...]
    cos_tab, sin_low, sin_high = tab_ref[0], tab_ref[1], tab_ref[2]
    for p in range(proj.shape[1] // 128):
        cols = slice(p * 128, (p + 1) * 128)
        q_ref[:, cols] = (turn(proj[:, cols], cos_tab, sin_low, sin_high) * SCALE).astype(bf16)


def layer_spec(shape, layer):
    return pl.BlockSpec((1,) + shape, lambda i: (layer,) + (0,) * len(shape))


def full_spec(shape):
    return pl.BlockSpec(shape, lambda i: (0,) * len(shape))


def middle_call(att, x, y, w_out, bias, gains, offs, w_q2, b_q2, tab):
    tokens, width = x.shape
    operands = (att, x, y, w_out, bias, gains, offs, w_q2, b_q2.reshape(1, -1), tab)
    specs = [full_spec(v.shape) for v in operands]
    specs[3] = layer_spec((width, width), 0)
    return pl.pallas_call(
        middle_kernel,
        grid=(1,),
        in_specs=specs,
        out_specs=[full_spec((tokens, width))] * 4,
        out_shape=[jax.ShapeDtypeStruct((tokens, width), bf16)] * 4,
        compiler_params=params(),
        cost_estimate=cost(4 * tokens * width * width, 10 << 20),
        name="middle",
    )(*operands)


def norm_back(values, grad_a, grad_m, gain_ref, small_ref, row):
    unit, inverse = unit_rows(values)
    small_ref[row : row + 1] = jnp.sum(grad_a * unit, axis=0, keepdims=True)
    small_ref[row + 1 : row + 2] = jnp.sum(grad_m * unit, axis=0, keepdims=True)
    small_ref[row + 2 : row + 3] = jnp.sum(grad_a, axis=0, keepdims=True)
    small_ref[row + 3 : row + 4] = jnp.sum(grad_m, axis=0, keepdims=True)
    grad_unit = grad_a * gain_ref[0:1] + grad_m * gain_ref[1:2]
    return inverse * (
        grad_unit
        - jnp.mean(grad_unit, axis=-1, keepdims=True)
        - unit * jnp.mean(grad_unit * unit, axis=-1, keepdims=True)
    )


def turn_kernel(
    x2_ref, y_ref, att2_ref, att1_ref, g_ref, na_ref, dq_ref, dnm_ref, wo1_ref, wo2_ref, wq_ref, bias_ref, gain_ref,
    hidden_ref, grads_ref, g1_ref, do1_ref, small_ref,
):
    width = x2_ref.shape[1]
    second = x2_ref[...].astype(f32)
    att2, grad, dq = att2_ref[...], g_ref[...], dq_ref[...]
    wide = grad.astype(f32)
    small_ref[...] = jnp.zeros_like(small_ref)
    grad_a = dot_nt(dq, wq_ref[...])
    g1 = (norm_back(second, grad_a, dnm_ref[...], gain_ref, small_ref, 0) + wide).astype(bf16)
    g1_ref[...] = g1
    do1_ref[...] = dot_nt(g1, wo1_ref[0]).astype(bf16)
    small_ref[4:5] = jnp.sum(wide, axis=0, keepdims=True)
    small_ref[5:6] = jnp.sum(dq.astype(f32), axis=0, keepdims=True)
    small_ref[6:7] = jnp.sum(g1.astype(f32), axis=0, keepdims=True)
    grads_ref[0:width] = dot_tn(att2, grad).astype(bf16)
    grads_ref[width : 2 * width] = dot_tn(na_ref[...], dq).astype(bf16)
    grads_ref[2 * width : 3 * width] = dot_tn(att1_ref[...], g1).astype(bf16)
    hidden_ref[...] = (second + dot_nn(att2, wo2_ref[0]) + y_ref[...] + bias_ref[...]).astype(bf16)


def turn_call(x2, y2, att2, att1, g, na2, dq2, dnm2, w_out, w_q2, bias, gains):
    tokens, width = x2.shape
    operands = (x2, y2, att2, att1, g, na2, dq2, dnm2, w_out, w_out, w_q2, bias, gains)
    specs = [full_spec(v.shape) for v in operands]
    specs[8] = layer_spec((width, width), 0)
    specs[9] = layer_spec((width, width), 1)
    tok = full_spec((tokens, width))
    tok_shape = jax.ShapeDtypeStruct((tokens, width), bf16)
    return pl.pallas_call(
        turn_kernel,
        grid=(1,),
        in_specs=specs,
        out_specs=[tok, full_spec((3 * width, width)), tok, tok, full_spec((8, width))],
        out_shape=[
            tok_shape,
            jax.ShapeDtypeStruct((3 * width, width), bf16),
            tok_shape,
            tok_shape,
            jax.ShapeDtypeStruct((8, width), f32),
        ],
        compiler_params=params(),
        cost_estimate=cost(12 * tokens * width * width, 20 << 20),
        name="turn",
    )(*operands)


def last_kernel(
    x_ref, g1_ref, na_ref, dq_ref, dkv_ref, dnm_ref, w_ref, gain_ref, tab_ref, grad_ref, grads_ref, small_ref
):
    tokens, width = x_ref.shape
    group = dkv_ref.shape[0]
    dkv = jnp.concatenate(
        [dkv_ref[:, s * 128 : (s + 1) * 128] for s in range(tokens // group)], axis=0
    ).astype(f32)
    low_half = lax.broadcasted_iota(jnp.int32, dkv.shape, 1) < 64
    dkv = jnp.where(low_half, turn(dkv, tab_ref[0], -tab_ref[1], -tab_ref[2]), dkv).astype(bf16)
    dq, norm_a = dq_ref[...], na_ref[...]
    small_ref[...] = jnp.zeros_like(small_ref)
    small_ref[4:5] = jnp.sum(dq.astype(f32), axis=0, keepdims=True)
    small_ref[5:6, 0:128] = jnp.sum(dkv.astype(f32), axis=0, keepdims=True)
    grads_ref[0:width] = dot_tn(norm_a, dq).astype(bf16)
    grads_ref[width : width + 128] = dot_tn(dkv, norm_a).astype(bf16)
    grad_a = dot_nt(dq, w_ref[:, :width]) + dot_nt(dkv, w_ref[:, width:])
    grad_ref[...] = g1_ref[...].astype(f32) + norm_back(
        x_ref[...].astype(f32), grad_a, dnm_ref[...], gain_ref, small_ref, 0
    )


def last_call(x, g1, na1, dq1, dkv, dnm1, w_qkv, gains, tab):
    tokens, width = x.shape
    return pl.pallas_call(
        last_kernel,
        in_specs=vmem(9),
        out_specs=vmem(3),
        out_shape=[
            jax.ShapeDtypeStruct((tokens, width), f32),
            jax.ShapeDtypeStruct((width + 128, width), bf16),
            jax.ShapeDtypeStruct((8, width), f32),
        ],
        compiler_params=params(),
        cost_estimate=cost(4 * tokens * width * (width + 128), 10 << 20),
        name="last",
    )(x, g1, na1, dq1, dkv, dnm1, w_qkv, gains, tab)


def swap_cores(values):
    return lax.ppermute(values, C, [(0, 1), (1, 0)])


def reduce_parts(send, keep):
    part = (swap_cores(send).astype(f32) + keep.astype(f32)).astype(bf16)
    part = lax.psum_scatter(part, B, scatter_dimension=0, tiled=True)
    return lax.psum_scatter(part, Z, scatter_dimension=0, tiled=True)


def gather_parts(part):
    return lax.all_gather(part, (C,) + B + (Z,), axis=0, tiled=True)


def halves(rows, core):
    half = rows.shape[0] // 2
    send = lax.dynamic_slice_in_dim(rows, (1 - core) * half, half, 0)
    keep = lax.dynamic_slice_in_dim(rows, core * half, half, 0)
    return send, keep


def place_kernel(in_ref, *refs):
    down_ref, up_ref = refs[-2:]
    for j in range(in_ref.shape[0] // (2 * UNIT)):
        rows = slice(j * UNIT, (j + 1) * UNIT)
        down_ref[0, rows] = in_ref[2 * j * UNIT : (2 * j + 1) * UNIT].astype(f32)
        up_ref[0, rows] = in_ref[(2 * j + 1) * UNIT : (2 * j + 2) * UNIT].astype(f32)


def place_call(rows, layer, before=None):
    width = rows.shape[1]
    hidden = rows.shape[0] // 2
    step_rows = TILE // 2
    in_specs = [pl.BlockSpec((TILE, width), lambda i: (i, 0))]
    operands = [rows]
    aliases = {}
    if before is not None:
        in_specs += [pl.BlockSpec(memory_space=pl.ANY)] * 2
        operands += list(before)
        aliases = {1: 0, 2: 1}
    return pl.pallas_call(
        place_kernel,
        grid=(hidden // step_rows,),
        in_specs=in_specs,
        out_specs=[
            pl.BlockSpec((1, step_rows, width), lambda i: (layer, i, 0)),
            pl.BlockSpec((1, step_rows, TILE), lambda i: (layer, i % 2, i // 2)),
        ],
        out_shape=[
            jax.ShapeDtypeStruct((2, hidden, width), f32),
            jax.ShapeDtypeStruct((2, width, hidden), f32),
        ],
        input_output_aliases=aliases,
        compiler_params=params(),
        cost_estimate=cost(0, rows.size * 6),
        name="place",
    )(*operands)


def rotary_tables(positions):
    half_rot = ROT // 2
    inverse = BASE ** (-(jnp.arange(half_rot, dtype=f32) * 2.0 / ROT))
    angles = positions.astype(f32).reshape(-1, 1) * inverse
    cos, sin = jnp.cos(angles), jnp.sin(angles)
    zero = jnp.zeros_like(sin)
    rest = jnp.zeros((cos.shape[0], 64 - ROT), f32)
    head = [
        jnp.concatenate([cos, cos, rest + 1.0], axis=-1),
        jnp.concatenate([-sin, zero, rest], axis=-1),
        jnp.concatenate([zero, sin, rest], axis=-1),
    ]
    return jnp.stack([jnp.concatenate([h, h], axis=-1) for h in head])


def local(
    hidden_in,
    positions,
    cotangent,
    norm_gains,
    norm_biases,
    w_qkv,
    b_qkv,
    w_q2,
    b_q2,
    w_out,
    w_up,
    b_up,
    w_down,
    out_bias,
):
    seqs, group, width = hidden_in.shape
    tokens = seqs * group
    hidden = w_up.shape[2]
    core = lax.axis_index(C)
    core_row = core.reshape(1).astype(jnp.int32)
    first = ((lax.axis_index(Z) * 2 + core) * group).reshape(1).astype(jnp.int32)
    x1 = hidden_in.reshape(tokens, width)
    g2 = cotangent.reshape(tokens, width)
    tab = rotary_tables(positions)

    na1, nm1, q1, kv_own = first_call(x1, norm_gains[0], norm_biases[0], w_qkv, b_qkv, tab, group)
    kv = lax.all_gather(kv_own, (Z, C), axis=0, tiled=True)
    y1, act1, slope1 = mlp_fwd_call(nm1, w_up, b_up, w_down, 0)
    do2 = lax.dot_general(
        g2, w_out[1], (((1,), (1,)), ((), ())), preferred_element_type=f32
    ).astype(bf16)
    att1, lse1 = attend_call(first, q1, kv)
    x2, na2, nm2, q2 = middle_call(
        att1, x1, y1, w_out, out_bias[0:1], norm_gains[1], norm_biases[1], w_q2, b_q2, tab
    )

    y2, dnm2, send, keep, bup2 = mlp_back_call(core_row, nm2, g2, w_up, w_down, 1, b_up=b_up)
    mlp2 = reduce_parts(send.reshape(hidden, width), keep.reshape(hidden, width))
    att2, lse2 = attend_call(first, q2, kv)
    dq2, dkv2 = attend_back_call(first, q2, kv, att2, do2, lse2, tab)
    hidden_out, grads2, g1, do1, small2 = turn_call(
        x2, y2, att2, att1, g2, na2, dq2, dnm2, w_out, w_q2, out_bias[1:2], norm_gains[1]
    )
    outs2 = reduce_parts(*halves(grads2, core))
    dq1, dkv1 = attend_back_call(first, q1, kv, att1, do1, lse1, tab, dkv2)
    dkv = lax.psum_scatter(dkv1.astype(bf16), (Z, C), scatter_dimension=0, tiled=True)
    dnm1, send, keep, bup1 = mlp_back_call(
        core_row, nm1, g1, w_up, w_down, 0, kept=(act1, slope1)
    )
    mlp1 = reduce_parts(send.reshape(hidden, width), keep.reshape(hidden, width))
    grad_input, grads1, small1 = last_call(x1, g1, na1, dq1, dkv, dnm1, w_qkv, norm_gains[0], tab)
    small = jnp.concatenate(
        [small1, small2, bup1.reshape(-1, width), bup2.reshape(-1, width)], axis=0
    ).astype(bf16)
    used = grads1.shape[0] + small.shape[0]
    total = -(-used // 256) * 256
    grads1 = jnp.concatenate([grads1, small, jnp.zeros((total - used, width), bf16)], axis=0)
    outs1 = reduce_parts(*halves(grads1, core))

    placed = place_call(gather_parts(mlp2), 1)
    outs2 = gather_parts(outs2)
    grad_down, grad_up = place_call(gather_parts(mlp1), 0, placed)
    outs1 = gather_parts(outs1)

    grad_out = jnp.stack([outs2[2 * width :], outs2[:width]]).astype(f32)
    grad_q2 = outs2[width : 2 * width].astype(f32)
    kv_rows = outs1[width : width + 128]
    grad_qkv = jnp.concatenate([outs1[:width], kv_rows.T], axis=1).astype(f32)
    small = outs1[width + 128 :].astype(f32)
    one, two = small[0:8], small[8:16]
    ups = hidden // width
    grad_up_bias = jnp.stack([small[16 : 16 + ups].reshape(-1), small[16 + ups : 16 + 2 * ups].reshape(-1)])
    grad_gains = jnp.stack([one[0:2], two[0:2]])
    grad_biases = jnp.stack([one[2:4], two[2:4]])
    grad_qkv_bias = jnp.concatenate([one[4], one[5, :128]])
    grad_out_bias = jnp.stack([two[6], two[4]])
    return (
        hidden_out.reshape(seqs, group, width),
        grad_input.reshape(seqs, group, width),
        grad_gains,
        grad_biases,
        grad_qkv,
        grad_qkv_bias,
        grad_q2,
        two[5],
        grad_out,
        grad_up,
        grad_up_bias,
        grad_down,
        grad_out_bias,
    )


def solution(mesh):
    batch, seq = mesh.shape["batch"], mesh.shape["seq"]
    fine = jax.sharding.Mesh(
        mesh.devices.reshape(2, batch // 2, seq // 2, 2), ("b0", "b1", "z", "c")
    )
    rows = P(B, (Z, C), None)
    return jax.shard_map(
        local,
        mesh=fine,
        in_specs=(rows, P(B, (Z, C)), rows) + (P(),) * 11,
        out_specs=(rows, rows) + (P(),) * 11,
        check_vma=False,
    )
```

```python
from functools import partial

import jax
import jax.numpy as jnp
from jax import lax
from jax.experimental import pallas as pl
from jax.experimental.pallas import tpu as pltpu
from jax.sharding import PartitionSpec as P

ROT = 16
EPSILON = 1e-05
SCALE = 0.125
NEGATIVE = -1e30
BASE = 10000.0

B = ("b0", "b1")
Z = "z"
C = "c"
TILE = 768
QUARTER = TILE // 2
KB = 256

f32 = jnp.float32
bf16 = jnp.bfloat16


def dot_nn(a, b):
    return lax.dot_general(a, b, (((1,), (0,)), ((), ())), preferred_element_type=f32)


def dot_nt(a, b):
    return lax.dot_general(a, b, (((1,), (1,)), ((), ())), preferred_element_type=f32)


def dot_tn(a, b):
    return lax.dot_general(a, b, (((0,), (0,)), ((), ())), preferred_element_type=f32)


def invoke(
    kernel, operands, deps, *, grid, in_specs, out_specs, out_shape, name, scalars=(), scratch=(), aliases={}, us=2
):
    ahead = len(scalars) + len(operands)

    def body(*refs):
        kernel(*refs[:ahead], *refs[ahead + len(deps) :])

    return pl.pallas_call(
        body,
        grid_spec=pltpu.PrefetchScalarGridSpec(
            num_scalar_prefetch=len(scalars),
            grid=grid,
            in_specs=list(in_specs) + [pl.BlockSpec(memory_space=pl.ANY)] * len(deps),
            out_specs=out_specs,
            scratch_shapes=scratch,
        ),
        out_shape=out_shape,
        input_output_aliases=aliases,
        compiler_params=pltpu.CompilerParams(vmem_limit_bytes=50 << 20),
        cost_estimate=pl.CostEstimate(
            flops=us * 600_000_000, bytes_accessed=us * 1_000_000, transcendentals=0
        ),
        name=name,
    )(*scalars, *operands, *deps)


def layer_spec(shape, layer):
    return pl.BlockSpec((1,) + shape, lambda *i: (layer,) + (0,) * len(shape))


def full_spec(shape):
    return pl.BlockSpec(shape, lambda *i: (0,) * len(shape))


def unit_rows(values):
    center = values - jnp.mean(values, axis=-1, keepdims=True)
    spread = jnp.mean(center * center, axis=-1, keepdims=True)
    inverse = lax.rsqrt(spread + EPSILON)
    return center * inverse, inverse


def turn(values, cos_tab, sin_low, sin_high):
    return (
        values * cos_tab
        + pltpu.roll(values, 120, 1) * sin_low
        + pltpu.roll(values, 8, 1) * sin_high
    )


def pairs_down(values):
    return jnp.concatenate(
        [values[:, p * 128 : (p + 1) * 128] for p in range(values.shape[1] // 128)], axis=0
    )


def gelu_parts(lifted):
    cdf = 0.5 + 0.5 * lax.erf(lifted * 0.7071067811865476)
    slope = cdf + lifted * (0.3989422804014327 * jnp.exp(-0.5 * lifted * lifted))
    return lifted * cdf, slope


def first_kernel(x_ref, gain_ref, off_ref, w_ref, b_ref, tab_ref, na_ref, nm_ref, q_ref, kv_ref):
    tokens, width = x_ref.shape
    unit = unit_rows(x_ref[...].astype(f32))[0]
    norm_a = (unit * gain_ref[0:1] + off_ref[0:1]).astype(bf16)
    na_ref[...] = norm_a
    nm_ref[...] = (unit * gain_ref[1:2] + off_ref[1:2]).astype(bf16)
    cos_tab, sin_low, sin_high = tab_ref[0], tab_ref[1], tab_ref[2]
    kv = dot_nn(norm_a, w_ref[:, width:]) + b_ref[:, width:]
    low_half = lax.broadcasted_iota(jnp.int32, kv.shape, 1) < 64
    kv = jnp.where(low_half, turn(kv, cos_tab, sin_low, sin_high), kv).astype(bf16)
    group = kv_ref.shape[0]
    for s in range(tokens // group):
        kv_ref[:, s * 128 : (s + 1) * 128] = kv[s * group : (s + 1) * group]
    proj = dot_nn(norm_a, w_ref[:, :width]) + b_ref[:, :width]
    for p in range(width // 128):
        cols = slice(p * 128, (p + 1) * 128)
        q_ref[:, cols] = (turn(proj[:, cols], cos_tab, sin_low, sin_high) * SCALE).astype(bf16)


def first_call(x, gains, offs, w_qkv, b_qkv, tab, group):
    tokens, width = x.shape
    operands = (x, gains, offs, w_qkv, b_qkv.reshape(1, -1), tab)
    shapes = [(tokens, width)] * 3 + [(group, tokens // group * 128)]
    return invoke(
        first_kernel,
        operands,
        (),
        grid=(1,),
        in_specs=[full_spec(v.shape) for v in operands],
        out_specs=[full_spec(v) for v in shapes],
        out_shape=[jax.ShapeDtypeStruct(v, bf16) for v in shapes],
        name="first",
        us=3,
    )


def mlp_fwd_kernel(nm_ref, up_ref, bup_ref, down_ref, y_ref, act_ref, slope_ref):
    lifted = dot_nn(nm_ref[...], up_ref[0]) + bup_ref[...]
    active, slope = gelu_parts(lifted)
    active = active.astype(bf16)
    act_ref[...] = active
    slope_ref[...] = slope.astype(bf16)

    @pl.when(pl.program_id(0) == 0)
    def _():
        y_ref[...] = jnp.zeros_like(y_ref)

    y_ref[...] += dot_nn(active, down_ref[0])


def mlp_fwd_call(nm, w_up, b_up, w_down, layer):
    tokens, width = nm.shape
    hidden = w_up.shape[2]
    return invoke(
        mlp_fwd_kernel,
        (nm, w_up, b_up[layer : layer + 1], w_down),
        (),
        grid=(hidden // TILE,),
        in_specs=[
            full_spec((tokens, width)),
            pl.BlockSpec((1, width, TILE), lambda t: (layer, 0, t)),
            pl.BlockSpec((1, TILE), lambda t: (0, t)),
            pl.BlockSpec((1, TILE, width), lambda t: (layer, t, 0)),
        ],
        out_specs=[
            full_spec((tokens, width)),
            pl.BlockSpec((tokens, TILE), lambda t: (0, t)),
            pl.BlockSpec((tokens, TILE), lambda t: (0, t)),
        ],
        out_shape=[
            jax.ShapeDtypeStruct((tokens, width), f32),
            jax.ShapeDtypeStruct((tokens, hidden), bf16),
            jax.ShapeDtypeStruct((tokens, hidden), bf16),
        ],
        name="mlp_fwd",
        us=10,
    )


def mlp_grads(active, slope, nm, nm_turned, grad, up, down, start, refs):
    grad_norm_ref, rows_ref, bias_ref = refs
    grad_lifted = (dot_nt(grad, down) * slope).astype(bf16)
    bias_ref[...] = jnp.sum(grad_lifted.astype(f32), axis=0, keepdims=True)

    @pl.when(pl.program_id(0) == 0)
    def _():
        grad_norm_ref[...] = jnp.zeros_like(grad_norm_ref) if start is None else start[...]
        nm_turned[...] = nm.T

    grad_norm_ref[...] += dot_nt(grad_lifted, up)
    grad_down = dot_tn(active, grad).astype(bf16)
    grad_up = dot_nn(nm_turned[...], grad_lifted).astype(bf16)
    for j in range(2):
        rows = slice(j * QUARTER, (j + 1) * QUARTER)
        rows_ref[0, 2 * j * QUARTER : (2 * j + 1) * QUARTER] = grad_down[rows]
        rows_ref[0, (2 * j + 1) * QUARTER : (2 * j + 2) * QUARTER] = grad_up[rows]


def mlp_both_kernel(more, core_ref, nm_ref, g_ref, up_ref, bup_ref, down_ref, *refs):
    y_start, grad_start = refs[:2] if more else (None, None)
    y_ref, *outs, nm_turned = refs[2:] if more else refs
    nm, up, down = nm_ref[...], up_ref[0], down_ref[0]
    active, slope = gelu_parts(dot_nn(nm, up) + bup_ref[...])
    active = active.astype(bf16)

    @pl.when(pl.program_id(0) == 0)
    def _():
        y_ref[...] = y_start[...] if more else jnp.zeros_like(y_ref)

    y_ref[...] += dot_nn(active, down)
    mlp_grads(active, slope, nm, nm_turned, g_ref[...], up, down, grad_start, outs)


def mlp_back_kernel(more, core_ref, nm_ref, g_ref, up_ref, down_ref, act_ref, slope_ref, *refs):
    grad_start = refs[0] if more else None
    *outs, nm_turned = refs[1:] if more else refs
    slope = slope_ref[...].astype(f32)
    mlp_grads(
        act_ref[...], slope, nm_ref[...], nm_turned, g_ref[...], up_ref[0], down_ref[0], grad_start, outs
    )


def mlp_back_call(core, nm, grad, w_up, w_down, layer, b_up=None, kept=None, before=None, deps=()):
    tokens, width = nm.shape
    hidden = w_up.shape[2]
    half = hidden // TILE // 2
    other = before is None

    def tile(t, core_ref):
        c = core_ref[0]
        return (1 - c if other else c) * half + t

    whole = full_spec((tokens, width))
    whole_shape = jax.ShapeDtypeStruct((tokens, width), f32)
    up_spec = pl.BlockSpec((1, width, TILE), lambda t, c: (layer, 0, tile(t, c)))
    down_spec = pl.BlockSpec((1, TILE, width), lambda t, c: (layer, tile(t, c), 0))
    cols_spec = pl.BlockSpec((tokens, TILE), lambda t, c: (0, tile(t, c)))
    both = kept is None
    if both:
        bias_spec = pl.BlockSpec((1, TILE), lambda t, c: (0, tile(t, c)))
        in_specs = [whole, whole, up_spec, bias_spec, down_spec]
        operands = (nm, grad, w_up, b_up[layer : layer + 1], w_down)
    else:
        in_specs = [whole, whole, up_spec, down_spec, cols_spec, cols_spec]
        operands = (nm, grad, w_up, w_down) + kept
    before = tuple(before or ())
    count = 2 if both else 1
    return invoke(
        partial(mlp_both_kernel if both else mlp_back_kernel, not other),
        operands + before,
        deps,
        scalars=(core,),
        grid=(half,),
        in_specs=in_specs + [whole] * len(before),
        out_specs=[whole] * count
        + [
            pl.BlockSpec((1, 2 * TILE, width), lambda t, c: (t, 0, 0)),
            pl.BlockSpec((1, TILE), lambda t, c: (0, t)),
        ],
        out_shape=[whole_shape] * count
        + [
            jax.ShapeDtypeStruct((half, 2 * TILE, width), bf16),
            jax.ShapeDtypeStruct((1, hidden // 2), f32),
        ],
        scratch=[pltpu.VMEM((width, tokens), bf16)],
        name="mlp_both" if both else "mlp_back",
        us=40 if both else 12,
    )


def spread_kv(pieces, order_ref, k0, k1, turned, forward):
    at = 0
    for ref in pieces:
        for p in range(ref.shape[0]):
            kv = ref[p].astype(f32)
            rows = kv.shape[0]
            swapped = pltpu.roll(kv, 64, 1)
            low_half = lax.broadcasted_iota(jnp.int32, kv.shape, 1) < 64
            zero = jnp.zeros_like(kv)
            block = order_ref[1 + at]
            place = pl.ds(pl.multiple_of(block * rows, rows), rows)
            k0[place] = jnp.where(low_half, kv, zero).astype(bf16)
            k1[place] = jnp.where(low_half, zero, swapped).astype(bf16)
            if forward:
                t0, t1 = turned
                rest = jnp.ones((64, rows), f32)
                part = kv.T[64:]
            else:
                v0, v1, t0, t1 = turned
                v0[place] = jnp.where(low_half, swapped, zero).astype(bf16)
                v1[place] = jnp.where(low_half, zero, kv).astype(bf16)
                rest = jnp.zeros((64, rows), f32)
                part = kv.T[:64]
            t0[block] = jnp.concatenate([part, rest], axis=0).astype(bf16)
            t1[block] = jnp.concatenate([rest, part], axis=0).astype(bf16)
            at += 1


def block_rows(index):
    return pl.ds(pl.multiple_of(index * KB, KB), KB)


def turned_block(ref, index):
    return jnp.concatenate([ref[2 * index], ref[2 * index + 1]], axis=1)


def visible(shape, first, start, group):
    key = lax.broadcasted_iota(jnp.int32, shape, 0)
    token = lax.broadcasted_iota(jnp.int32, shape, 1) % group
    return key - token <= first - start


def attend_kernel(count, first_ref, q_ref, *refs):
    pieces, (o_ref, lse_ref, k0, k1, t0, t1) = refs[:count], refs[count:]
    first = first_ref[0]
    group, width = q_ref.shape
    spread_kv(pieces, first_ref, k0, k1, (t0, t1), True)
    q6 = pairs_down(q_ref[...])
    full = first // KB

    def block(kb, carry):
        done = []
        for keys, vals, (top, summed) in zip((k0, k1), (t0, t1), carry or (2 * ((None, None),))):
            scores = dot_nt(keys[block_rows(kb), :], q6)
            if carry is None:
                scores = jnp.where(
                    visible(scores.shape, first, full * KB, group), scores, NEGATIVE
                )
            new_top = jnp.max(scores, axis=0, keepdims=True)
            if carry is not None:
                new_top = jnp.maximum(top, new_top)
            weights = jnp.exp(scores - new_top).astype(bf16)
            part = dot_nn(turned_block(vals, kb), weights)
            if carry is not None:
                part = part + summed * jnp.exp(top - new_top)
            done.append((new_top, part))
        return tuple(done)

    (top0, sum0), (top1, sum1) = lax.fori_loop(0, full, block, block(full, None))
    total0, total1 = sum0[64:65], sum1[0:1]
    both = jnp.concatenate([sum0[:64] / total0, sum1[64:] / total1], axis=0).T.astype(bf16)
    for p in range(width // 128):
        o_ref[:, p * 128 : (p + 1) * 128] = both[p * group : (p + 1) * group]
    shape = lse_ref.shape[2:]
    lse_ref[0, 0] = jnp.broadcast_to(top0 + jnp.log(total0), shape)
    lse_ref[0, 1] = jnp.broadcast_to(top1 + jnp.log(total1), shape)


def piece_specs(kv):
    return [pl.BlockSpec(v.shape[:2] + (128,), lambda s, f: (0, 0, s)) for v in kv]


def attend_call(first, q, kv, deps=()):
    tokens, width = q.shape
    length = sum(v.shape[0] for v in kv) * kv[0].shape[1]
    seqs = kv[0].shape[2] // 128
    group = tokens // seqs
    rows = group * width // 128
    return invoke(
        partial(attend_kernel, len(kv)),
        (q,) + kv,
        deps,
        scalars=(first,),
        grid=(seqs,),
        in_specs=[pl.BlockSpec((group, width), lambda s, f: (s, 0))] + piece_specs(kv),
        out_specs=[
            pl.BlockSpec((group, width), lambda s, f: (s, 0)),
            pl.BlockSpec((1, 2, 8, rows), lambda s, f: (s, 0, 0, 0)),
        ],
        scratch=[pltpu.VMEM((length, 128), bf16)] * 2
        + [pltpu.VMEM((length // 128, 128, 128), bf16)] * 2,
        out_shape=[
            jax.ShapeDtypeStruct((tokens, width), bf16),
            jax.ShapeDtypeStruct((seqs, 2, 8, rows), f32),
        ],
        name="attend",
        us=60,
    )


def attend_back_kernel(count, has_start, first_ref, q_ref, *refs):
    pieces, refs = refs[:count], refs[count:]
    if has_start:
        o_ref, do_ref, lse_ref, tab_ref, start_ref, dq_out, dkv_ref, k0, k1, v0, v1, t0, t1, dq_ref = refs
        dkv_ref[...] = start_ref[...]
    else:
        o_ref, do_ref, lse_ref, tab_ref, dq_out, dkv_ref, k0, k1, v0, v1, t0, t1, dq_ref = refs
        dkv_ref[...] = jnp.zeros_like(dkv_ref)
    first = first_ref[0]
    group = q_ref.shape[0]
    spread_kv(pieces, first_ref, k0, k1, (v0, v1, t0, t1), False)
    q6 = pairs_down(q_ref[...])
    do6 = pairs_down(do_ref[...])
    deltas = (do6.astype(f32) * pairs_down(o_ref[...]).astype(f32)).T
    halves = (
        (k0, v0, lse_ref[0, 0, 0:1], jnp.sum(deltas[:64], axis=0, keepdims=True)),
        (k1, v1, lse_ref[0, 1, 0:1], jnp.sum(deltas[64:], axis=0, keepdims=True)),
    )
    dq_ref[...] = jnp.zeros_like(dq_ref)
    full = first // KB
    low_half = lax.broadcasted_iota(jnp.int32, (KB, 128), 1) < 64

    def block(kb, masked):
        rows = block_rows(kb)
        grads, keys, vals = [], [], []
        for k, v, lse, delta in halves:
            probs = jnp.exp(dot_nt(k[rows, :], q6) - lse)
            if masked:
                probs = jnp.where(visible(probs.shape, first, full * KB, group), probs, 0.0)
            grad_probs = dot_nt(v[rows, :], do6)
            grad_scores = (probs * (grad_probs - delta)).astype(bf16)
            grads.append(grad_scores)
            keys.append(dot_nn(grad_scores, q6))
            vals.append(dot_nn(probs.astype(bf16), do6))
        dkv_ref[rows, :] += jnp.where(low_half, keys[0], vals[1]) + pltpu.roll(
            jnp.where(low_half, vals[0], keys[1]), 64, 1
        )
        turned = jnp.concatenate([turned_block(t0, kb), turned_block(t1, kb)], axis=1)
        dq_ref[...] += dot_nn(turned, jnp.concatenate(grads, axis=0))

    block(full, True)

    def step(kb, carry):
        block(kb, False)
        return carry

    lax.fori_loop(0, full, step, 0)
    cos_tab, sin_low, sin_high = tab_ref[0], -tab_ref[1], -tab_ref[2]
    dq = dq_ref[...].T * SCALE
    for p in range(q_ref.shape[1] // 128):
        part = dq[p * group : (p + 1) * group]
        dq_out[:, p * 128 : (p + 1) * 128] = turn(part, cos_tab, sin_low, sin_high).astype(bf16)


def attend_back_call(first, q, kv, attended, grad, lse, tab, start=None, deps=()):
    tokens, width = q.shape
    length = sum(v.shape[0] for v in kv) * kv[0].shape[1]
    seqs = kv[0].shape[2] // 128
    group = tokens // seqs
    rows = group * width // 128
    tok_spec = pl.BlockSpec((group, width), lambda s, f: (s, 0))
    len_spec = pl.BlockSpec((length, 128), lambda s, f: (0, s))
    in_specs = [
        tok_spec,
        *piece_specs(kv),
        tok_spec,
        tok_spec,
        pl.BlockSpec((1, 2, 8, rows), lambda s, f: (s, 0, 0, 0)),
        pl.BlockSpec((3, group, 128), lambda s, f: (0, s, 0)),
    ]
    operands = [q, *kv, attended, grad, lse, tab]
    if start is not None:
        in_specs.append(len_spec)
        operands.append(start)
    return invoke(
        partial(attend_back_kernel, len(kv), start is not None),
        operands,
        deps,
        scalars=(first,),
        grid=(seqs,),
        in_specs=in_specs,
        out_specs=[tok_spec, len_spec],
        scratch=[pltpu.VMEM((length, 128), bf16)] * 4
        + [pltpu.VMEM((length // 128, 128, 128), bf16)] * 2
        + [pltpu.VMEM((128, rows), f32)],
        out_shape=[
            jax.ShapeDtypeStruct((tokens, width), bf16),
            jax.ShapeDtypeStruct((length, seqs * 128), f32),
        ],
        name="attend_back",
        us=90,
    )


def back_kernel(g_ref, w_ref, out_ref):
    out_ref[...] = dot_nt(g_ref[...], w_ref[0]).astype(bf16)


def back_call(grad, w_out, layer, deps=()):
    tokens, width = grad.shape
    return invoke(
        back_kernel,
        (grad, w_out),
        deps,
        grid=(1,),
        in_specs=[full_spec((tokens, width)), layer_spec((width, width), layer)],
        out_specs=full_spec((tokens, width)),
        out_shape=jax.ShapeDtypeStruct((tokens, width), bf16),
        name="back",
    )


def middle_kernel(
    att_ref, x_ref, y_ref, wo_ref, bias_ref, gain_ref, off_ref, wq_ref, bq_ref, tab_ref,
    x2_ref, na_ref, nm_ref, q_ref,
):
    second = (
        x_ref[...].astype(f32) + dot_nn(att_ref[...], wo_ref[0]) + y_ref[...] + bias_ref[...]
    ).astype(bf16)
    x2_ref[...] = second
    unit = unit_rows(second.astype(f32))[0]
    norm_a = (unit * gain_ref[0:1] + off_ref[0:1]).astype(bf16)
    na_ref[...] = norm_a
    nm_ref[...] = (unit * gain_ref[1:2] + off_ref[1:2]).astype(bf16)
    proj = dot_nn(norm_a, wq_ref[...]) + bq_ref[...]
    cos_tab, sin_low, sin_high = tab_ref[0], tab_ref[1], tab_ref[2]
    for p in range(proj.shape[1] // 128):
        cols = slice(p * 128, (p + 1) * 128)
        q_ref[:, cols] = (turn(proj[:, cols], cos_tab, sin_low, sin_high) * SCALE).astype(bf16)


def middle_call(att, x, y, w_out, bias, gains, offs, w_q2, b_q2, tab):
    tokens, width = x.shape
    operands = (att, x, y, w_out, bias, gains, offs, w_q2, b_q2.reshape(1, -1), tab)
    specs = [full_spec(v.shape) for v in operands]
    specs[3] = layer_spec((width, width), 0)
    return invoke(
        middle_kernel,
        operands,
        (),
        grid=(1,),
        in_specs=specs,
        out_specs=[full_spec((tokens, width))] * 4,
        out_shape=[jax.ShapeDtypeStruct((tokens, width), bf16)] * 4,
        name="middle",
        us=5,
    )


def norm_back(values, grad_a, grad_m, gain_ref, small_ref, row):
    unit, inverse = unit_rows(values)
    small_ref[row : row + 1] = jnp.sum(grad_a * unit, axis=0, keepdims=True)
    small_ref[row + 1 : row + 2] = jnp.sum(grad_m * unit, axis=0, keepdims=True)
    small_ref[row + 2 : row + 3] = jnp.sum(grad_a, axis=0, keepdims=True)
    small_ref[row + 3 : row + 4] = jnp.sum(grad_m, axis=0, keepdims=True)
    grad_unit = grad_a * gain_ref[0:1] + grad_m * gain_ref[1:2]
    return inverse * (
        grad_unit
        - jnp.mean(grad_unit, axis=-1, keepdims=True)
        - unit * jnp.mean(grad_unit * unit, axis=-1, keepdims=True)
    )


def turn_kernel(
    x2_ref, y_ref, att2_ref, att1_ref, g_ref, na_ref, dq_ref, dnm_ref, wo1_ref, wo2_ref, wq_ref, bias_ref, gain_ref,
    hidden_ref, grads_ref, g1_ref, do1_ref, small_ref,
):
    width = x2_ref.shape[1]
    second = x2_ref[...].astype(f32)
    att2, grad, dq = att2_ref[...], g_ref[...], dq_ref[...]
    wide = grad.astype(f32)
    small_ref[...] = jnp.zeros_like(small_ref)
    grad_a = dot_nt(dq, wq_ref[...])
    g1 = (norm_back(second, grad_a, dnm_ref[...], gain_ref, small_ref, 0) + wide).astype(bf16)
    g1_ref[...] = g1
    do1_ref[...] = dot_nt(g1, wo1_ref[0]).astype(bf16)
    small_ref[4:5] = jnp.sum(wide, axis=0, keepdims=True)
    small_ref[5:6] = jnp.sum(dq.astype(f32), axis=0, keepdims=True)
    small_ref[6:7] = jnp.sum(g1.astype(f32), axis=0, keepdims=True)
    grads_ref[0:width] = dot_tn(att2, grad).astype(bf16)
    grads_ref[width : 2 * width] = dot_tn(na_ref[...], dq).astype(bf16)
    grads_ref[2 * width : 3 * width] = dot_tn(att1_ref[...], g1).astype(bf16)
    hidden_ref[...] = (second + dot_nn(att2, wo2_ref[0]) + y_ref[...] + bias_ref[...]).astype(bf16)


def turn_call(x2, y2, att2, att1, g, na2, dq2, dnm2, w_out, w_q2, bias, gains, deps=()):
    tokens, width = x2.shape
    operands = (x2, y2, att2, att1, g, na2, dq2, dnm2, w_out, w_out, w_q2, bias, gains)
    specs = [full_spec(v.shape) for v in operands]
    specs[8] = layer_spec((width, width), 0)
    specs[9] = layer_spec((width, width), 1)
    tok = full_spec((tokens, width))
    tok_shape = jax.ShapeDtypeStruct((tokens, width), bf16)
    return invoke(
        turn_kernel,
        operands,
        deps,
        grid=(1,),
        in_specs=specs,
        out_specs=[tok, full_spec((3 * width, width)), tok, tok, full_spec((8, width))],
        out_shape=[
            tok_shape,
            jax.ShapeDtypeStruct((3 * width, width), bf16),
            tok_shape,
            tok_shape,
            jax.ShapeDtypeStruct((8, width), f32),
        ],
        name="turn",
        us=60,
    )


def last_kernel(
    x_ref, g1_ref, na_ref, dq_ref, dkv_ref, dnm_ref, w_ref, gain_ref, tab_ref, grad_ref, grads_ref, small_ref
):
    tokens, width = x_ref.shape
    group = dkv_ref.shape[0]
    dkv = jnp.concatenate(
        [dkv_ref[:, s * 128 : (s + 1) * 128] for s in range(tokens // group)], axis=0
    ).astype(f32)
    low_half = lax.broadcasted_iota(jnp.int32, dkv.shape, 1) < 64
    dkv = jnp.where(low_half, turn(dkv, tab_ref[0], -tab_ref[1], -tab_ref[2]), dkv).astype(bf16)
    dq, norm_a = dq_ref[...], na_ref[...]
    small_ref[...] = jnp.zeros_like(small_ref)
    small_ref[4:5] = jnp.sum(dq.astype(f32), axis=0, keepdims=True)
    small_ref[5:6, 0:128] = jnp.sum(dkv.astype(f32), axis=0, keepdims=True)
    grads_ref[0:width] = dot_tn(norm_a, dq).astype(bf16)
    grads_ref[width : width + 128] = dot_tn(dkv, norm_a).astype(bf16)
    grad_a = dot_nt(dq, w_ref[:, :width]) + dot_nt(dkv, w_ref[:, width:])
    grad_ref[...] = g1_ref[...].astype(f32) + norm_back(
        x_ref[...].astype(f32), grad_a, dnm_ref[...], gain_ref, small_ref, 0
    )


def last_call(x, g1, na1, dq1, dkv, dnm1, w_qkv, gains, tab, deps=()):
    tokens, width = x.shape
    operands = (x, g1, na1, dq1, dkv, dnm1, w_qkv, gains, tab)
    out_shape = [
        jax.ShapeDtypeStruct((tokens, width), f32),
        jax.ShapeDtypeStruct((width + 128, width), bf16),
        jax.ShapeDtypeStruct((8, width), f32),
    ]
    return invoke(
        last_kernel,
        operands,
        deps,
        grid=(1,),
        in_specs=[full_spec(v.shape) for v in operands],
        out_specs=[full_spec(v.shape) for v in out_shape],
        out_shape=out_shape,
        name="last",
        us=10,
    )


PAIR = [(0, 1), (1, 0)]


def swap(values, axis):
    return lax.ppermute(values, axis, PAIR)


def add_low(first, *rest):
    total = first.astype(f32)
    for value in rest:
        total = total + value.astype(f32)
    return total.astype(bf16)


def pick(values, index):
    return lax.dynamic_index_in_dim(values, index, 0, keepdims=False)


def square():
    return lax.axis_size("b0") == 2 and lax.axis_size("b1") == 2 and lax.axis_size(Z) == 4


def turns(values_at):
    size = lax.axis_size(Z)
    return [
        lax.ppermute(values_at(k), Z, [(i, (i + k) % size) for i in range(size)])
        for k in range(1, size)
    ]


def reduce_offloaded(part):
    part = lax.psum_scatter(part, B, scatter_dimension=0, tiled=True)
    return lax.psum_scatter(part, Z, scatter_dimension=0, tiled=True)


def gather_offloaded(part):
    return lax.all_gather(part, (C,) + B + (Z,), axis=0, tiled=True)


def combine(groups, where, deps, grid=(1,), name="combine", us=2):
    terms = [t for sums, *_ in groups for parts in sums for t in parts]

    def kernel(where_ref, *refs):
        ins, outs = iter(refs[: len(terms)]), refs[len(terms) :]
        for (sums, *_), out_ref in zip(groups, outs):
            for i, parts in enumerate(sums):
                total = next(ins)[...].astype(f32)
                for _ in parts[1:]:
                    total = total + next(ins)[...].astype(f32)
                if len(sums) == 1:
                    out_ref[...] = total.reshape(out_ref.shape).astype(bf16)
                else:
                    out_ref[i] = total.reshape(out_ref.shape[1:]).astype(bf16)

    return invoke(
        kernel,
        [t[0] for t in terms],
        deps,
        scalars=(where,),
        grid=grid,
        in_specs=[pl.BlockSpec(t[1], t[2]) for t in terms],
        out_specs=[pl.BlockSpec(g[1], g[2]) for g in groups],
        out_shape=[jax.ShapeDtypeStruct(g[3], bf16) for g in groups],
        name=name,
        us=us,
    )


def sum_cores(keep, got, where, deps=()):
    width = keep.shape[-1]
    keep, got = (v.reshape(2, 2, 2, -1, width) for v in (keep, got))
    quarter = keep.shape[3]
    half = quarter // 2
    maps = (
        lambda i, j, w: (i, 1 - w[1], 0, j, 0),
        lambda i, j, w: (i, w[1], 0, j, 0),
        lambda i, j, w: (1 - w[0], i, 1, j, 0),
        lambda i, j, w: (w[0], i, 1, j, 0),
    )
    block = (1, 1, 1, half, width)
    groups = [
        (
            [[(keep, block, m), (got, block, m)]],
            (1, half, width),
            lambda i, j, w: (i, j, 0),
            (2, quarter, width),
        )
        for m in maps
    ]
    return combine(groups, where, deps, grid=(2, 2), name="sum_cores")


def sum_first(one, one_got, two, two_got, where, deps=()):
    _, quarter, width = one.shape
    half = quarter // 2
    groups = []
    for values, got, m in (
        (one, one_got, lambda j, w: (1 - w[0], j, 0)),
        (one, one_got, lambda j, w: (w[0], j, 0)),
        (two, two_got, lambda j, w: (1 - w[1], j, 0)),
        (two, two_got, lambda j, w: (w[1], j, 0)),
    ):
        block = (1, half, width)
        groups.append(
            ([[(values, block, m), (got, block, m)]], block, lambda j, w: (0, j, 0), (1, quarter, width))
        )
    return combine(groups, where, deps, grid=(2,), name="sum_first")


def sum_second(one, one_got, two, two_got, where, deps=()):
    width = one.shape[-1]
    one, one_got, two, two_got = (v.reshape(4, -1, width) for v in (one, one_got, two, two_got))
    block = (1,) + one.shape[1:]
    groups = []
    for k in range(4):
        m = lambda i, w, k=k: (lax.rem(w[2] + k, 4), 0, 0)
        groups.append(
            (
                [[(a, block, m), (b, block, m)] for a, b in ((one, one_got), (two, two_got))],
                (2,) + one.shape[1:],
                lambda i, w: (0, 0, 0),
                (2,) + one.shape[1:],
            )
        )
    return combine(groups, where, deps, name="sum_second", us=100)


def sum_third(parts, where, deps=()):
    shape = parts[0].shape
    m = lambda i, w: (0, 0, 0)
    return combine([([[(p, shape, m) for p in parts]], shape, m, shape)], where, deps, name="sum_third")[0]


def join(parts, leads, where, deps=()):
    shape = parts[0].shape[1:]
    groups = [
        (
            [[(p, (1,) + shape, lambda i, w, a=a: (a,) + (0,) * len(shape))] for p in parts],
            (len(parts),) + shape,
            lambda i, w: (0,) * (len(shape) + 1),
            (len(parts),) + shape,
        )
        for a in leads
    ]
    return combine(groups, where, deps, name="join")


def gather_blocks(both):
    return lax.all_gather(both, (C,) + B + (Z,), axis=0, tiled=False)


def place_kernel(count, quarter, where_ref, *refs):
    ins, out_ref = refs[:count], refs[-1]
    step = pl.program_id(0)
    z = where_ref[2 * count]
    unit = quarter // 4
    for a in range(count):

        @pl.when(step // 2 == a)
        def _():
            for k in range(4):
                rows = pl.ds(pl.multiple_of(lax.rem(z - k + 4, 4) * unit, 16), unit)
                out_ref[0, rows] = ins[a][k * unit : (k + 1) * unit].astype(f32)


def place_relative(parts, out_map, out_shape, before, deps=()):
    values = [v for v, _ in parts]
    count, width = len(parts), values[0].shape[1]
    quarter = values[0].shape[0] // 2
    where = jnp.stack([m for _, marks in parts for m in marks] + [lax.axis_index(Z)])
    return invoke(
        partial(place_kernel, count, quarter),
        values + [before],
        deps,
        scalars=(where.astype(jnp.int32),),
        grid=(2 * count,),
        in_specs=[
            pl.BlockSpec((quarter, width), lambda i, w, a=a: (jnp.clip(i - 2 * a, 0, 1), 0))
            for a in range(count)
        ]
        + [pl.BlockSpec(memory_space=pl.ANY)],
        out_specs=pl.BlockSpec((1, quarter, width), lambda i, w: out_map(w[i])),
        out_shape=jax.ShapeDtypeStruct(out_shape, f32),
        aliases={1 + count: 0},
        name="place",
        us=6,
    )


def spread_kernel(z_first, in_ref, *refs):
    down_ref, up_ref = refs[-2:]
    unit = QUARTER // 4
    for z in range(4):
        rows = slice(z * unit, (z + 1) * unit)
        down_ref[0, rows] = (in_ref[0, z, 0] if z_first else in_ref[0, 0, z]).astype(f32)
        up_ref[0, rows] = (in_ref[0, z, 1] if z_first else in_ref[0, 1, z]).astype(f32)


def place_ordered(rows, layer, before=None, z_first=False, deps=()):
    width = rows.shape[-1]
    hidden = rows.size // width // 2
    inner = (4, 2) if z_first else (2, 4)
    rows = rows.reshape((hidden // QUARTER,) + inner + (QUARTER // 4, width))
    return invoke(
        partial(spread_kernel, z_first),
        [rows] + list(before or ()),
        deps,
        grid=(hidden // QUARTER,),
        in_specs=[pl.BlockSpec((1,) + rows.shape[1:], lambda i: (i, 0, 0, 0, 0))]
        + [pl.BlockSpec(memory_space=pl.ANY)] * len(before or ()),
        out_specs=[
            pl.BlockSpec((1, QUARTER, width), lambda i: (layer, i, 0)),
            pl.BlockSpec((1, QUARTER, TILE), lambda i: (layer, i % 2, i // 2)),
        ],
        out_shape=[
            jax.ShapeDtypeStruct((2, hidden, width), f32),
            jax.ShapeDtypeStruct((2, width, hidden), f32),
        ],
        aliases={1: 0, 2: 1} if before else {},
        name="spread",
        us=10,
    )


def finish_kernel(in_ref, out_ref, q2_ref, qkv_ref, small_ref, flat):
    width = out_ref.shape[2]
    size = in_ref.shape[2]
    for w in range(8):
        for two in range(2):
            for z in range(4):
                at = ((w * 2 + two) * 4 + z) * size
                flat[at : at + size] = in_ref[w * 4 + z, two].astype(f32)
    half = flat.shape[0] // 2
    rest = half - 2 * width
    out_ref[1] = flat[:width]
    q2_ref[...] = flat[width : 2 * width]
    out_ref[0] = flat[half : half + width]
    qkv_ref[:, :width] = flat[half + width : half + 2 * width]
    qkv_ref[:, width:] = flat[2 * width : 2 * width + 128].T
    small_ref[: rest - 128] = flat[2 * width + 128 : half]
    small_ref[rest - 128 :] = flat[half + 2 * width :]


def finish_call(blocks, deps=()):
    width = blocks.shape[-1]
    rows = blocks.size // width
    shapes = [(2, width, width), (width, width), (width, width + 128), (rows - 4 * width - 128, width)]
    return invoke(
        finish_kernel,
        (blocks,),
        deps,
        grid=(1,),
        in_specs=[full_spec(blocks.shape)],
        out_specs=[full_spec(v) for v in shapes],
        out_shape=[jax.ShapeDtypeStruct(v, f32) for v in shapes],
        scratch=[pltpu.VMEM((rows, width), f32)],
        name="finish",
        us=6,
    )


def rotary_tables(positions):
    half_rot = ROT // 2
    inverse = BASE ** (-(jnp.arange(half_rot, dtype=f32) * 2.0 / ROT))
    angles = positions.astype(f32).reshape(-1, 1) * inverse
    cos, sin = jnp.cos(angles), jnp.sin(angles)
    zero = jnp.zeros_like(sin)
    rest = jnp.zeros((cos.shape[0], 64 - ROT), f32)
    head = [
        jnp.concatenate([cos, cos, rest + 1.0], axis=-1),
        jnp.concatenate([-sin, zero, rest], axis=-1),
        jnp.concatenate([zero, sin, rest], axis=-1),
    ]
    return jnp.stack([jnp.concatenate([h, h], axis=-1) for h in head])


def local(
    hidden_in,
    positions,
    cotangent,
    norm_gains,
    norm_biases,
    w_qkv,
    b_qkv,
    w_q2,
    b_q2,
    w_out,
    w_up,
    b_up,
    w_down,
    out_bias,
):
    seqs, group, width = hidden_in.shape
    tokens = seqs * group
    hidden = w_up.shape[2]
    y, x, z, core = (lax.axis_index(a) for a in ("b0", "b1", Z, C))
    core_row = core.reshape(1).astype(jnp.int32)
    where = jnp.stack([y, x, z, core]).astype(jnp.int32)
    direct = square()
    x1 = hidden_in.reshape(tokens, width)
    g2 = cotangent.reshape(tokens, width)
    tab = rotary_tables(positions)

    na1, nm1, q1, kv_own = first_call(x1, norm_gains[0], norm_biases[0], w_qkv, b_qkv, tab, group)
    if direct:
        got = turns(lambda k: kv_own)
        y1, act1, slope1 = mlp_fwd_call(nm1, w_up, b_up, w_down, 0)
        mine = join([v[None] for v in (kv_own, *got)], (0,), where, (y1,))[0]
        theirs = swap(mine, C)
        kv = (mine, theirs)
        back = (z - jnp.arange(4)) % 4 * 2
        order = jnp.concatenate([back + core, back + 1 - core])
        do2 = back_call(g2, w_out, 1, (mine,))
    else:
        kv = (lax.all_gather(kv_own, (Z, C), axis=0, tiled=False),)
        order = jnp.arange(kv[0].shape[0])
        y1, act1, slope1 = mlp_fwd_call(nm1, w_up, b_up, w_down, 0)
        do2 = back_call(g2, w_out, 1)
    first = jnp.concatenate([((z * 2 + core) * group).reshape(1), order]).astype(jnp.int32)
    att1, lse1 = attend_call(first, q1, kv, (do2,))
    x2, na2, nm2, q2 = middle_call(
        att1, x1, y1, w_out, out_bias[0:1], norm_gains[1], norm_biases[1], w_q2, b_q2, tab
    )
    y2, dnm2, send, bup_send = mlp_back_call(core_row, nm2, g2, w_up, w_down, 1, b_up=b_up)
    got = swap(send.reshape(hidden, width), C)
    y2, dnm2, keep, bup_keep = mlp_back_call(
        core_row, nm2, g2, w_up, w_down, 1, b_up=b_up, before=(y2, dnm2)
    )
    keep = keep.reshape(hidden, width)

    def in_order(own, other):
        both = jnp.concatenate([own, other], axis=0)
        return jnp.where(core == 0, both, jnp.concatenate([other, own], axis=0)).reshape(-1, width)

    bup2 = in_order(bup_keep, bup_send)

    def swaps(one, two, axes):
        return swap(one, axes[0]), swap(two, axes[1])

    wait = ()
    if direct:
        one_send, one, two_send, two = sum_cores(keep, got, where)
        one_got, two_got = swaps(one_send, two_send, ("b1", "b0"))
        wait = (one,)
    else:
        mlp2 = add_low(keep, got)
    att2, lse2 = attend_call(first, q2, kv, wait)
    dq2, dkv2 = attend_back_call(first, q2, kv, att2, do2, lse2, tab)
    if direct:
        one_send, one, two_send, two = sum_first(one, one_got, two, two_got, where, (dq2,))
        one_got, two_got = swaps(one_send, two_send, ("b0", "b1"))
        wait = (one,)
    hidden_out, grads2, g1, do1, small2 = turn_call(
        x2, y2, att2, att1, g2, na2, dq2, dnm2, w_out, w_q2, out_bias[1:2], norm_gains[1], deps=wait
    )
    if direct:
        parts = sum_second(one, one_got, two, two_got, where, (g1,))
        ahead = turns(lambda k: parts[k])
        wait = (parts[0],)
    dnm1, send, bup_send = mlp_back_call(
        core_row, nm1, g1, w_up, w_down, 0, kept=(act1, slope1), deps=wait
    )
    got = swap(send.reshape(hidden, width), C)
    dnm1, keep, bup_keep = mlp_back_call(
        core_row, nm1, g1, w_up, w_down, 0, kept=(act1, slope1), before=(dnm1,)
    )
    keep = keep.reshape(hidden, width)
    bup1 = in_order(bup_keep, bup_send)
    if direct:
        one_send, one, two_send, two = sum_cores(keep, got, where)
        one_got, two_got = swaps(one_send, two_send, ("b1", "b0"))
        mlp2 = sum_third([parts[0]] + ahead, where, (one,))
        wait = (mlp2,)
        mlp2 = gather_blocks(mlp2)
    dq1, dkv1 = attend_back_call(
        first, q1, kv, att1, do1, lse1, tab, dkv2, deps=wait + (dnm1,)
    )
    low = dkv1.astype(bf16)
    if direct:
        low = low.reshape(4, 2, group, -1)
        at = lambda c: lax.dynamic_index_in_dim(low, c, 1, keepdims=False)
        dkv_got = swap(at(1 - core), C)
        one_send, one, two_send, two = sum_first(one, one_got, two, two_got, where, (dq1,))
        one_got, two_got = swaps(one_send, two_send, ("b0", "b1"))
        block = (1,) + low.shape[2:]
        dkv_parts = combine(
            [
                (
                    [
                        [
                            (
                                low.reshape((8,) + low.shape[2:]),
                                block,
                                lambda i, w, k=k: (lax.rem(w[2] + k, 4) * 2 + w[3], 0, 0),
                            ),
                            (dkv_got, block, lambda i, w, k=k: (lax.rem(w[2] + k, 4), 0, 0)),
                        ]
                    ],
                    block,
                    lambda i, w: (0, 0, 0),
                    block,
                )
                for k in range(4)
            ],
            where,
            (one,),
            name="sum_kv",
        )
        dkv_got = turns(lambda k: dkv_parts[k])
        dkv = sum_third([dkv_parts[0]] + dkv_got, where)[0]
    else:
        dkv = lax.psum_scatter(low, (Z, C), scatter_dimension=0, tiled=True)
        mlp1 = add_low(keep, got)
    grad_input, grads1, small1 = last_call(x1, g1, na1, dq1, dkv, dnm1, w_qkv, norm_gains[0], tab)
    small = jnp.concatenate(
        [grads1[width:]] + [v.astype(bf16) for v in (small1, small2, bup1, bup2)], axis=0
    )
    extra = 256
    small = jnp.concatenate(
        [small, jnp.zeros((2 * extra - small.shape[0], width), bf16)], axis=0
    )
    rows = jnp.concatenate(
        [grads2[: 2 * width], small[:extra], grads2[2 * width :], grads1[:width], small[extra:]], axis=0
    ).reshape(2, -1, width)
    outs_keep, outs_got = pick(rows, core), swap(pick(rows, 1 - core), C)

    if direct:
        parts = sum_second(one, one_got, two, two_got, where, (grad_input,))
        ahead = turns(lambda k: parts[k])
        o1_send, o1, o2_send, o2 = sum_cores(outs_keep, outs_got, where, (parts[0],))
        o1_got, o2_got = swaps(o1_send, o2_send, ("b1", "b0"))
        both = sum_third([parts[0]] + ahead, where, (o1,))
        ahead = turns(lambda k: both)
        o1_send, o1, o2_send, o2 = sum_first(o1, o1_got, o2, o2_got, where, (both,))
        o1_got, o2_got = swaps(o1_send, o2_send, ("b0", "b1"))
        parts = sum_second(o1, o1_got, o2, o2_got, where)
        outs_ahead = turns(lambda k: parts[k])
        one, two = join([both] + ahead, (0, 1), where, (parts[0],))
        one_got, two_got = swaps(one, two, ("b0", "b1"))
        outs = sum_third([parts[0]] + outs_ahead, where, (one, mlp2))
        outs = gather_blocks(outs)
        one_near, two_near = (
            join([v[None], g[None]], (0,), where)[0].reshape(-1, width)
            for v, g in ((one, one_got), (two, two_got))
        )
        one_far, two_far = swaps(one_near, two_near, ("b1", "b0"))
        one_near_got, two_near_got = swap(one_near, C), swap(two_near, C)
        grad_down, grad_up = place_ordered(mlp2, 1, z_first=True, deps=(one_near, two_near))
        mark = lambda c, v, u: c * 4 + v * 2 + u
        down_map = lambda w: (0, w, 0)
        up_map = lambda w: (0, w % 2, w // 2)

        def down_marks(c, far):
            u = 1 - x if far else x
            return (mark(c, y, u), mark(c, 1 - y, u))

        def up_marks(c, far):
            v = 1 - y if far else y
            return (mark(c, v, x), mark(c, v, 1 - x))

        def put(down, up, one, two, far, cores):
            down = place_relative(
                [(o, down_marks(c, far)) for o, c in zip(one, cores)], down_map, down.shape, down
            )
            up = place_relative(
                [(t, up_marks(c, far)) for t, c in zip(two, cores)], up_map, up.shape, up
            )
            return down, up

        near_one, near_two = (one_near, one_near_got), (two_near, two_near_got)
        grad_down, grad_up = put(grad_down, grad_up, near_one, near_two, False, (core, 1 - core))
        one_far_got, two_far_got = swap(one_far, C), swap(two_far, C)
        grad_down, grad_up = put(grad_down, grad_up, (one_far,), (two_far,), True, (core,))
        grad_down, grad_up = put(
            grad_down, grad_up, (one_far_got,), (two_far_got,), True, (1 - core,)
        )
    else:
        mlp2 = gather_offloaded(reduce_offloaded(mlp2))
        placed = place_ordered(mlp2, 1)
        grad_down, grad_up = place_ordered(gather_offloaded(reduce_offloaded(mlp1)), 0, placed)
        outs = gather_offloaded(reduce_offloaded(add_low(outs_keep, outs_got)))
        outs = outs.reshape(8, 2, 4, -1, width).transpose(0, 2, 1, 3, 4).reshape(32, 2, -1, width)
    grad_out, grad_q2, grad_qkv, small = finish_call(outs)
    one, two = small[0:8], small[8:16]
    ups = hidden // width
    grad_up_bias = jnp.stack([small[16 : 16 + ups].reshape(-1), small[16 + ups : 16 + 2 * ups].reshape(-1)])
    grad_gains = jnp.stack([one[0:2], two[0:2]])
    grad_biases = jnp.stack([one[2:4], two[2:4]])
    grad_qkv_bias = jnp.concatenate([one[4], one[5, :128]])
    grad_out_bias = jnp.stack([two[6], two[4]])
    return (
        hidden_out.reshape(seqs, group, width),
        grad_input.reshape(seqs, group, width),
        grad_gains,
        grad_biases,
        grad_qkv,
        grad_qkv_bias,
        grad_q2,
        two[5],
        grad_out,
        grad_up,
        grad_up_bias,
        grad_down,
        grad_out_bias,
    )


def solution(mesh):
    batch, seq = mesh.shape["batch"], mesh.shape["seq"]
    fine = jax.sharding.Mesh(
        mesh.devices.reshape(2, batch // 2, seq // 2, 2), ("b0", "b1", "z", "c")
    )
    rows = P(B, (Z, C), None)
    return jax.shard_map(
        local,
        mesh=fine,
        in_specs=(rows, P(B, (Z, C)), rows) + (P(),) * 11,
        out_specs=(rows, rows) + (P(),) * 11,
        check_vma=False,
    )
```

```python
from functools import partial

import jax
import jax.numpy as jnp
from jax import lax
from jax.experimental import pallas as pl
from jax.experimental.pallas import tpu as pltpu
from jax.sharding import PartitionSpec as P

ROT = 16
EPSILON = 1e-05
SCALE = 0.125
NEGATIVE = -1e30
BASE = 10000.0

B = ("b0", "b1")
Z = "z"
C = "c"
TILE = 768
QUARTER = TILE // 2
EXTRA = 256
KB = 256

f32 = jnp.float32
bf16 = jnp.bfloat16


def dot_nn(a, b):
    return lax.dot_general(a, b, (((1,), (0,)), ((), ())), preferred_element_type=f32)


def dot_nt(a, b):
    return lax.dot_general(a, b, (((1,), (1,)), ((), ())), preferred_element_type=f32)


def dot_tn(a, b):
    return lax.dot_general(a, b, (((0,), (0,)), ((), ())), preferred_element_type=f32)


def invoke(
    kernel, operands, deps, *, grid, in_specs, out_specs, out_shape, name, scalars=(), scratch=(), aliases={}, us=2, vmem=50
):
    ahead = len(scalars) + len(operands)

    def body(*refs):
        kernel(*refs[:ahead], *refs[ahead + len(deps) :])

    return pl.pallas_call(
        body,
        grid_spec=pltpu.PrefetchScalarGridSpec(
            num_scalar_prefetch=len(scalars),
            grid=grid,
            in_specs=list(in_specs) + [pl.BlockSpec(memory_space=pl.ANY)] * len(deps),
            out_specs=out_specs,
            scratch_shapes=scratch,
        ),
        out_shape=out_shape,
        input_output_aliases=aliases,
        compiler_params=pltpu.CompilerParams(vmem_limit_bytes=vmem << 20),
        cost_estimate=pl.CostEstimate(
            flops=us * 600_000_000, bytes_accessed=us * 1_000_000, transcendentals=0
        ),
        name=name,
    )(*scalars, *operands, *deps)


def layer_spec(shape, layer):
    return pl.BlockSpec((1,) + shape, lambda *i: (layer,) + (0,) * len(shape))


def full_spec(shape):
    return pl.BlockSpec(shape, lambda *i: (0,) * len(shape))


def unit_rows(values):
    center = values - jnp.mean(values, axis=-1, keepdims=True)
    spread = jnp.mean(center * center, axis=-1, keepdims=True)
    inverse = lax.rsqrt(spread + EPSILON)
    return center * inverse, inverse


def turn(values, cos_tab, sin_low, sin_high):
    return (
        values * cos_tab
        + pltpu.roll(values, 120, 1) * sin_low
        + pltpu.roll(values, 8, 1) * sin_high
    )


def pairs_down(values):
    return jnp.concatenate(
        [values[:, p * 128 : (p + 1) * 128] for p in range(values.shape[1] // 128)], axis=0
    )


def gelu_parts(lifted):
    cdf = 0.5 + 0.5 * lax.erf(lifted * 0.7071067811865476)
    slope = cdf + lifted * (0.3989422804014327 * jnp.exp(-0.5 * lifted * lifted))
    return lifted * cdf, slope


def first_kernel(x_ref, gain_ref, off_ref, w_ref, b_ref, tab_ref, na_ref, nm_ref, q_ref, kv_ref):
    tokens, width = x_ref.shape
    unit = unit_rows(x_ref[...].astype(f32))[0]
    norm_a = (unit * gain_ref[0:1] + off_ref[0:1]).astype(bf16)
    na_ref[...] = norm_a
    nm_ref[...] = (unit * gain_ref[1:2] + off_ref[1:2]).astype(bf16)
    cos_tab, sin_low, sin_high = tab_ref[0], tab_ref[1], tab_ref[2]
    kv = dot_nn(norm_a, w_ref[:, width:]) + b_ref[:, width:]
    low_half = lax.broadcasted_iota(jnp.int32, kv.shape, 1) < 64
    kv = jnp.where(low_half, turn(kv, cos_tab, sin_low, sin_high), kv).astype(bf16)
    group = kv_ref.shape[0]
    for s in range(tokens // group):
        kv_ref[:, s * 128 : (s + 1) * 128] = kv[s * group : (s + 1) * group]
    proj = dot_nn(norm_a, w_ref[:, :width]) + b_ref[:, :width]
    for p in range(width // 128):
        cols = slice(p * 128, (p + 1) * 128)
        q_ref[:, cols] = (turn(proj[:, cols], cos_tab, sin_low, sin_high) * SCALE).astype(bf16)


def first_call(x, gains, offs, w_qkv, b_qkv, tab, group):
    tokens, width = x.shape
    operands = (x, gains, offs, w_qkv, b_qkv.reshape(1, -1), tab)
    shapes = [(tokens, width)] * 3 + [(group, tokens // group * 128)]
    return invoke(
        first_kernel,
        operands,
        (),
        grid=(1,),
        in_specs=[full_spec(v.shape) for v in operands],
        out_specs=[full_spec(v) for v in shapes],
        out_shape=[jax.ShapeDtypeStruct(v, bf16) for v in shapes],
        name="first",
        us=3,
    )


def mlp_fwd_kernel(nm_ref, up_ref, bup_ref, down_ref, y_ref, act_ref, slope_ref):
    lifted = dot_nn(nm_ref[...], up_ref[0]) + bup_ref[...]
    active, slope = gelu_parts(lifted)
    active = active.astype(bf16)
    act_ref[...] = active
    slope_ref[...] = slope.astype(bf16)

    @pl.when(pl.program_id(0) == 0)
    def _():
        y_ref[...] = jnp.zeros_like(y_ref)

    y_ref[...] += dot_nn(active, down_ref[0])


def mlp_fwd_call(nm, w_up, b_up, w_down, layer):
    tokens, width = nm.shape
    hidden = w_up.shape[2]
    return invoke(
        mlp_fwd_kernel,
        (nm, w_up, b_up[layer : layer + 1], w_down),
        (),
        grid=(hidden // TILE,),
        in_specs=[
            full_spec((tokens, width)),
            pl.BlockSpec((1, width, TILE), lambda t: (layer, 0, t)),
            pl.BlockSpec((1, TILE), lambda t: (0, t)),
            pl.BlockSpec((1, TILE, width), lambda t: (layer, t, 0)),
        ],
        out_specs=[
            full_spec((tokens, width)),
            pl.BlockSpec((tokens, TILE), lambda t: (0, t)),
            pl.BlockSpec((tokens, TILE), lambda t: (0, t)),
        ],
        out_shape=[
            jax.ShapeDtypeStruct((tokens, width), f32),
            jax.ShapeDtypeStruct((tokens, hidden), bf16),
            jax.ShapeDtypeStruct((tokens, hidden), bf16),
        ],
        name="mlp_fwd",
        us=10,
    )


def mlp_grads(active, slope, nm, nm_turned, grad, up, down, start, refs):
    grad_norm_ref, rows_ref, bias_ref = refs
    grad_lifted = (dot_nt(grad, down) * slope).astype(bf16)
    bias_ref[...] = jnp.sum(grad_lifted.astype(f32), axis=0, keepdims=True)

    @pl.when(pl.program_id(0) == 0)
    def _():
        grad_norm_ref[...] = jnp.zeros_like(grad_norm_ref) if start is None else start[...]
        nm_turned[...] = nm.T

    grad_norm_ref[...] += dot_nt(grad_lifted, up)
    grad_down = dot_tn(active, grad).astype(bf16)
    grad_up = dot_nn(nm_turned[...], grad_lifted).astype(bf16)
    for j in range(2):
        rows = slice(j * QUARTER, (j + 1) * QUARTER)
        rows_ref[0, 2 * j * QUARTER : (2 * j + 1) * QUARTER] = grad_down[rows]
        rows_ref[0, (2 * j + 1) * QUARTER : (2 * j + 2) * QUARTER] = grad_up[rows]


def mlp_both_kernel(more, core_ref, nm_ref, g_ref, up_ref, bup_ref, down_ref, *refs):
    y_start, grad_start = refs[:2] if more else (None, None)
    y_ref, *outs, nm_turned = refs[2:] if more else refs
    nm, up, down = nm_ref[...], up_ref[0], down_ref[0]
    active, slope = gelu_parts(dot_nn(nm, up) + bup_ref[...])
    active = active.astype(bf16)

    @pl.when(pl.program_id(0) == 0)
    def _():
        y_ref[...] = y_start[...] if more else jnp.zeros_like(y_ref)

    y_ref[...] += dot_nn(active, down)
    mlp_grads(active, slope, nm, nm_turned, g_ref[...], up, down, grad_start, outs)


def mlp_back_kernel(more, core_ref, nm_ref, g_ref, up_ref, down_ref, act_ref, slope_ref, *refs):
    grad_start = refs[0] if more else None
    *outs, nm_turned = refs[1:] if more else refs
    slope = slope_ref[...].astype(f32)
    mlp_grads(
        act_ref[...], slope, nm_ref[...], nm_turned, g_ref[...], up_ref[0], down_ref[0], grad_start, outs
    )


def mlp_back_call(core, nm, grad, w_up, w_down, layer, b_up=None, kept=None, before=None, deps=()):
    tokens, width = nm.shape
    hidden = w_up.shape[2]
    half = hidden // TILE // 2
    other = before is None

    def tile(t, core_ref):
        c = core_ref[0]
        return (1 - c if other else c) * half + t

    whole = full_spec((tokens, width))
    whole_shape = jax.ShapeDtypeStruct((tokens, width), f32)
    up_spec = pl.BlockSpec((1, width, TILE), lambda t, c: (layer, 0, tile(t, c)))
    down_spec = pl.BlockSpec((1, TILE, width), lambda t, c: (layer, tile(t, c), 0))
    cols_spec = pl.BlockSpec((tokens, TILE), lambda t, c: (0, tile(t, c)))
    both = kept is None
    if both:
        bias_spec = pl.BlockSpec((1, TILE), lambda t, c: (0, tile(t, c)))
        in_specs = [whole, whole, up_spec, bias_spec, down_spec]
        operands = (nm, grad, w_up, b_up[layer : layer + 1], w_down)
    else:
        in_specs = [whole, whole, up_spec, down_spec, cols_spec, cols_spec]
        operands = (nm, grad, w_up, w_down) + kept
    before = tuple(before or ())
    count = 2 if both else 1
    return invoke(
        partial(mlp_both_kernel if both else mlp_back_kernel, not other),
        operands + before,
        deps,
        scalars=(core,),
        grid=(half,),
        in_specs=in_specs + [whole] * len(before),
        out_specs=[whole] * count
        + [
            pl.BlockSpec((1, 2 * TILE, width), lambda t, c: (t, 0, 0)),
            pl.BlockSpec((1, TILE), lambda t, c: (0, t)),
        ],
        out_shape=[whole_shape] * count
        + [
            jax.ShapeDtypeStruct((half, 2 * TILE, width), bf16),
            jax.ShapeDtypeStruct((1, hidden // 2), f32),
        ],
        scratch=[pltpu.VMEM((width, tokens), bf16)],
        name="mlp_both" if both else "mlp_back",
        us=40 if both else (12 if other else 150),
    )


def spread_kv(pieces, order_ref, k0, k1, turned, forward):
    at = 0
    for ref in pieces:
        for p in range(ref.shape[0]):
            kv = ref[p].astype(f32)
            rows = kv.shape[0]
            swapped = pltpu.roll(kv, 64, 1)
            low_half = lax.broadcasted_iota(jnp.int32, kv.shape, 1) < 64
            zero = jnp.zeros_like(kv)
            block = order_ref[1 + at]
            place = pl.ds(pl.multiple_of(block * rows, rows), rows)
            k0[place] = jnp.where(low_half, kv, zero).astype(bf16)
            k1[place] = jnp.where(low_half, zero, swapped).astype(bf16)
            if forward:
                t0, t1 = turned
                rest = jnp.ones((64, rows), f32)
                part = kv.T[64:]
            else:
                v0, v1, t0, t1 = turned
                v0[place] = jnp.where(low_half, swapped, zero).astype(bf16)
                v1[place] = jnp.where(low_half, zero, kv).astype(bf16)
                rest = jnp.zeros((64, rows), f32)
                part = kv.T[:64]
            t0[block] = jnp.concatenate([part, rest], axis=0).astype(bf16)
            t1[block] = jnp.concatenate([rest, part], axis=0).astype(bf16)
            at += 1


def block_rows(index):
    return pl.ds(pl.multiple_of(index * KB, KB), KB)


def turned_block(ref, index):
    return jnp.concatenate([ref[2 * index], ref[2 * index + 1]], axis=1)


def visible(shape, first, start, group):
    key = lax.broadcasted_iota(jnp.int32, shape, 0)
    token = lax.broadcasted_iota(jnp.int32, shape, 1) % group
    return key - token <= first - start


def attend_kernel(count, first_ref, q_ref, *refs):
    pieces, (o_ref, lse_ref, k0, k1, t0, t1) = refs[:count], refs[count:]
    first = first_ref[0]
    group, width = q_ref.shape
    spread_kv(pieces, first_ref, k0, k1, (t0, t1), True)
    q6 = pairs_down(q_ref[...])
    full = first // KB

    def block(kb, carry):
        done = []
        for keys, vals, (top, summed) in zip((k0, k1), (t0, t1), carry or (2 * ((None, None),))):
            scores = dot_nt(keys[block_rows(kb), :], q6)
            if carry is None:
                scores = jnp.where(
                    visible(scores.shape, first, full * KB, group), scores, NEGATIVE
                )
            new_top = jnp.max(scores, axis=0, keepdims=True)
            if carry is not None:
                new_top = jnp.maximum(top, new_top)
            weights = jnp.exp(scores - new_top).astype(bf16)
            part = dot_nn(turned_block(vals, kb), weights)
            if carry is not None:
                part = part + summed * jnp.exp(top - new_top)
            done.append((new_top, part))
        return tuple(done)

    (top0, sum0), (top1, sum1) = lax.fori_loop(0, full, block, block(full, None))
    total0, total1 = sum0[64:65], sum1[0:1]
    both = jnp.concatenate([sum0[:64] / total0, sum1[64:] / total1], axis=0).T.astype(bf16)
    for p in range(width // 128):
        o_ref[:, p * 128 : (p + 1) * 128] = both[p * group : (p + 1) * group]
    shape = lse_ref.shape[2:]
    lse_ref[0, 0] = jnp.broadcast_to(top0 + jnp.log(total0), shape)
    lse_ref[0, 1] = jnp.broadcast_to(top1 + jnp.log(total1), shape)


def piece_specs(kv):
    return [pl.BlockSpec(v.shape[:2] + (128,), lambda s, f: (0, 0, s)) for v in kv]


def attend_call(first, q, kv, deps=()):
    tokens, width = q.shape
    length = sum(v.shape[0] for v in kv) * kv[0].shape[1]
    seqs = kv[0].shape[2] // 128
    group = tokens // seqs
    rows = group * width // 128
    return invoke(
        partial(attend_kernel, len(kv)),
        (q,) + kv,
        deps,
        scalars=(first,),
        grid=(seqs,),
        in_specs=[pl.BlockSpec((group, width), lambda s, f: (s, 0))] + piece_specs(kv),
        out_specs=[
            pl.BlockSpec((group, width), lambda s, f: (s, 0)),
            pl.BlockSpec((1, 2, 8, rows), lambda s, f: (s, 0, 0, 0)),
        ],
        scratch=[pltpu.VMEM((length, 128), bf16)] * 2
        + [pltpu.VMEM((length // 128, 128, 128), bf16)] * 2,
        out_shape=[
            jax.ShapeDtypeStruct((tokens, width), bf16),
            jax.ShapeDtypeStruct((seqs, 2, 8, rows), f32),
        ],
        name="attend",
        us=60,
    )


def attend_back_kernel(count, has_start, unread, first_ref, q_ref, *refs):
    pieces, refs = refs[:count], refs[count:]
    ins = 5 if has_start else 4
    refs = refs[:ins] + refs[ins + unread :]
    if has_start:
        o_ref, do_ref, lse_ref, tab_ref, start_ref, dq_out, dkv_ref, k0, k1, v0, v1, t0, t1, dq_ref = refs
        dkv_ref[...] = start_ref[...]
    else:
        o_ref, do_ref, lse_ref, tab_ref, dq_out, dkv_ref, k0, k1, v0, v1, t0, t1, dq_ref = refs
        dkv_ref[...] = jnp.zeros_like(dkv_ref)
    first = first_ref[0]
    group = q_ref.shape[0]
    spread_kv(pieces, first_ref, k0, k1, (v0, v1, t0, t1), False)
    q6 = pairs_down(q_ref[...])
    do6 = pairs_down(do_ref[...])
    deltas = (do6.astype(f32) * pairs_down(o_ref[...]).astype(f32)).T
    halves = (
        (k0, v0, lse_ref[0, 0, 0:1], jnp.sum(deltas[:64], axis=0, keepdims=True)),
        (k1, v1, lse_ref[0, 1, 0:1], jnp.sum(deltas[64:], axis=0, keepdims=True)),
    )
    dq_ref[...] = jnp.zeros_like(dq_ref)
    full = first // KB
    low_half = lax.broadcasted_iota(jnp.int32, (KB, 128), 1) < 64

    def block(kb, masked):
        rows = block_rows(kb)
        grads, keys, vals = [], [], []
        for k, v, lse, delta in halves:
            probs = jnp.exp(dot_nt(k[rows, :], q6) - lse)
            if masked:
                probs = jnp.where(visible(probs.shape, first, full * KB, group), probs, 0.0)
            grad_probs = dot_nt(v[rows, :], do6)
            grad_scores = (probs * (grad_probs - delta)).astype(bf16)
            grads.append(grad_scores)
            keys.append(dot_nn(grad_scores, q6))
            vals.append(dot_nn(probs.astype(bf16), do6))
        dkv_ref[rows, :] += jnp.where(low_half, keys[0], vals[1]) + pltpu.roll(
            jnp.where(low_half, vals[0], keys[1]), 64, 1
        )
        turned = jnp.concatenate([turned_block(t0, kb), turned_block(t1, kb)], axis=1)
        dq_ref[...] += dot_nn(turned, jnp.concatenate(grads, axis=0))

    block(full, True)

    def step(kb, carry):
        block(kb, False)
        return carry

    lax.fori_loop(0, full, step, 0)
    cos_tab, sin_low, sin_high = tab_ref[0], -tab_ref[1], -tab_ref[2]
    dq = dq_ref[...].T * SCALE
    for p in range(q_ref.shape[1] // 128):
        part = dq[p * group : (p + 1) * group]
        dq_out[:, p * 128 : (p + 1) * 128] = turn(part, cos_tab, sin_low, sin_high).astype(bf16)


def attend_back_call(first, q, kv, attended, grad, lse, tab, part, start=None, before=(), deps=()):
    tokens, width = q.shape
    length = sum(v.shape[0] for v in kv) * kv[0].shape[1]
    seqs = kv[0].shape[2] // 128
    group = tokens // seqs
    rows = group * width // 128
    count = seqs if part is None else seqs // 2
    at = (part or 0) * count
    tok_spec = pl.BlockSpec((group, width), lambda s, f: (at + s, 0))
    len_spec = pl.BlockSpec((length, 128), lambda s, f: (0, at + s))
    in_specs = [
        tok_spec,
        *[pl.BlockSpec(v.shape[:2] + (128,), lambda s, f: (0, 0, at + s)) for v in kv],
        tok_spec,
        tok_spec,
        pl.BlockSpec((1, 2, 8, rows), lambda s, f: (at + s, 0, 0, 0)),
        pl.BlockSpec((3, group, 128), lambda s, f: (0, at + s, 0)),
    ]
    operands = [q, *kv, attended, grad, lse, tab]
    if start is not None:
        in_specs.append(len_spec)
        operands.append(start)
    return invoke(
        partial(attend_back_kernel, len(kv), start is not None, len(before)),
        operands + list(before),
        deps,
        scalars=(first,),
        grid=(count,),
        in_specs=in_specs + [pl.BlockSpec(memory_space=pl.ANY)] * len(before),
        out_specs=[tok_spec, len_spec],
        scratch=[pltpu.VMEM((length, 128), bf16)] * 4
        + [pltpu.VMEM((length // 128, 128, 128), bf16)] * 2
        + [pltpu.VMEM((128, rows), f32)],
        out_shape=[
            jax.ShapeDtypeStruct((tokens, width), bf16),
            jax.ShapeDtypeStruct((length, seqs * 128), f32),
        ],
        aliases={1 + len(operands) + i: i for i in range(len(before))},
        name="attend_back",
        us=45,
    )


def back_kernel(g_ref, w_ref, out_ref):
    out_ref[...] = dot_nt(g_ref[...], w_ref[0]).astype(bf16)


def back_call(grad, w_out, layer, deps=()):
    tokens, width = grad.shape
    return invoke(
        back_kernel,
        (grad, w_out),
        deps,
        grid=(1,),
        in_specs=[full_spec((tokens, width)), layer_spec((width, width), layer)],
        out_specs=full_spec((tokens, width)),
        out_shape=jax.ShapeDtypeStruct((tokens, width), bf16),
        name="back",
    )


def middle_kernel(
    att_ref, x_ref, y_ref, wo_ref, bias_ref, gain_ref, off_ref, wq_ref, bq_ref, tab_ref,
    x2_ref, na_ref, nm_ref, q_ref,
):
    second = (
        x_ref[...].astype(f32) + dot_nn(att_ref[...], wo_ref[0]) + y_ref[...] + bias_ref[...]
    ).astype(bf16)
    x2_ref[...] = second
    unit = unit_rows(second.astype(f32))[0]
    norm_a = (unit * gain_ref[0:1] + off_ref[0:1]).astype(bf16)
    na_ref[...] = norm_a
    nm_ref[...] = (unit * gain_ref[1:2] + off_ref[1:2]).astype(bf16)
    proj = dot_nn(norm_a, wq_ref[...]) + bq_ref[...]
    cos_tab, sin_low, sin_high = tab_ref[0], tab_ref[1], tab_ref[2]
    for p in range(proj.shape[1] // 128):
        cols = slice(p * 128, (p + 1) * 128)
        q_ref[:, cols] = (turn(proj[:, cols], cos_tab, sin_low, sin_high) * SCALE).astype(bf16)


def middle_call(att, x, y, w_out, bias, gains, offs, w_q2, b_q2, tab):
    tokens, width = x.shape
    operands = (att, x, y, w_out, bias, gains, offs, w_q2, b_q2.reshape(1, -1), tab)
    specs = [full_spec(v.shape) for v in operands]
    specs[3] = layer_spec((width, width), 0)
    return invoke(
        middle_kernel,
        operands,
        (),
        grid=(1,),
        in_specs=specs,
        out_specs=[full_spec((tokens, width))] * 4,
        out_shape=[jax.ShapeDtypeStruct((tokens, width), bf16)] * 4,
        name="middle",
        us=5,
    )


def norm_back(values, grad_a, grad_m, gain_ref, small_ref, row):
    unit, inverse = unit_rows(values)
    small_ref[row : row + 1] = jnp.sum(grad_a * unit, axis=0, keepdims=True)
    small_ref[row + 1 : row + 2] = jnp.sum(grad_m * unit, axis=0, keepdims=True)
    small_ref[row + 2 : row + 3] = jnp.sum(grad_a, axis=0, keepdims=True)
    small_ref[row + 3 : row + 4] = jnp.sum(grad_m, axis=0, keepdims=True)
    grad_unit = grad_a * gain_ref[0:1] + grad_m * gain_ref[1:2]
    return inverse * (
        grad_unit
        - jnp.mean(grad_unit, axis=-1, keepdims=True)
        - unit * jnp.mean(grad_unit * unit, axis=-1, keepdims=True)
    )


def by_core(core, send_ref, keep_ref, put):
    @pl.when(core == 0)
    def _():
        put(keep_ref, send_ref)

    @pl.when(core != 0)
    def _():
        put(send_ref, keep_ref)


def turn_kernel(
    x2_ref, y_ref, att2_ref, att1_ref, g_ref, na_ref, dq_ref, dnm_ref, wo1_ref, wo2_ref, wq_ref, bias_ref, gain_ref,
    hidden_ref, grads_ref, g1_ref, do1_ref, small_ref,
):
    width = x2_ref.shape[1]
    second = x2_ref[...].astype(f32)
    att2, grad, dq = att2_ref[...], g_ref[...], dq_ref[...]
    wide = grad.astype(f32)
    small_ref[...] = jnp.zeros_like(small_ref)
    grad_a = dot_nt(dq, wq_ref[...])
    g1 = (norm_back(second, grad_a, dnm_ref[...], gain_ref, small_ref, 0) + wide).astype(bf16)
    g1_ref[...] = g1
    do1_ref[...] = dot_nt(g1, wo1_ref[0]).astype(bf16)
    small_ref[4:5] = jnp.sum(wide, axis=0, keepdims=True)
    small_ref[5:6] = jnp.sum(dq.astype(f32), axis=0, keepdims=True)
    small_ref[6:7] = jnp.sum(g1.astype(f32), axis=0, keepdims=True)
    grads_ref[0:width] = dot_tn(att2, grad).astype(bf16)
    grads_ref[width : 2 * width] = dot_tn(na_ref[...], dq).astype(bf16)
    grads_ref[2 * width : 3 * width] = dot_tn(att1_ref[...], g1).astype(bf16)
    hidden_ref[...] = (second + dot_nn(att2, wo2_ref[0]) + y_ref[...] + bias_ref[...]).astype(bf16)


def turn_call(x2, y2, att2, att1, g, na2, dq2, dnm2, w_out, w_q2, bias, gains, deps=()):
    tokens, width = x2.shape
    operands = (x2, y2, att2, att1, g, na2, dq2, dnm2, w_out, w_out, w_q2, bias, gains)
    specs = [full_spec(v.shape) for v in operands]
    specs[8] = layer_spec((width, width), 0)
    specs[9] = layer_spec((width, width), 1)
    tok = full_spec((tokens, width))
    tok_shape = jax.ShapeDtypeStruct((tokens, width), bf16)
    return invoke(
        turn_kernel,
        operands,
        deps,
        grid=(1,),
        in_specs=specs,
        out_specs=[tok, full_spec((3 * width, width)), tok, tok, full_spec((8, width))],
        out_shape=[
            tok_shape,
            jax.ShapeDtypeStruct((3 * width, width), bf16),
            tok_shape,
            tok_shape,
            jax.ShapeDtypeStruct((8, width), f32),
        ],
        name="turn",
        us=60,
    )


def last_kernel(
    core_ref, x_ref, g1_ref, na_ref, dq_ref, dkv_ref, dnm_ref, w_ref, gain_ref, tab_ref, small2_ref, bup1_ref, bup2_ref,
    early_ref, grad_ref, send_ref, keep_ref, small_ref,
):
    tokens, width = x_ref.shape
    group = dkv_ref.shape[0]
    dkv = jnp.concatenate(
        [dkv_ref[:, s * 128 : (s + 1) * 128] for s in range(tokens // group)], axis=0
    ).astype(f32)
    low_half = lax.broadcasted_iota(jnp.int32, dkv.shape, 1) < 64
    dkv = jnp.where(low_half, turn(dkv, tab_ref[0], -tab_ref[1], -tab_ref[2]), dkv).astype(bf16)
    dq, norm_a = dq_ref[...], na_ref[...]
    small_ref[...] = jnp.zeros_like(small_ref)
    small_ref[4:5] = jnp.sum(dq.astype(f32), axis=0, keepdims=True)
    small_ref[5:6, 0:128] = jnp.sum(dkv.astype(f32), axis=0, keepdims=True)
    grad_a = dot_nt(dq, w_ref[:, :width]) + dot_nt(dkv, w_ref[:, width:])
    grad_ref[...] = g1_ref[...].astype(f32) + norm_back(
        x_ref[...].astype(f32), grad_a, dnm_ref[...], gain_ref, small_ref, 0
    )
    q1 = dot_tn(norm_a, dq).astype(bf16)
    kv = dot_tn(dkv, norm_a).astype(bf16)
    smalls = [small_ref[...], small2_ref[...], bup1_ref[...], bup2_ref[...]]
    smalls.append(jnp.zeros((EXTRA - 128 - sum(v.shape[0] for v in smalls), width), f32))
    smalls = jnp.concatenate(smalls, axis=0).astype(bf16)

    def put(one, two):
        one[: 2 * width] = early_ref[: 2 * width]
        one[2 * width : 2 * width + 128] = kv
        one[2 * width + 128 :] = smalls
        two[:width] = early_ref[2 * width :]
        two[width : 2 * width] = q1
        two[2 * width :] = jnp.zeros((EXTRA, width), bf16)

    by_core(core_ref[0], send_ref, keep_ref, put)


def last_call(core, x, g1, na1, dq1, dkv, dnm1, w_qkv, gains, tab, small2, bup1, bup2, early, deps=()):
    tokens, width = x.shape
    operands = (x, g1, na1, dq1, dkv, dnm1, w_qkv, gains, tab, small2, bup1, bup2, early)
    out_shape = [
        jax.ShapeDtypeStruct((tokens, width), f32),
        jax.ShapeDtypeStruct((2 * width + EXTRA, width), bf16),
        jax.ShapeDtypeStruct((2 * width + EXTRA, width), bf16),
    ]
    return invoke(
        last_kernel,
        operands,
        deps,
        scalars=(core,),
        grid=(1,),
        in_specs=[full_spec(v.shape) for v in operands],
        out_specs=[full_spec(v.shape) for v in out_shape],
        out_shape=out_shape,
        scratch=[pltpu.VMEM((8, width), f32)],
        name="last",
        us=10,
    )


PAIR = [(0, 1), (1, 0)]


def swap(values, axis):
    return lax.ppermute(values, axis, PAIR)


def add_low(first, *rest):
    total = first.astype(f32)
    for value in rest:
        total = total + value.astype(f32)
    return total.astype(bf16)


def pick(values, index):
    return lax.dynamic_index_in_dim(values, index, 0, keepdims=False)


def square():
    return lax.axis_size("b0") == 2 and lax.axis_size("b1") == 2 and lax.axis_size(Z) == 4


def turns(values_at):
    size = lax.axis_size(Z)
    return [
        lax.ppermute(values_at(k), Z, [(i, (i + k) % size) for i in range(size)])
        for k in range(1, size)
    ]


def reduce_offloaded(part):
    part = lax.psum_scatter(part, B, scatter_dimension=0, tiled=True)
    return lax.psum_scatter(part, Z, scatter_dimension=0, tiled=True)


def gather_offloaded(part):
    return lax.all_gather(part, (C,) + B + (Z,), axis=0, tiled=True)


def combine(groups, where, deps, grid=(1,), name="combine", us=2, vmem=50):
    terms = [t for sums, *_ in groups for parts in sums for t in parts]

    def kernel(where_ref, *refs):
        ins, outs = iter(refs[: len(terms)]), refs[len(terms) :]
        for (sums, *_), out_ref in zip(groups, outs):
            for i, parts in enumerate(sums):
                total = next(ins)[...].astype(f32)
                for _ in parts[1:]:
                    total = total + next(ins)[...].astype(f32)
                if len(sums) == 1:
                    out_ref[...] = total.reshape(out_ref.shape).astype(bf16)
                else:
                    out_ref[i] = total.reshape(out_ref.shape[1:]).astype(bf16)

    return invoke(
        kernel,
        [t[0] for t in terms],
        deps,
        scalars=(where,),
        grid=grid,
        in_specs=[pl.BlockSpec(t[1], t[2]) for t in terms],
        out_specs=[pl.BlockSpec(g[1], g[2]) for g in groups],
        out_shape=[jax.ShapeDtypeStruct(g[3], bf16) for g in groups],
        name=name,
        us=us,
        vmem=vmem,
    )


def sum_cores(keep, got, where, deps=(), us=20):
    width = keep.shape[-1]
    keep, got = (v.reshape(2, 2, 2, -1, width) for v in (keep, got))
    quarter = keep.shape[3]
    half = quarter // 2
    maps = (
        lambda i, j, w: (i, 1 - w[1], 0, j, 0),
        lambda i, j, w: (i, w[1], 0, j, 0),
        lambda i, j, w: (1 - w[0], i, 1, j, 0),
        lambda i, j, w: (w[0], i, 1, j, 0),
    )
    block = (1, 1, 1, half, width)
    groups = [
        (
            [[(keep, block, m), (got, block, m)]],
            (1, half, width),
            lambda i, j, w: (i, j, 0),
            (2, quarter, width),
        )
        for m in maps
    ]
    return combine(groups, where, deps, grid=(2, 2), name="sum_cores", us=us)


def sum_first(one, one_got, two, two_got, where, deps=(), us=30):
    _, quarter, width = one.shape
    half = quarter // 2
    groups = []
    for values, got, m in (
        (one, one_got, lambda j, w: (1 - w[0], j, 0)),
        (one, one_got, lambda j, w: (w[0], j, 0)),
        (two, two_got, lambda j, w: (1 - w[1], j, 0)),
        (two, two_got, lambda j, w: (w[1], j, 0)),
    ):
        block = (1, half, width)
        groups.append(
            ([[(values, block, m), (got, block, m)]], block, lambda j, w: (0, j, 0), (1, quarter, width))
        )
    return combine(groups, where, deps, grid=(2,), name="sum_first", us=us)


def sum_second(one, one_got, two, two_got, where, deps=(), us=100):
    width = one.shape[-1]
    one, one_got, two, two_got = (v.reshape(4, -1, width) for v in (one, one_got, two, two_got))
    block = (1,) + one.shape[1:]
    groups = []
    for k in range(4):
        m = lambda i, w, k=k: (lax.rem(w[2] + k, 4), 0, 0)
        groups.append(
            (
                [[(a, block, m), (b, block, m)] for a, b in ((one, one_got), (two, two_got))],
                (2,) + one.shape[1:],
                lambda i, w: (0, 0, 0),
                (2,) + one.shape[1:],
            )
        )
    return combine(groups, where, deps, name="sum_second", us=us)


def sum_third(parts, where, deps=(), us=10):
    shape = parts[0].shape
    m = lambda i, w: (0, 0, 0)
    return combine([([[(p, shape, m) for p in parts]], shape, m, shape)], where, deps, name="sum_third", us=us)[0]


def join(parts, leads, where, deps=()):
    shape = parts[0].shape[1:]
    groups = [
        (
            [[(p, (1,) + shape, lambda i, w, a=a: (a,) + (0,) * len(shape))] for p in parts],
            (len(parts),) + shape,
            lambda i, w: (0,) * (len(shape) + 1),
            (len(parts),) + shape,
        )
        for a in leads
    ]
    return combine(groups, where, deps, name="join")


def gather_blocks(both):
    return lax.all_gather(both, (C,) + B + (Z,), axis=0, tiled=False)


def relay(values, where, deps):
    block = (values[0].shape[0] // 2, values[0].shape[1])
    m = lambda i, w: (i, 0)
    groups = [([[(v, block, m)]], block, m, v.shape) for v in values]
    return combine(groups, where, deps, grid=(2,), name="relay")


def place_kernel(count, quarter, where_ref, *refs):
    ins, out_ref = refs[:count], refs[-1]
    step = pl.program_id(0)
    z = where_ref[2 * count]
    unit = quarter // 4
    for a in range(count):

        @pl.when(step // 2 == a)
        def _():
            for k in range(4):
                rows = pl.ds(pl.multiple_of(lax.rem(z - k + 4, 4) * unit, 16), unit)
                out_ref[0, rows] = ins[a][k * unit : (k + 1) * unit].astype(f32)


def place_relative(parts, out_map, out_shape, before, deps=()):
    values = [v for v, _ in parts]
    count, width = len(parts), values[0].shape[1]
    quarter = values[0].shape[0] // 2
    where = jnp.stack([m for _, marks in parts for m in marks] + [lax.axis_index(Z)])
    return invoke(
        partial(place_kernel, count, quarter),
        values + [before],
        deps,
        scalars=(where.astype(jnp.int32),),
        grid=(2 * count,),
        in_specs=[
            pl.BlockSpec((quarter, width), lambda i, w, a=a: (jnp.clip(i - 2 * a, 0, 1), 0))
            for a in range(count)
        ]
        + [pl.BlockSpec(memory_space=pl.ANY)],
        out_specs=pl.BlockSpec((1, quarter, width), lambda i, w: out_map(w[i])),
        out_shape=jax.ShapeDtypeStruct(out_shape, f32),
        aliases={1 + count: 0},
        name="place",
        us=2,
    )


def spread_kernel(z_first, in_ref, *refs):
    down_ref, up_ref = refs[-2:]
    unit = QUARTER // 4
    for z in range(4):
        rows = slice(z * unit, (z + 1) * unit)
        down_ref[0, rows] = (in_ref[0, z, 0] if z_first else in_ref[0, 0, z]).astype(f32)
        up_ref[0, rows] = (in_ref[0, z, 1] if z_first else in_ref[0, 1, z]).astype(f32)


def place_ordered(rows, layer, before=None, z_first=False, deps=()):
    width = rows.shape[-1]
    hidden = rows.size // width // 2
    inner = (4, 2) if z_first else (2, 4)
    rows = rows.reshape((hidden // QUARTER,) + inner + (QUARTER // 4, width))
    return invoke(
        partial(spread_kernel, z_first),
        [rows] + list(before or ()),
        deps,
        grid=(hidden // QUARTER,),
        in_specs=[pl.BlockSpec((1,) + rows.shape[1:], lambda i: (i, 0, 0, 0, 0))]
        + [pl.BlockSpec(memory_space=pl.ANY)] * len(before or ()),
        out_specs=[
            pl.BlockSpec((1, QUARTER, width), lambda i: (layer, i, 0)),
            pl.BlockSpec((1, QUARTER, TILE), lambda i: (layer, i % 2, i // 2)),
        ],
        out_shape=[
            jax.ShapeDtypeStruct((2, hidden, width), f32),
            jax.ShapeDtypeStruct((2, width, hidden), f32),
        ],
        aliases={1: 0, 2: 1} if before else {},
        name="spread",
        us=2,
    )


def finish_kernel(in_ref, out_ref, q2_ref, qkv_ref, small_ref, flat):
    width = out_ref.shape[2]
    size = in_ref.shape[2]
    for w in range(8):
        for two in range(2):
            for z in range(4):
                at = ((w * 2 + two) * 4 + z) * size
                flat[at : at + size] = in_ref[w * 4 + z, two].astype(f32)
    half = flat.shape[0] // 2
    out_ref[1] = flat[:width]
    q2_ref[...] = flat[width : 2 * width]
    out_ref[0] = flat[half : half + width]
    qkv_ref[:, :width] = flat[half + width : half + 2 * width]
    qkv_ref[:, width:] = flat[2 * width : 2 * width + 128].T
    small_ref[...] = flat[2 * width + 128 : half]


def finish_call(blocks):
    width = blocks.shape[-1]
    rows = blocks.size // width
    shapes = [(2, width, width), (width, width), (width, width + 128), (EXTRA - 128, width)]
    return invoke(
        finish_kernel,
        (blocks,),
        (),
        grid=(1,),
        in_specs=[full_spec(blocks.shape)],
        out_specs=[full_spec(v) for v in shapes],
        out_shape=[jax.ShapeDtypeStruct(v, f32) for v in shapes],
        scratch=[pltpu.VMEM((rows, width), f32)],
        name="finish",
        us=6,
    )


def rotary_tables(positions):
    half_rot = ROT // 2
    inverse = BASE ** (-(jnp.arange(half_rot, dtype=f32) * 2.0 / ROT))
    angles = positions.astype(f32).reshape(-1, 1) * inverse
    cos, sin = jnp.cos(angles), jnp.sin(angles)
    zero = jnp.zeros_like(sin)
    rest = jnp.zeros((cos.shape[0], 64 - ROT), f32)
    head = [
        jnp.concatenate([cos, cos, rest + 1.0], axis=-1),
        jnp.concatenate([-sin, zero, rest], axis=-1),
        jnp.concatenate([zero, sin, rest], axis=-1),
    ]
    return jnp.stack([jnp.concatenate([h, h], axis=-1) for h in head])


def local(
    hidden_in,
    positions,
    cotangent,
    norm_gains,
    norm_biases,
    w_qkv,
    b_qkv,
    w_q2,
    b_q2,
    w_out,
    w_up,
    b_up,
    w_down,
    out_bias,
):
    seqs, group, width = hidden_in.shape
    tokens = seqs * group
    hidden = w_up.shape[2]
    y, x, z, core = (lax.axis_index(a) for a in ("b0", "b1", Z, C))
    core_row = core.reshape(1).astype(jnp.int32)
    where = jnp.stack([y, x, z, core]).astype(jnp.int32)
    direct = square()
    x1 = hidden_in.reshape(tokens, width)
    g2 = cotangent.reshape(tokens, width)
    tab = rotary_tables(positions)

    na1, nm1, q1, kv_own = first_call(x1, norm_gains[0], norm_biases[0], w_qkv, b_qkv, tab, group)
    if direct:
        got = turns(lambda k: kv_own)
        y1, act1, slope1 = mlp_fwd_call(nm1, w_up, b_up, w_down, 0)
        mine = join([v[None] for v in (kv_own, *got)], (0,), where, (y1,))[0]
        theirs = swap(mine, C)
        kv = (mine, theirs)
        back = (z - jnp.arange(4)) % 4 * 2
        order = jnp.concatenate([back + core, back + 1 - core])
        do2 = back_call(g2, w_out, 1, (mine,))
    else:
        kv = (lax.all_gather(kv_own, (Z, C), axis=0, tiled=False),)
        order = jnp.arange(kv[0].shape[0])
        y1, act1, slope1 = mlp_fwd_call(nm1, w_up, b_up, w_down, 0)
        do2 = back_call(g2, w_out, 1)
    first = jnp.concatenate([((z * 2 + core) * group).reshape(1), order]).astype(jnp.int32)
    att1, lse1 = attend_call(first, q1, kv, (do2,))
    x2, na2, nm2, q2 = middle_call(
        att1, x1, y1, w_out, out_bias[0:1], norm_gains[1], norm_biases[1], w_q2, b_q2, tab
    )
    y2, dnm2, send, bup_send = mlp_back_call(core_row, nm2, g2, w_up, w_down, 1, b_up=b_up)
    got = swap(send.reshape(hidden, width), C)
    y2, dnm2, keep, bup_keep = mlp_back_call(
        core_row, nm2, g2, w_up, w_down, 1, b_up=b_up, before=(y2, dnm2)
    )
    keep = keep.reshape(hidden, width)

    def in_order(own, other):
        both = jnp.concatenate([own, other], axis=0)
        return jnp.where(core == 0, both, jnp.concatenate([other, own], axis=0)).reshape(-1, width)

    bup2 = in_order(bup_keep, bup_send)

    def swaps(one, two, axes):
        return swap(one, axes[0]), swap(two, axes[1])

    wait = ()
    if direct:
        one_send, one, two_send, two = sum_cores(keep, got, where)
        one_got, two_got = swaps(one_send, two_send, ("b1", "b0"))
        wait = (one,)
    else:
        mlp2 = add_low(keep, got)
    att2, lse2 = attend_call(first, q2, kv, wait)
    back2 = attend_back_call(first, q2, kv, att2, do2, lse2, tab, 0)
    if direct:
        one_send, one, two_send, two = sum_first(one, one_got, two, two_got, where, (back2[0],))
        one_got, two_got = swaps(one_send, two_send, ("b0", "b1"))
        wait = (one,)
    dq2, dkv2 = attend_back_call(first, q2, kv, att2, do2, lse2, tab, 1, before=back2, deps=wait)
    if direct:
        parts = sum_second(one, one_got, two, two_got, where, (dq2,))
        ahead = turns(lambda k: parts[k])
        wait = (parts[0],)
    hidden_out, early, g1, do1, small2 = turn_call(
        x2, y2, att2, att1, g2, na2, dq2, dnm2, w_out, w_q2, out_bias[1:2], norm_gains[1], deps=wait
    )
    dnm1, send, bup_send = mlp_back_call(
        core_row, nm1, g1, w_up, w_down, 0, kept=(act1, slope1)
    )
    got = swap(send.reshape(hidden, width), C)
    wait = ()
    if direct:
        mlp2 = sum_third([parts[0]] + ahead, where, (dnm1,))
        wait = (mlp2,)
        mlp2 = gather_blocks(mlp2)
    dnm1, keep, bup_keep = mlp_back_call(
        core_row, nm1, g1, w_up, w_down, 0, kept=(act1, slope1), before=(dnm1,), deps=wait
    )
    keep = keep.reshape(hidden, width)
    bup1 = in_order(bup_keep, bup_send)
    if direct:
        one_send, one, two_send, two = sum_cores(keep, got, where)
        one_got, two_got = swaps(one_send, two_send, ("b1", "b0"))
        wait = (one,)
    dq1, dkv1 = attend_back_call(
        first, q1, kv, att1, do1, lse1, tab, None, dkv2, deps=wait + (dnm1,)
    )
    if direct:
        one_send, one, two_send, two = sum_first(one, one_got, two, two_got, where, (dq1,))
        one_got, two_got = swaps(one_send, two_send, ("b0", "b1"))
    low = dkv1.astype(bf16)
    if direct:
        low = low.reshape(4, 2, group, -1)
        at = lambda c: lax.dynamic_index_in_dim(low, c, 1, keepdims=False)
        dkv_got = swap(at(1 - core), C)
        block = (1,) + low.shape[2:]
        dkv_parts = combine(
            [
                (
                    [
                        [
                            (
                                low.reshape((8,) + low.shape[2:]),
                                block,
                                lambda i, w, k=k: (lax.rem(w[2] + k, 4) * 2 + w[3], 0, 0),
                            ),
                            (dkv_got, block, lambda i, w, k=k: (lax.rem(w[2] + k, 4), 0, 0)),
                        ]
                    ],
                    block,
                    lambda i, w: (0, 0, 0),
                    block,
                )
                for k in range(4)
            ],
            where,
            (one,),
            name="sum_kv",
        )
        dkv_got = turns(lambda k: dkv_parts[k])
        dkv = sum_third([dkv_parts[0]] + dkv_got, where)[0]
        parts = sum_second(one, one_got, two, two_got, where, (dkv,))
        ahead = turns(lambda k: parts[k])
        wait = (parts[0],)
    else:
        dkv = lax.psum_scatter(low, (Z, C), scatter_dimension=0, tiled=True)
        mlp1 = add_low(keep, got)
        wait = ()
    grad_input, late_send, late = last_call(
        core_row, x1, g1, na1, dq1, dkv, dnm1, w_qkv, norm_gains[0], tab, small2, bup1, bup2, early, deps=wait
    )
    late_got = swap(late_send, C)

    if direct:
        both = sum_third([parts[0]] + ahead, where, (grad_input,), us=400)
        ahead = turns(lambda k: both)
        l1_send, l1, l2_send, l2 = sum_cores(late, late_got, where, (both,), us=1)
        l1_got, l2_got = swaps(l1_send, l2_send, ("b1", "b0"))
        l1_send, l1, l2_send, l2 = sum_first(l1, l1_got, l2, l2_got, where, us=1)
        l1_got, l2_got = swaps(l1_send, l2_send, ("b0", "b1"))
        one, two = join([both] + ahead, (0, 1), where, (l1,))
        one_got, two_got = swaps(one, two, ("b0", "b1"))
        parts = sum_second(l1, l1_got, l2, l2_got, where, (one,), us=1)
        late_ahead = turns(lambda k: parts[k])
        late = sum_third([parts[0]] + late_ahead, where, (mlp2,))
        outs = gather_blocks(late)
        one_near, two_near = (
            join([v[None], g[None]], (0,), where, (late,))[0].reshape(-1, width)
            for v, g in ((one, one_got), (two, two_got))
        )
        one_far, two_far = swaps(one_near, two_near, ("b1", "b0"))
        one_near_got, two_near_got = swap(one_near, C), swap(two_near, C)
        grad_down, grad_up = place_ordered(mlp2, 1, z_first=True, deps=(one_near, two_near))
        mark = lambda c, v, u: c * 4 + v * 2 + u
        down_map = lambda w: (0, w, 0)
        up_map = lambda w: (0, w % 2, w // 2)

        def down_marks(c, far):
            u = 1 - x if far else x
            return (mark(c, y, u), mark(c, 1 - y, u))

        def up_marks(c, far):
            v = 1 - y if far else y
            return (mark(c, v, x), mark(c, v, 1 - x))

        def put(down, up, one, two, far, cores):
            down = place_relative(
                [(o, down_marks(c, far)) for o, c in zip(one, cores)], down_map, down.shape, down
            )
            up = place_relative(
                [(t, up_marks(c, far)) for t, c in zip(two, cores)], up_map, up.shape, up
            )
            return down, up

        near_one, near_two = (one_near, one_near_got), (two_near, two_near_got)
        grad_down, grad_up = put(grad_down, grad_up, near_one, near_two, False, (core, 1 - core))
        one_far, two_far = relay((one_far, two_far), where, (grad_down, grad_up))
        one_far_got, two_far_got = swap(one_far, C), swap(two_far, C)
        grad_down, grad_up = put(grad_down, grad_up, (one_far,), (two_far,), True, (core,))
        grad_down, grad_up = put(
            grad_down, grad_up, (one_far_got,), (two_far_got,), True, (1 - core,)
        )
    else:
        mlp2 = gather_offloaded(reduce_offloaded(mlp2))
        placed = place_ordered(mlp2, 1)
        grad_down, grad_up = place_ordered(gather_offloaded(reduce_offloaded(mlp1)), 0, placed)
        outs = gather_offloaded(reduce_offloaded(add_low(late, late_got)))
        outs = outs.reshape(8, 2, 4, -1, width).transpose(0, 2, 1, 3, 4).reshape(32, 2, -1, width)
    grad_out, grad_q2, grad_qkv, small = finish_call(outs)
    one, two = small[0:8], small[8:16]
    ups = hidden // width
    grad_up_bias = jnp.stack([small[16 : 16 + ups].reshape(-1), small[16 + ups : 16 + 2 * ups].reshape(-1)])
    grad_gains = jnp.stack([one[0:2], two[0:2]])
    grad_biases = jnp.stack([one[2:4], two[2:4]])
    grad_qkv_bias = jnp.concatenate([one[4], one[5, :128]])
    grad_out_bias = jnp.stack([two[6], two[4]])
    return (
        hidden_out.reshape(seqs, group, width),
        grad_input.reshape(seqs, group, width),
        grad_gains,
        grad_biases,
        grad_qkv,
        grad_qkv_bias,
        grad_q2,
        two[5],
        grad_out,
        grad_up,
        grad_up_bias,
        grad_down,
        grad_out_bias,
    )


def solution(mesh):
    batch, seq = mesh.shape["batch"], mesh.shape["seq"]
    fine = jax.sharding.Mesh(
        mesh.devices.reshape(2, batch // 2, seq // 2, 2), ("b0", "b1", "z", "c")
    )
    rows = P(B, (Z, C), None)
    return jax.shard_map(
        local,
        mesh=fine,
        in_specs=(rows, P(B, (Z, C)), rows) + (P(),) * 11,
        out_specs=(rows, rows) + (P(),) * 11,
        check_vma=False,
    )
```

```python
from functools import partial

import jax
import jax.numpy as jnp
from jax import lax
from jax.experimental import pallas as pl
from jax.experimental.pallas import tpu as pltpu
from jax.sharding import PartitionSpec as P

ROT = 16
EPSILON = 1e-05
SCALE = 0.125
NEGATIVE = -1e30
BASE = 10000.0

B = ("b0", "b1")
Z = "z"
C = "c"
TILE = 768
QUARTER = TILE // 2
EXTRA = 256
KB = 256

f32 = jnp.float32
bf16 = jnp.bfloat16


def dot_nn(a, b):
    return lax.dot_general(a, b, (((1,), (0,)), ((), ())), preferred_element_type=f32)


def dot_nt(a, b):
    return lax.dot_general(a, b, (((1,), (1,)), ((), ())), preferred_element_type=f32)


def dot_tn(a, b):
    return lax.dot_general(a, b, (((0,), (0,)), ((), ())), preferred_element_type=f32)


def invoke(
    kernel, operands, deps, *, grid, in_specs, out_specs, out_shape, name, scalars=(), scratch=(), aliases={}, us=2, vmem=50
):
    ahead = len(scalars) + len(operands)

    def body(*refs):
        kernel(*refs[:ahead], *refs[ahead + len(deps) :])

    return pl.pallas_call(
        body,
        grid_spec=pltpu.PrefetchScalarGridSpec(
            num_scalar_prefetch=len(scalars),
            grid=grid,
            in_specs=list(in_specs) + [pl.BlockSpec(memory_space=pl.ANY)] * len(deps),
            out_specs=out_specs,
            scratch_shapes=scratch,
        ),
        out_shape=out_shape,
        input_output_aliases=aliases,
        compiler_params=pltpu.CompilerParams(vmem_limit_bytes=vmem << 20),
        cost_estimate=pl.CostEstimate(
            flops=us * 600_000_000, bytes_accessed=us * 1_000_000, transcendentals=0
        ),
        name=name,
    )(*scalars, *operands, *deps)


def layer_spec(shape, layer):
    return pl.BlockSpec((1,) + shape, lambda *i: (layer,) + (0,) * len(shape))


def full_spec(shape):
    return pl.BlockSpec(shape, lambda *i: (0,) * len(shape))


def unit_rows(values):
    center = values - jnp.mean(values, axis=-1, keepdims=True)
    spread = jnp.mean(center * center, axis=-1, keepdims=True)
    inverse = lax.rsqrt(spread + EPSILON)
    return center * inverse, inverse


def turn(values, cos_tab, sin_low, sin_high):
    return (
        values * cos_tab
        + pltpu.roll(values, 120, 1) * sin_low
        + pltpu.roll(values, 8, 1) * sin_high
    )


def pairs_down(values):
    return jnp.concatenate(
        [values[:, p * 128 : (p + 1) * 128] for p in range(values.shape[1] // 128)], axis=0
    )


def gelu_parts(lifted):
    cdf = 0.5 + 0.5 * lax.erf(lifted * 0.7071067811865476)
    slope = cdf + lifted * (0.3989422804014327 * jnp.exp(-0.5 * lifted * lifted))
    return lifted * cdf, slope


def first_kernel(x_ref, gain_ref, off_ref, w_ref, b_ref, tab_ref, na_ref, nm_ref, q_ref, kv_ref):
    tokens, width = x_ref.shape
    unit = unit_rows(x_ref[...].astype(f32))[0]
    norm_a = (unit * gain_ref[0:1] + off_ref[0:1]).astype(bf16)
    na_ref[...] = norm_a
    nm_ref[...] = (unit * gain_ref[1:2] + off_ref[1:2]).astype(bf16)
    cos_tab, sin_low, sin_high = tab_ref[0], tab_ref[1], tab_ref[2]
    kv = dot_nn(norm_a, w_ref[:, width:]) + b_ref[:, width:]
    low_half = lax.broadcasted_iota(jnp.int32, kv.shape, 1) < 64
    kv = jnp.where(low_half, turn(kv, cos_tab, sin_low, sin_high), kv).astype(bf16)
    group = kv_ref.shape[0]
    for s in range(tokens // group):
        kv_ref[:, s * 128 : (s + 1) * 128] = kv[s * group : (s + 1) * group]
    proj = dot_nn(norm_a, w_ref[:, :width]) + b_ref[:, :width]
    for p in range(width // 128):
        cols = slice(p * 128, (p + 1) * 128)
        q_ref[:, cols] = (turn(proj[:, cols], cos_tab, sin_low, sin_high) * SCALE).astype(bf16)


def first_call(x, gains, offs, w_qkv, b_qkv, tab, group):
    tokens, width = x.shape
    operands = (x, gains, offs, w_qkv, b_qkv.reshape(1, -1), tab)
    shapes = [(tokens, width)] * 3 + [(group, tokens // group * 128)]
    return invoke(
        first_kernel,
        operands,
        (),
        grid=(1,),
        in_specs=[full_spec(v.shape) for v in operands],
        out_specs=[full_spec(v) for v in shapes],
        out_shape=[jax.ShapeDtypeStruct(v, bf16) for v in shapes],
        name="first",
        us=3,
    )


def mlp_fwd_kernel(nm_ref, up_ref, bup_ref, down_ref, y_ref, act_ref, slope_ref):
    lifted = dot_nn(nm_ref[...], up_ref[0]) + bup_ref[...]
    active, slope = gelu_parts(lifted)
    active = active.astype(bf16)
    act_ref[...] = active
    slope_ref[...] = slope.astype(bf16)

    @pl.when(pl.program_id(0) == 0)
    def _():
        y_ref[...] = jnp.zeros_like(y_ref)

    y_ref[...] += dot_nn(active, down_ref[0])


def mlp_fwd_call(nm, w_up, b_up, w_down, layer):
    tokens, width = nm.shape
    hidden = w_up.shape[2]
    return invoke(
        mlp_fwd_kernel,
        (nm, w_up, b_up[layer : layer + 1], w_down),
        (),
        grid=(hidden // TILE,),
        in_specs=[
            full_spec((tokens, width)),
            pl.BlockSpec((1, width, TILE), lambda t: (layer, 0, t)),
            pl.BlockSpec((1, TILE), lambda t: (0, t)),
            pl.BlockSpec((1, TILE, width), lambda t: (layer, t, 0)),
        ],
        out_specs=[
            full_spec((tokens, width)),
            pl.BlockSpec((tokens, TILE), lambda t: (0, t)),
            pl.BlockSpec((tokens, TILE), lambda t: (0, t)),
        ],
        out_shape=[
            jax.ShapeDtypeStruct((tokens, width), f32),
            jax.ShapeDtypeStruct((tokens, hidden), bf16),
            jax.ShapeDtypeStruct((tokens, hidden), bf16),
        ],
        name="mlp_fwd",
        us=10,
    )


def mlp_grads(active, slope, nm, nm_turned, grad, up, down, start, refs):
    grad_norm_ref, rows_ref, bias_ref = refs
    grad_lifted = (dot_nt(grad, down) * slope).astype(bf16)
    bias_ref[...] = jnp.sum(grad_lifted.astype(f32), axis=0, keepdims=True)

    @pl.when(pl.program_id(0) == 0)
    def _():
        grad_norm_ref[...] = jnp.zeros_like(grad_norm_ref) if start is None else start[...]
        nm_turned[...] = nm.T

    grad_norm_ref[...] += dot_nt(grad_lifted, up)
    grad_down = dot_tn(active, grad).astype(bf16)
    grad_up = dot_nn(nm_turned[...], grad_lifted).astype(bf16)
    for j in range(2):
        rows = slice(j * QUARTER, (j + 1) * QUARTER)
        rows_ref[0, 2 * j * QUARTER : (2 * j + 1) * QUARTER] = grad_down[rows]
        rows_ref[0, (2 * j + 1) * QUARTER : (2 * j + 2) * QUARTER] = grad_up[rows]


def mlp_both_kernel(more, core_ref, nm_ref, g_ref, up_ref, bup_ref, down_ref, *refs):
    y_start, grad_start = refs[:2] if more else (None, None)
    y_ref, *outs, nm_turned = refs[2:] if more else refs
    nm, up, down = nm_ref[...], up_ref[0], down_ref[0]
    active, slope = gelu_parts(dot_nn(nm, up) + bup_ref[...])
    active = active.astype(bf16)

    @pl.when(pl.program_id(0) == 0)
    def _():
        y_ref[...] = y_start[...] if more else jnp.zeros_like(y_ref)

    y_ref[...] += dot_nn(active, down)
    mlp_grads(active, slope, nm, nm_turned, g_ref[...], up, down, grad_start, outs)


def mlp_back_kernel(more, core_ref, nm_ref, g_ref, up_ref, down_ref, act_ref, slope_ref, *refs):
    grad_start = refs[0] if more else None
    *outs, nm_turned = refs[1:] if more else refs
    slope = slope_ref[...].astype(f32)
    mlp_grads(
        act_ref[...], slope, nm_ref[...], nm_turned, g_ref[...], up_ref[0], down_ref[0], grad_start, outs
    )


def mlp_back_call(core, nm, grad, w_up, w_down, layer, b_up=None, kept=None, before=None, deps=()):
    tokens, width = nm.shape
    hidden = w_up.shape[2]
    half = hidden // TILE // 2
    other = before is None

    def tile(t, core_ref):
        c = core_ref[0]
        return (1 - c if other else c) * half + t

    whole = full_spec((tokens, width))
    whole_shape = jax.ShapeDtypeStruct((tokens, width), f32)
    up_spec = pl.BlockSpec((1, width, TILE), lambda t, c: (layer, 0, tile(t, c)))
    down_spec = pl.BlockSpec((1, TILE, width), lambda t, c: (layer, tile(t, c), 0))
    cols_spec = pl.BlockSpec((tokens, TILE), lambda t, c: (0, tile(t, c)))
    both = kept is None
    if both:
        bias_spec = pl.BlockSpec((1, TILE), lambda t, c: (0, tile(t, c)))
        in_specs = [whole, whole, up_spec, bias_spec, down_spec]
        operands = (nm, grad, w_up, b_up[layer : layer + 1], w_down)
    else:
        in_specs = [whole, whole, up_spec, down_spec, cols_spec, cols_spec]
        operands = (nm, grad, w_up, w_down) + kept
    before = tuple(before or ())
    count = 2 if both else 1
    return invoke(
        partial(mlp_both_kernel if both else mlp_back_kernel, not other),
        operands + before,
        deps,
        scalars=(core,),
        grid=(half,),
        in_specs=in_specs + [whole] * len(before),
        out_specs=[whole] * count
        + [
            pl.BlockSpec((1, 2 * TILE, width), lambda t, c: (t, 0, 0)),
            pl.BlockSpec((1, TILE), lambda t, c: (0, t)),
        ],
        out_shape=[whole_shape] * count
        + [
            jax.ShapeDtypeStruct((half, 2 * TILE, width), bf16),
            jax.ShapeDtypeStruct((1, hidden // 2), f32),
        ],
        scratch=[pltpu.VMEM((width, tokens), bf16)],
        name="mlp_both" if both else "mlp_back",
        us=40 if both else (12 if other else 150),
    )


def spread_kv(pieces, order_ref, k0, k1, turned, forward):
    at = 0
    for ref in pieces:
        for p in range(ref.shape[0]):
            kv = ref[p].astype(f32)
            rows = kv.shape[0]
            swapped = pltpu.roll(kv, 64, 1)
            low_half = lax.broadcasted_iota(jnp.int32, kv.shape, 1) < 64
            zero = jnp.zeros_like(kv)
            block = order_ref[1 + at]
            place = pl.ds(pl.multiple_of(block * rows, rows), rows)
            k0[place] = jnp.where(low_half, kv, zero).astype(bf16)
            k1[place] = jnp.where(low_half, zero, swapped).astype(bf16)
            if forward:
                t0, t1 = turned
                rest = jnp.ones((64, rows), f32)
                part = kv.T[64:]
            else:
                v0, v1, t0, t1 = turned
                v0[place] = jnp.where(low_half, swapped, zero).astype(bf16)
                v1[place] = jnp.where(low_half, zero, kv).astype(bf16)
                rest = jnp.zeros((64, rows), f32)
                part = kv.T[:64]
            t0[block] = jnp.concatenate([part, rest], axis=0).astype(bf16)
            t1[block] = jnp.concatenate([rest, part], axis=0).astype(bf16)
            at += 1


def block_rows(index):
    return pl.ds(pl.multiple_of(index * KB, KB), KB)


def turned_block(ref, index):
    return jnp.concatenate([ref[2 * index], ref[2 * index + 1]], axis=1)


def visible(shape, first, start, group):
    key = lax.broadcasted_iota(jnp.int32, shape, 0)
    token = lax.broadcasted_iota(jnp.int32, shape, 1) % group
    return key - token <= first - start


def attend_kernel(count, first_ref, q_ref, *refs):
    pieces, (o_ref, lse_ref, k0, k1, t0, t1) = refs[:count], refs[count:]
    first = first_ref[0]
    group, width = q_ref.shape
    spread_kv(pieces, first_ref, k0, k1, (t0, t1), True)
    q6 = pairs_down(q_ref[...])
    full = first // KB

    def block(kb, carry):
        done = []
        for keys, vals, (top, summed) in zip((k0, k1), (t0, t1), carry or (2 * ((None, None),))):
            scores = dot_nt(keys[block_rows(kb), :], q6)
            if carry is None:
                scores = jnp.where(
                    visible(scores.shape, first, full * KB, group), scores, NEGATIVE
                )
            new_top = jnp.max(scores, axis=0, keepdims=True)
            if carry is not None:
                new_top = jnp.maximum(top, new_top)
            weights = jnp.exp(scores - new_top).astype(bf16)
            part = dot_nn(turned_block(vals, kb), weights)
            if carry is not None:
                part = part + summed * jnp.exp(top - new_top)
            done.append((new_top, part))
        return tuple(done)

    (top0, sum0), (top1, sum1) = lax.fori_loop(0, full, block, block(full, None))
    total0, total1 = sum0[64:65], sum1[0:1]
    both = jnp.concatenate([sum0[:64] / total0, sum1[64:] / total1], axis=0).T.astype(bf16)
    for p in range(width // 128):
        o_ref[:, p * 128 : (p + 1) * 128] = both[p * group : (p + 1) * group]
    shape = lse_ref.shape[2:]
    lse_ref[0, 0] = jnp.broadcast_to(top0 + jnp.log(total0), shape)
    lse_ref[0, 1] = jnp.broadcast_to(top1 + jnp.log(total1), shape)


def piece_specs(kv):
    return [pl.BlockSpec(v.shape[:2] + (128,), lambda s, f: (0, 0, s)) for v in kv]


def attend_call(first, q, kv, deps=()):
    tokens, width = q.shape
    length = sum(v.shape[0] for v in kv) * kv[0].shape[1]
    seqs = kv[0].shape[2] // 128
    group = tokens // seqs
    rows = group * width // 128
    return invoke(
        partial(attend_kernel, len(kv)),
        (q,) + kv,
        deps,
        scalars=(first,),
        grid=(seqs,),
        in_specs=[pl.BlockSpec((group, width), lambda s, f: (s, 0))] + piece_specs(kv),
        out_specs=[
            pl.BlockSpec((group, width), lambda s, f: (s, 0)),
            pl.BlockSpec((1, 2, 8, rows), lambda s, f: (s, 0, 0, 0)),
        ],
        scratch=[pltpu.VMEM((length, 128), bf16)] * 2
        + [pltpu.VMEM((length // 128, 128, 128), bf16)] * 2,
        out_shape=[
            jax.ShapeDtypeStruct((tokens, width), bf16),
            jax.ShapeDtypeStruct((seqs, 2, 8, rows), f32),
        ],
        name="attend",
        us=60,
    )


def attend_back_kernel(count, has_start, unread, first_ref, q_ref, *refs):
    pieces, refs = refs[:count], refs[count:]
    ins = 5 if has_start else 4
    refs = refs[:ins] + refs[ins + unread :]
    if has_start:
        o_ref, do_ref, lse_ref, tab_ref, start_ref, dq_out, dkv_ref, k0, k1, v0, v1, t0, t1, dq_ref = refs
        dkv_ref[...] = start_ref[...]
    else:
        o_ref, do_ref, lse_ref, tab_ref, dq_out, dkv_ref, k0, k1, v0, v1, t0, t1, dq_ref = refs
        dkv_ref[...] = jnp.zeros_like(dkv_ref)
    first = first_ref[0]
    group = q_ref.shape[0]
    spread_kv(pieces, first_ref, k0, k1, (v0, v1, t0, t1), False)
    q6 = pairs_down(q_ref[...])
    do6 = pairs_down(do_ref[...])
    deltas = (do6.astype(f32) * pairs_down(o_ref[...]).astype(f32)).T
    halves = (
        (k0, v0, lse_ref[0, 0, 0:1], jnp.sum(deltas[:64], axis=0, keepdims=True)),
        (k1, v1, lse_ref[0, 1, 0:1], jnp.sum(deltas[64:], axis=0, keepdims=True)),
    )
    dq_ref[...] = jnp.zeros_like(dq_ref)
    full = first // KB
    low_half = lax.broadcasted_iota(jnp.int32, (KB, 128), 1) < 64

    def block(kb, masked):
        rows = block_rows(kb)
        grads, keys, vals = [], [], []
        for k, v, lse, delta in halves:
            probs = jnp.exp(dot_nt(k[rows, :], q6) - lse)
            if masked:
                probs = jnp.where(visible(probs.shape, first, full * KB, group), probs, 0.0)
            grad_probs = dot_nt(v[rows, :], do6)
            grad_scores = (probs * (grad_probs - delta)).astype(bf16)
            grads.append(grad_scores)
            keys.append(dot_nn(grad_scores, q6))
            vals.append(dot_nn(probs.astype(bf16), do6))
        dkv_ref[rows, :] += jnp.where(low_half, keys[0], vals[1]) + pltpu.roll(
            jnp.where(low_half, vals[0], keys[1]), 64, 1
        )
        turned = jnp.concatenate([turned_block(t0, kb), turned_block(t1, kb)], axis=1)
        dq_ref[...] += dot_nn(turned, jnp.concatenate(grads, axis=0))

    block(full, True)

    def step(kb, carry):
        block(kb, False)
        return carry

    lax.fori_loop(0, full, step, 0)
    cos_tab, sin_low, sin_high = tab_ref[0], -tab_ref[1], -tab_ref[2]
    dq = dq_ref[...].T * SCALE
    for p in range(q_ref.shape[1] // 128):
        part = dq[p * group : (p + 1) * group]
        dq_out[:, p * 128 : (p + 1) * 128] = turn(part, cos_tab, sin_low, sin_high).astype(bf16)


def attend_back_call(first, q, kv, attended, grad, lse, tab, part, start=None, before=(), deps=()):
    tokens, width = q.shape
    length = sum(v.shape[0] for v in kv) * kv[0].shape[1]
    seqs = kv[0].shape[2] // 128
    group = tokens // seqs
    rows = group * width // 128
    count = seqs if part is None else seqs // 2
    at = (part or 0) * count
    tok_spec = pl.BlockSpec((group, width), lambda s, f: (at + s, 0))
    len_spec = pl.BlockSpec((length, 128), lambda s, f: (0, at + s))
    in_specs = [
        tok_spec,
        *[pl.BlockSpec(v.shape[:2] + (128,), lambda s, f: (0, 0, at + s)) for v in kv],
        tok_spec,
        tok_spec,
        pl.BlockSpec((1, 2, 8, rows), lambda s, f: (at + s, 0, 0, 0)),
        pl.BlockSpec((3, group, 128), lambda s, f: (0, at + s, 0)),
    ]
    operands = [q, *kv, attended, grad, lse, tab]
    if start is not None:
        in_specs.append(len_spec)
        operands.append(start)
    return invoke(
        partial(attend_back_kernel, len(kv), start is not None, len(before)),
        operands + list(before),
        deps,
        scalars=(first,),
        grid=(count,),
        in_specs=in_specs + [pl.BlockSpec(memory_space=pl.ANY)] * len(before),
        out_specs=[tok_spec, len_spec],
        scratch=[pltpu.VMEM((length, 128), bf16)] * 4
        + [pltpu.VMEM((length // 128, 128, 128), bf16)] * 2
        + [pltpu.VMEM((128, rows), f32)],
        out_shape=[
            jax.ShapeDtypeStruct((tokens, width), bf16),
            jax.ShapeDtypeStruct((length, seqs * 128), f32),
        ],
        aliases={1 + len(operands) + i: i for i in range(len(before))},
        name="attend_back",
        us=45,
    )


def back_kernel(g_ref, w_ref, out_ref):
    out_ref[...] = dot_nt(g_ref[...], w_ref[0]).astype(bf16)


def back_call(grad, w_out, layer, deps=()):
    tokens, width = grad.shape
    return invoke(
        back_kernel,
        (grad, w_out),
        deps,
        grid=(1,),
        in_specs=[full_spec((tokens, width)), layer_spec((width, width), layer)],
        out_specs=full_spec((tokens, width)),
        out_shape=jax.ShapeDtypeStruct((tokens, width), bf16),
        name="back",
    )


def middle_kernel(
    att_ref, x_ref, y_ref, wo_ref, bias_ref, gain_ref, off_ref, wq_ref, bq_ref, tab_ref,
    x2_ref, na_ref, nm_ref, q_ref,
):
    second = (
        x_ref[...].astype(f32) + dot_nn(att_ref[...], wo_ref[0]) + y_ref[...] + bias_ref[...]
    ).astype(bf16)
    x2_ref[...] = second
    unit = unit_rows(second.astype(f32))[0]
    norm_a = (unit * gain_ref[0:1] + off_ref[0:1]).astype(bf16)
    na_ref[...] = norm_a
    nm_ref[...] = (unit * gain_ref[1:2] + off_ref[1:2]).astype(bf16)
    proj = dot_nn(norm_a, wq_ref[...]) + bq_ref[...]
    cos_tab, sin_low, sin_high = tab_ref[0], tab_ref[1], tab_ref[2]
    for p in range(proj.shape[1] // 128):
        cols = slice(p * 128, (p + 1) * 128)
        q_ref[:, cols] = (turn(proj[:, cols], cos_tab, sin_low, sin_high) * SCALE).astype(bf16)


def middle_call(att, x, y, w_out, bias, gains, offs, w_q2, b_q2, tab):
    tokens, width = x.shape
    operands = (att, x, y, w_out, bias, gains, offs, w_q2, b_q2.reshape(1, -1), tab)
    specs = [full_spec(v.shape) for v in operands]
    specs[3] = layer_spec((width, width), 0)
    return invoke(
        middle_kernel,
        operands,
        (),
        grid=(1,),
        in_specs=specs,
        out_specs=[full_spec((tokens, width))] * 4,
        out_shape=[jax.ShapeDtypeStruct((tokens, width), bf16)] * 4,
        name="middle",
        us=5,
    )


def norm_back(values, grad_a, grad_m, gain_ref, small_ref, row):
    unit, inverse = unit_rows(values)
    small_ref[row : row + 1] = jnp.sum(grad_a * unit, axis=0, keepdims=True)
    small_ref[row + 1 : row + 2] = jnp.sum(grad_m * unit, axis=0, keepdims=True)
    small_ref[row + 2 : row + 3] = jnp.sum(grad_a, axis=0, keepdims=True)
    small_ref[row + 3 : row + 4] = jnp.sum(grad_m, axis=0, keepdims=True)
    grad_unit = grad_a * gain_ref[0:1] + grad_m * gain_ref[1:2]
    return inverse * (
        grad_unit
        - jnp.mean(grad_unit, axis=-1, keepdims=True)
        - unit * jnp.mean(grad_unit * unit, axis=-1, keepdims=True)
    )


def by_core(core, send_ref, keep_ref, put):
    @pl.when(core == 0)
    def _():
        put(keep_ref, send_ref)

    @pl.when(core != 0)
    def _():
        put(send_ref, keep_ref)


def turn_kernel(
    x2_ref, y_ref, att2_ref, att1_ref, g_ref, na_ref, dq_ref, dnm_ref, wo1_ref, wo2_ref, wq_ref, bias_ref, gain_ref,
    hidden_ref, grads_ref, g1_ref, do1_ref, small_ref,
):
    width = x2_ref.shape[1]
    second = x2_ref[...].astype(f32)
    att2, grad, dq = att2_ref[...], g_ref[...], dq_ref[...]
    wide = grad.astype(f32)
    small_ref[...] = jnp.zeros_like(small_ref)
    grad_a = dot_nt(dq, wq_ref[...])
    g1 = (norm_back(second, grad_a, dnm_ref[...], gain_ref, small_ref, 0) + wide).astype(bf16)
    g1_ref[...] = g1
    do1_ref[...] = dot_nt(g1, wo1_ref[0]).astype(bf16)
    small_ref[4:5] = jnp.sum(wide, axis=0, keepdims=True)
    small_ref[5:6] = jnp.sum(dq.astype(f32), axis=0, keepdims=True)
    small_ref[6:7] = jnp.sum(g1.astype(f32), axis=0, keepdims=True)
    grads_ref[0:width] = dot_tn(att2, grad).astype(bf16)
    grads_ref[width : 2 * width] = dot_tn(na_ref[...], dq).astype(bf16)
    grads_ref[2 * width : 3 * width] = dot_tn(att1_ref[...], g1).astype(bf16)
    hidden_ref[...] = (second + dot_nn(att2, wo2_ref[0]) + y_ref[...] + bias_ref[...]).astype(bf16)


def turn_call(x2, y2, att2, att1, g, na2, dq2, dnm2, w_out, w_q2, bias, gains, deps=()):
    tokens, width = x2.shape
    operands = (x2, y2, att2, att1, g, na2, dq2, dnm2, w_out, w_out, w_q2, bias, gains)
    specs = [full_spec(v.shape) for v in operands]
    specs[8] = layer_spec((width, width), 0)
    specs[9] = layer_spec((width, width), 1)
    tok = full_spec((tokens, width))
    tok_shape = jax.ShapeDtypeStruct((tokens, width), bf16)
    return invoke(
        turn_kernel,
        operands,
        deps,
        grid=(1,),
        in_specs=specs,
        out_specs=[tok, full_spec((3 * width, width)), tok, tok, full_spec((8, width))],
        out_shape=[
            tok_shape,
            jax.ShapeDtypeStruct((3 * width, width), bf16),
            tok_shape,
            tok_shape,
            jax.ShapeDtypeStruct((8, width), f32),
        ],
        name="turn",
        us=60,
    )


def last_kernel(
    core_ref, x_ref, g1_ref, na_ref, dq_ref, dkv_ref, dnm_ref, w_ref, gain_ref, tab_ref, small2_ref, bup1_ref, bup2_ref,
    early_ref, grad_ref, send_ref, keep_ref, small_ref,
):
    tokens, width = x_ref.shape
    group = dkv_ref.shape[0]
    dkv = jnp.concatenate(
        [dkv_ref[:, s * 128 : (s + 1) * 128] for s in range(tokens // group)], axis=0
    ).astype(f32)
    low_half = lax.broadcasted_iota(jnp.int32, dkv.shape, 1) < 64
    dkv = jnp.where(low_half, turn(dkv, tab_ref[0], -tab_ref[1], -tab_ref[2]), dkv).astype(bf16)
    dq, norm_a = dq_ref[...], na_ref[...]
    small_ref[...] = jnp.zeros_like(small_ref)
    small_ref[4:5] = jnp.sum(dq.astype(f32), axis=0, keepdims=True)
    small_ref[5:6, 0:128] = jnp.sum(dkv.astype(f32), axis=0, keepdims=True)
    grad_a = dot_nt(dq, w_ref[:, :width]) + dot_nt(dkv, w_ref[:, width:])
    grad_ref[...] = g1_ref[...].astype(f32) + norm_back(
        x_ref[...].astype(f32), grad_a, dnm_ref[...], gain_ref, small_ref, 0
    )
    q1 = dot_tn(norm_a, dq).astype(bf16)
    kv = dot_tn(dkv, norm_a).astype(bf16)
    smalls = [small_ref[...], small2_ref[...], bup1_ref[...], bup2_ref[...]]
    smalls.append(jnp.zeros((EXTRA - 128 - sum(v.shape[0] for v in smalls), width), f32))
    smalls = jnp.concatenate(smalls, axis=0).astype(bf16)

    def put(one, two):
        one[: 2 * width] = early_ref[: 2 * width]
        one[2 * width : 2 * width + 128] = kv
        one[2 * width + 128 :] = smalls
        two[:width] = early_ref[2 * width :]
        two[width : 2 * width] = q1
        two[2 * width :] = jnp.zeros((EXTRA, width), bf16)

    by_core(core_ref[0], send_ref, keep_ref, put)


def last_call(core, x, g1, na1, dq1, dkv, dnm1, w_qkv, gains, tab, small2, bup1, bup2, early, deps=()):
    tokens, width = x.shape
    operands = (x, g1, na1, dq1, dkv, dnm1, w_qkv, gains, tab, small2, bup1, bup2, early)
    out_shape = [
        jax.ShapeDtypeStruct((tokens, width), f32),
        jax.ShapeDtypeStruct((2 * width + EXTRA, width), bf16),
        jax.ShapeDtypeStruct((2 * width + EXTRA, width), bf16),
    ]
    return invoke(
        last_kernel,
        operands,
        deps,
        scalars=(core,),
        grid=(1,),
        in_specs=[full_spec(v.shape) for v in operands],
        out_specs=[full_spec(v.shape) for v in out_shape],
        out_shape=out_shape,
        scratch=[pltpu.VMEM((8, width), f32)],
        name="last",
        us=10,
    )


PAIR = [(0, 1), (1, 0)]


def swap(values, axis):
    return lax.ppermute(values, axis, PAIR)


def add_low(first, *rest):
    total = first.astype(f32)
    for value in rest:
        total = total + value.astype(f32)
    return total.astype(bf16)


def pick(values, index):
    return lax.dynamic_index_in_dim(values, index, 0, keepdims=False)


def square():
    return lax.axis_size("b0") == 2 and lax.axis_size("b1") == 2 and lax.axis_size(Z) == 4


def turns(values_at):
    size = lax.axis_size(Z)
    return [
        lax.ppermute(values_at(k), Z, [(i, (i + k) % size) for i in range(size)])
        for k in range(1, size)
    ]


def reduce_offloaded(part):
    part = lax.psum_scatter(part, B, scatter_dimension=0, tiled=True)
    return lax.psum_scatter(part, Z, scatter_dimension=0, tiled=True)


def gather_offloaded(part):
    return lax.all_gather(part, (C,) + B + (Z,), axis=0, tiled=True)


def combine(groups, where, deps, grid=(1,), name="combine", us=2, vmem=50):
    terms = [t for sums, *_ in groups for parts in sums for t in parts]

    def kernel(where_ref, *refs):
        ins, outs = iter(refs[: len(terms)]), refs[len(terms) :]
        for (sums, *_), out_ref in zip(groups, outs):
            for i, parts in enumerate(sums):
                total = next(ins)[...].astype(f32)
                for _ in parts[1:]:
                    total = total + next(ins)[...].astype(f32)
                if len(sums) == 1:
                    out_ref[...] = total.reshape(out_ref.shape).astype(bf16)
                else:
                    out_ref[i] = total.reshape(out_ref.shape[1:]).astype(bf16)

    return invoke(
        kernel,
        [t[0] for t in terms],
        deps,
        scalars=(where,),
        grid=grid,
        in_specs=[pl.BlockSpec(t[1], t[2]) for t in terms],
        out_specs=[pl.BlockSpec(g[1], g[2]) for g in groups],
        out_shape=[jax.ShapeDtypeStruct(g[3], bf16) for g in groups],
        name=name,
        us=us,
        vmem=vmem,
    )


def sum_cores(keep, got, where, deps=(), us=20):
    width = keep.shape[-1]
    keep, got = (v.reshape(2, 2, 2, -1, width) for v in (keep, got))
    quarter = keep.shape[3]
    half = quarter // 2
    maps = (
        lambda i, j, w: (i, 1 - w[1], 0, j, 0),
        lambda i, j, w: (i, w[1], 0, j, 0),
        lambda i, j, w: (1 - w[0], i, 1, j, 0),
        lambda i, j, w: (w[0], i, 1, j, 0),
    )
    block = (1, 1, 1, half, width)
    groups = [
        (
            [[(keep, block, m), (got, block, m)]],
            (1, half, width),
            lambda i, j, w: (i, j, 0),
            (2, quarter, width),
        )
        for m in maps
    ]
    return combine(groups, where, deps, grid=(2, 2), name="sum_cores", us=us)


def sum_first(one, one_got, two, two_got, where, deps=(), us=30):
    _, quarter, width = one.shape
    half = quarter // 2
    groups = []
    for values, got, m in (
        (one, one_got, lambda j, w: (1 - w[0], j, 0)),
        (one, one_got, lambda j, w: (w[0], j, 0)),
        (two, two_got, lambda j, w: (1 - w[1], j, 0)),
        (two, two_got, lambda j, w: (w[1], j, 0)),
    ):
        block = (1, half, width)
        groups.append(
            ([[(values, block, m), (got, block, m)]], block, lambda j, w: (0, j, 0), (1, quarter, width))
        )
    return combine(groups, where, deps, grid=(2,), name="sum_first", us=us)


def sum_second(one, one_got, two, two_got, where, deps=(), us=100):
    width = one.shape[-1]
    one, one_got, two, two_got = (v.reshape(4, -1, width) for v in (one, one_got, two, two_got))
    block = (1,) + one.shape[1:]
    groups = []
    for k in range(4):
        m = lambda i, w, k=k: (lax.rem(w[2] + k, 4), 0, 0)
        groups.append(
            (
                [[(a, block, m), (b, block, m)] for a, b in ((one, one_got), (two, two_got))],
                (2,) + one.shape[1:],
                lambda i, w: (0, 0, 0),
                (2,) + one.shape[1:],
            )
        )
    return combine(groups, where, deps, name="sum_second", us=us)


def sum_third(parts, where, deps=(), us=10):
    shape = parts[0].shape
    m = lambda i, w: (0, 0, 0)
    return combine([([[(p, shape, m) for p in parts]], shape, m, shape)], where, deps, name="sum_third", us=us)[0]


def join(parts, leads, where, deps=()):
    shape = parts[0].shape[1:]
    groups = [
        (
            [[(p, (1,) + shape, lambda i, w, a=a: (a,) + (0,) * len(shape))] for p in parts],
            (len(parts),) + shape,
            lambda i, w: (0,) * (len(shape) + 1),
            (len(parts),) + shape,
        )
        for a in leads
    ]
    return combine(groups, where, deps, name="join")


def gather_blocks(both):
    return lax.all_gather(both, (C,) + B + (Z,), axis=0, tiled=False)


def relay(values, where, deps):
    block = (values[0].shape[0] // 2, values[0].shape[1])
    m = lambda i, w: (i, 0)
    groups = [([[(v, block, m)]], block, m, v.shape) for v in values]
    return combine(groups, where, deps, grid=(2,), name="relay")


def place_kernel(count, quarter, where_ref, *refs):
    ins, out_ref = refs[:count], refs[-1]
    step = pl.program_id(0)
    z = where_ref[2 * count]
    unit = quarter // 4
    for a in range(count):

        @pl.when(step // 2 == a)
        def _():
            for k in range(4):
                rows = pl.ds(pl.multiple_of(lax.rem(z - k + 4, 4) * unit, 16), unit)
                out_ref[0, rows] = ins[a][k * unit : (k + 1) * unit].astype(f32)


def place_relative(parts, out_map, out_shape, before, deps=()):
    values = [v for v, _ in parts]
    count, width = len(parts), values[0].shape[1]
    quarter = values[0].shape[0] // 2
    where = jnp.stack([m for _, marks in parts for m in marks] + [lax.axis_index(Z)])
    return invoke(
        partial(place_kernel, count, quarter),
        values + [before],
        deps,
        scalars=(where.astype(jnp.int32),),
        grid=(2 * count,),
        in_specs=[
            pl.BlockSpec((quarter, width), lambda i, w, a=a: (jnp.clip(i - 2 * a, 0, 1), 0))
            for a in range(count)
        ]
        + [pl.BlockSpec(memory_space=pl.ANY)],
        out_specs=pl.BlockSpec((1, quarter, width), lambda i, w: out_map(w[i])),
        out_shape=jax.ShapeDtypeStruct(out_shape, f32),
        aliases={1 + count: 0},
        name="place",
        us=2,
    )


def spread_kernel(z_first, in_ref, *refs):
    down_ref, up_ref = refs[-2:]
    unit = QUARTER // 4
    for z in range(4):
        rows = slice(z * unit, (z + 1) * unit)
        down_ref[0, rows] = (in_ref[0, z, 0] if z_first else in_ref[0, 0, z]).astype(f32)
        up_ref[0, rows] = (in_ref[0, z, 1] if z_first else in_ref[0, 1, z]).astype(f32)


def spread_turned_kernel(where_ref, in_ref, down_ref, up_ref):
    unit = QUARTER // 4
    for k in range(4):
        rows = pl.ds(pl.multiple_of(lax.rem(where_ref[2] - k + 4, 4) * unit, 16), unit)
        down_ref[0, rows] = in_ref[0, k, 0].astype(f32)
        up_ref[0, rows] = in_ref[0, k, 1].astype(f32)


def place_gathered(blocks, layer, where, deps=()):
    unit, width = blocks.shape[-2:]
    hidden = blocks.size // width // 2
    return invoke(
        spread_turned_kernel,
        (blocks,),
        deps,
        scalars=(where,),
        grid=(8,),
        in_specs=[
            pl.BlockSpec((1, 4, 2, unit, width), lambda i, w: (i % 4 * 2 + i // 4, 0, 0, 0, 0))
        ],
        out_specs=[
            pl.BlockSpec((1, QUARTER, width), lambda i, w: (layer, i, 0)),
            pl.BlockSpec((1, QUARTER, TILE), lambda i, w: (layer, i % 2, i // 2)),
        ],
        out_shape=[
            jax.ShapeDtypeStruct((2, hidden, width), f32),
            jax.ShapeDtypeStruct((2, width, hidden), f32),
        ],
        name="spread",
        us=2,
    )


def place_ordered(rows, layer, before=None, z_first=False, deps=()):
    width = rows.shape[-1]
    hidden = rows.size // width // 2
    inner = (4, 2) if z_first else (2, 4)
    rows = rows.reshape((hidden // QUARTER,) + inner + (QUARTER // 4, width))
    return invoke(
        partial(spread_kernel, z_first),
        [rows] + list(before or ()),
        deps,
        grid=(hidden // QUARTER,),
        in_specs=[pl.BlockSpec((1,) + rows.shape[1:], lambda i: (i, 0, 0, 0, 0))]
        + [pl.BlockSpec(memory_space=pl.ANY)] * len(before or ()),
        out_specs=[
            pl.BlockSpec((1, QUARTER, width), lambda i: (layer, i, 0)),
            pl.BlockSpec((1, QUARTER, TILE), lambda i: (layer, i % 2, i // 2)),
        ],
        out_shape=[
            jax.ShapeDtypeStruct((2, hidden, width), f32),
            jax.ShapeDtypeStruct((2, width, hidden), f32),
        ],
        aliases={1: 0, 2: 1} if before else {},
        name="spread",
        us=2,
    )


def finish_kernel(in_ref, out_ref, q2_ref, qkv_ref, small_ref, flat):
    width = out_ref.shape[2]
    size = in_ref.shape[2]
    for w in range(8):
        for two in range(2):
            for z in range(4):
                at = ((w * 2 + two) * 4 + z) * size
                flat[at : at + size] = in_ref[w * 4 + z, two].astype(f32)
    half = flat.shape[0] // 2
    out_ref[1] = flat[:width]
    q2_ref[...] = flat[width : 2 * width]
    out_ref[0] = flat[half : half + width]
    qkv_ref[:, :width] = flat[half + width : half + 2 * width]
    qkv_ref[:, width:] = flat[2 * width : 2 * width + 128].T
    small_ref[...] = flat[2 * width + 128 : half]


def finish_call(blocks):
    width = blocks.shape[-1]
    rows = blocks.size // width
    shapes = [(2, width, width), (width, width), (width, width + 128), (EXTRA - 128, width)]
    return invoke(
        finish_kernel,
        (blocks,),
        (),
        grid=(1,),
        in_specs=[full_spec(blocks.shape)],
        out_specs=[full_spec(v) for v in shapes],
        out_shape=[jax.ShapeDtypeStruct(v, f32) for v in shapes],
        scratch=[pltpu.VMEM((rows, width), f32)],
        name="finish",
        us=6,
    )


def rotary_tables(positions):
    half_rot = ROT // 2
    inverse = BASE ** (-(jnp.arange(half_rot, dtype=f32) * 2.0 / ROT))
    angles = positions.astype(f32).reshape(-1, 1) * inverse
    cos, sin = jnp.cos(angles), jnp.sin(angles)
    zero = jnp.zeros_like(sin)
    rest = jnp.zeros((cos.shape[0], 64 - ROT), f32)
    head = [
        jnp.concatenate([cos, cos, rest + 1.0], axis=-1),
        jnp.concatenate([-sin, zero, rest], axis=-1),
        jnp.concatenate([zero, sin, rest], axis=-1),
    ]
    return jnp.stack([jnp.concatenate([h, h], axis=-1) for h in head])


def local(
    hidden_in,
    positions,
    cotangent,
    norm_gains,
    norm_biases,
    w_qkv,
    b_qkv,
    w_q2,
    b_q2,
    w_out,
    w_up,
    b_up,
    w_down,
    out_bias,
):
    seqs, group, width = hidden_in.shape
    tokens = seqs * group
    hidden = w_up.shape[2]
    y, x, z, core = (lax.axis_index(a) for a in ("b0", "b1", Z, C))
    core_row = core.reshape(1).astype(jnp.int32)
    where = jnp.stack([y, x, z, core]).astype(jnp.int32)
    direct = square()
    x1 = hidden_in.reshape(tokens, width)
    g2 = cotangent.reshape(tokens, width)
    tab = rotary_tables(positions)

    na1, nm1, q1, kv_own = first_call(x1, norm_gains[0], norm_biases[0], w_qkv, b_qkv, tab, group)
    if direct:
        got = turns(lambda k: kv_own)
        y1, act1, slope1 = mlp_fwd_call(nm1, w_up, b_up, w_down, 0)
        mine = join([v[None] for v in (kv_own, *got)], (0,), where, (y1,))[0]
        theirs = swap(mine, C)
        kv = (mine, theirs)
        back = (z - jnp.arange(4)) % 4 * 2
        order = jnp.concatenate([back + core, back + 1 - core])
        do2 = back_call(g2, w_out, 1, (mine,))
    else:
        kv = (lax.all_gather(kv_own, (Z, C), axis=0, tiled=False),)
        order = jnp.arange(kv[0].shape[0])
        y1, act1, slope1 = mlp_fwd_call(nm1, w_up, b_up, w_down, 0)
        do2 = back_call(g2, w_out, 1)
    first = jnp.concatenate([((z * 2 + core) * group).reshape(1), order]).astype(jnp.int32)
    att1, lse1 = attend_call(first, q1, kv, (do2,))
    x2, na2, nm2, q2 = middle_call(
        att1, x1, y1, w_out, out_bias[0:1], norm_gains[1], norm_biases[1], w_q2, b_q2, tab
    )
    y2, dnm2, send, bup_send = mlp_back_call(core_row, nm2, g2, w_up, w_down, 1, b_up=b_up)
    got = swap(send.reshape(hidden, width), C)
    y2, dnm2, keep, bup_keep = mlp_back_call(
        core_row, nm2, g2, w_up, w_down, 1, b_up=b_up, before=(y2, dnm2)
    )
    keep = keep.reshape(hidden, width)

    def in_order(own, other):
        both = jnp.concatenate([own, other], axis=0)
        return jnp.where(core == 0, both, jnp.concatenate([other, own], axis=0)).reshape(-1, width)

    bup2 = in_order(bup_keep, bup_send)

    def swaps(one, two, axes):
        return swap(one, axes[0]), swap(two, axes[1])

    wait = ()
    if direct:
        one_send, one, two_send, two = sum_cores(keep, got, where)
        one_got, two_got = swaps(one_send, two_send, ("b1", "b0"))
        wait = (one,)
    else:
        mlp2 = add_low(keep, got)
    att2, lse2 = attend_call(first, q2, kv, wait)
    back2 = attend_back_call(first, q2, kv, att2, do2, lse2, tab, 0)
    if direct:
        one_send, one, two_send, two = sum_first(one, one_got, two, two_got, where, (back2[0],))
        one_got, two_got = swaps(one_send, two_send, ("b0", "b1"))
        wait = (one,)
    dq2, dkv2 = attend_back_call(first, q2, kv, att2, do2, lse2, tab, 1, before=back2, deps=wait)
    if direct:
        parts = sum_second(one, one_got, two, two_got, where, (dq2,))
        ahead = turns(lambda k: parts[k])
        wait = (parts[0],)
    hidden_out, early, g1, do1, small2 = turn_call(
        x2, y2, att2, att1, g2, na2, dq2, dnm2, w_out, w_q2, out_bias[1:2], norm_gains[1], deps=wait
    )
    dnm1, send, bup_send = mlp_back_call(
        core_row, nm1, g1, w_up, w_down, 0, kept=(act1, slope1)
    )
    got = swap(send.reshape(hidden, width), C)
    wait = ()
    if direct:
        mlp2 = sum_third([parts[0]] + ahead, where, (dnm1,))
        wait = (mlp2,)
        ahead = turns(lambda k: mlp2)
    dnm1, keep, bup_keep = mlp_back_call(
        core_row, nm1, g1, w_up, w_down, 0, kept=(act1, slope1), before=(dnm1,), deps=wait
    )
    keep = keep.reshape(hidden, width)
    bup1 = in_order(bup_keep, bup_send)
    if direct:
        one_send, one, two_send, two = sum_cores(keep, got, where)
        one_got, two_got = swaps(one_send, two_send, ("b1", "b0"))
        mlp2 = join([v[None] for v in (mlp2, *ahead)], (0,), where, (one,))[0]
        wait = (mlp2,)
        mlp2 = lax.all_gather(mlp2, B + (C,), axis=0, tiled=False)
    dq1, dkv1 = attend_back_call(
        first, q1, kv, att1, do1, lse1, tab, None, dkv2, deps=wait + (dnm1,)
    )
    if direct:
        one_send, one, two_send, two = sum_first(one, one_got, two, two_got, where, (dq1,))
        one_got, two_got = swaps(one_send, two_send, ("b0", "b1"))
    low = dkv1.astype(bf16)
    if direct:
        low = low.reshape(4, 2, group, -1)
        at = lambda c: lax.dynamic_index_in_dim(low, c, 1, keepdims=False)
        dkv_got = swap(at(1 - core), C)
        block = (1,) + low.shape[2:]
        dkv_parts = combine(
            [
                (
                    [
                        [
                            (
                                low.reshape((8,) + low.shape[2:]),
                                block,
                                lambda i, w, k=k: (lax.rem(w[2] + k, 4) * 2 + w[3], 0, 0),
                            ),
                            (dkv_got, block, lambda i, w, k=k: (lax.rem(w[2] + k, 4), 0, 0)),
                        ]
                    ],
                    block,
                    lambda i, w: (0, 0, 0),
                    block,
                )
                for k in range(4)
            ],
            where,
            (one,),
            name="sum_kv",
        )
        dkv_got = turns(lambda k: dkv_parts[k])
        dkv = sum_third([dkv_parts[0]] + dkv_got, where)[0]
        parts = sum_second(one, one_got, two, two_got, where, (dkv,))
        ahead = turns(lambda k: parts[k])
        wait = (parts[0],)
    else:
        dkv = lax.psum_scatter(low, (Z, C), scatter_dimension=0, tiled=True)
        mlp1 = add_low(keep, got)
        wait = ()
    grad_input, late_send, late = last_call(
        core_row, x1, g1, na1, dq1, dkv, dnm1, w_qkv, norm_gains[0], tab, small2, bup1, bup2, early, deps=wait
    )
    late_got = swap(late_send, C)

    if direct:
        both = sum_third([parts[0]] + ahead, where, (grad_input,), us=400)
        ahead = turns(lambda k: both)
        l1_send, l1, l2_send, l2 = sum_cores(late, late_got, where, (both,), us=1)
        l1_got, l2_got = swaps(l1_send, l2_send, ("b1", "b0"))
        l1_send, l1, l2_send, l2 = sum_first(l1, l1_got, l2, l2_got, where, us=1)
        l1_got, l2_got = swaps(l1_send, l2_send, ("b0", "b1"))
        one, two = join([both] + ahead, (0, 1), where, (l1,))
        one_got, two_got = swaps(one, two, ("b0", "b1"))
        parts = sum_second(l1, l1_got, l2, l2_got, where, (one,), us=1)
        late_ahead = turns(lambda k: parts[k])
        late = sum_third([parts[0]] + late_ahead, where, (mlp2,))
        outs = gather_blocks(late)
        one_near, two_near = (
            join([v[None], g[None]], (0,), where, (late,))[0].reshape(-1, width)
            for v, g in ((one, one_got), (two, two_got))
        )
        one_far, two_far = swaps(one_near, two_near, ("b1", "b0"))
        one_near_got, two_near_got = swap(one_near, C), swap(two_near, C)
        grad_down, grad_up = place_gathered(mlp2, 1, where, (one_near, two_near))
        mark = lambda c, v, u: c * 4 + v * 2 + u
        down_map = lambda w: (0, w, 0)
        up_map = lambda w: (0, w % 2, w // 2)

        def down_marks(c, far):
            u = 1 - x if far else x
            return (mark(c, y, u), mark(c, 1 - y, u))

        def up_marks(c, far):
            v = 1 - y if far else y
            return (mark(c, v, x), mark(c, v, 1 - x))

        def put(down, up, one, two, far, cores):
            down = place_relative(
                [(o, down_marks(c, far)) for o, c in zip(one, cores)], down_map, down.shape, down
            )
            up = place_relative(
                [(t, up_marks(c, far)) for t, c in zip(two, cores)], up_map, up.shape, up
            )
            return down, up

        near_one, near_two = (one_near, one_near_got), (two_near, two_near_got)
        grad_down, grad_up = put(grad_down, grad_up, near_one, near_two, False, (core, 1 - core))
        one_far, two_far = relay((one_far, two_far), where, (grad_down, grad_up))
        one_far_got, two_far_got = swap(one_far, C), swap(two_far, C)
        grad_down, grad_up = put(grad_down, grad_up, (one_far,), (two_far,), True, (core,))
        grad_down, grad_up = put(
            grad_down, grad_up, (one_far_got,), (two_far_got,), True, (1 - core,)
        )
    else:
        mlp2 = gather_offloaded(reduce_offloaded(mlp2))
        placed = place_ordered(mlp2, 1)
        grad_down, grad_up = place_ordered(gather_offloaded(reduce_offloaded(mlp1)), 0, placed)
        outs = gather_offloaded(reduce_offloaded(add_low(late, late_got)))
        outs = outs.reshape(8, 2, 4, -1, width).transpose(0, 2, 1, 3, 4).reshape(32, 2, -1, width)
    grad_out, grad_q2, grad_qkv, small = finish_call(outs)
    one, two = small[0:8], small[8:16]
    ups = hidden // width
    grad_up_bias = jnp.stack([small[16 : 16 + ups].reshape(-1), small[16 + ups : 16 + 2 * ups].reshape(-1)])
    grad_gains = jnp.stack([one[0:2], two[0:2]])
    grad_biases = jnp.stack([one[2:4], two[2:4]])
    grad_qkv_bias = jnp.concatenate([one[4], one[5, :128]])
    grad_out_bias = jnp.stack([two[6], two[4]])
    return (
        hidden_out.reshape(seqs, group, width),
        grad_input.reshape(seqs, group, width),
        grad_gains,
        grad_biases,
        grad_qkv,
        grad_qkv_bias,
        grad_q2,
        two[5],
        grad_out,
        grad_up,
        grad_up_bias,
        grad_down,
        grad_out_bias,
    )


def solution(mesh):
    batch, seq = mesh.shape["batch"], mesh.shape["seq"]
    fine = jax.sharding.Mesh(
        mesh.devices.reshape(2, batch // 2, seq // 2, 2), ("b0", "b1", "z", "c")
    )
    rows = P(B, (Z, C), None)
    return jax.shard_map(
        local,
        mesh=fine,
        in_specs=(rows, P(B, (Z, C)), rows) + (P(),) * 11,
        out_specs=(rows, rows) + (P(),) * 11,
        check_vma=False,
    )
```

```python
from functools import partial

import jax
import jax.numpy as jnp
from jax import lax
from jax.experimental import pallas as pl
from jax.experimental.pallas import tpu as pltpu
from jax.sharding import PartitionSpec as P

ROT = 16
EPSILON = 1e-05
SCALE = 0.125
NEGATIVE = -1e30
BASE = 10000.0

B = ("b0", "b1")
Z = "z"
C = "c"
TILE = 768
QUARTER = TILE // 2
EXTRA = 256
KB = 256

f32 = jnp.float32
bf16 = jnp.bfloat16


def dot_nn(a, b):
    return lax.dot_general(a, b, (((1,), (0,)), ((), ())), preferred_element_type=f32)


def dot_nt(a, b):
    return lax.dot_general(a, b, (((1,), (1,)), ((), ())), preferred_element_type=f32)


def dot_tn(a, b):
    return lax.dot_general(a, b, (((0,), (0,)), ((), ())), preferred_element_type=f32)


def invoke(
    kernel, operands, deps, *, grid, in_specs, out_specs, out_shape, name, scalars=(), scratch=(), aliases={}, us=2, vmem=50
):
    ahead = len(scalars) + len(operands)

    def body(*refs):
        kernel(*refs[:ahead], *refs[ahead + len(deps) :])

    return pl.pallas_call(
        body,
        grid_spec=pltpu.PrefetchScalarGridSpec(
            num_scalar_prefetch=len(scalars),
            grid=grid,
            in_specs=list(in_specs) + [pl.BlockSpec(memory_space=pl.ANY)] * len(deps),
            out_specs=out_specs,
            scratch_shapes=scratch,
        ),
        out_shape=out_shape,
        input_output_aliases=aliases,
        compiler_params=pltpu.CompilerParams(vmem_limit_bytes=vmem << 20),
        cost_estimate=pl.CostEstimate(
            flops=us * 600_000_000, bytes_accessed=us * 1_000_000, transcendentals=0
        ),
        name=name,
    )(*scalars, *operands, *deps)


def layer_spec(shape, layer):
    return pl.BlockSpec((1,) + shape, lambda *i: (layer,) + (0,) * len(shape))


def full_spec(shape):
    return pl.BlockSpec(shape, lambda *i: (0,) * len(shape))


def unit_rows(values):
    center = values - jnp.mean(values, axis=-1, keepdims=True)
    spread = jnp.mean(center * center, axis=-1, keepdims=True)
    inverse = lax.rsqrt(spread + EPSILON)
    return center * inverse, inverse


def turn(values, cos_tab, sin_low, sin_high):
    return (
        values * cos_tab
        + pltpu.roll(values, 120, 1) * sin_low
        + pltpu.roll(values, 8, 1) * sin_high
    )


def pairs_down(values):
    return jnp.concatenate(
        [values[:, p * 128 : (p + 1) * 128] for p in range(values.shape[1] // 128)], axis=0
    )


def gelu_parts(lifted):
    cdf = 0.5 + 0.5 * lax.erf(lifted * 0.7071067811865476)
    slope = cdf + lifted * (0.3989422804014327 * jnp.exp(-0.5 * lifted * lifted))
    return lifted * cdf, slope


def first_kernel(x_ref, gain_ref, off_ref, w_ref, b_ref, tab_ref, na_ref, nm_ref, q_ref, kv_ref):
    tokens, width = x_ref.shape
    unit = unit_rows(x_ref[...].astype(f32))[0]
    norm_a = (unit * gain_ref[0:1] + off_ref[0:1]).astype(bf16)
    na_ref[...] = norm_a
    nm_ref[...] = (unit * gain_ref[1:2] + off_ref[1:2]).astype(bf16)
    cos_tab, sin_low, sin_high = tab_ref[0], tab_ref[1], tab_ref[2]
    kv = dot_nn(norm_a, w_ref[:, width:]) + b_ref[:, width:]
    low_half = lax.broadcasted_iota(jnp.int32, kv.shape, 1) < 64
    kv = jnp.where(low_half, turn(kv, cos_tab, sin_low, sin_high), kv).astype(bf16)
    group = kv_ref.shape[0]
    for s in range(tokens // group):
        kv_ref[:, s * 128 : (s + 1) * 128] = kv[s * group : (s + 1) * group]
    proj = dot_nn(norm_a, w_ref[:, :width]) + b_ref[:, :width]
    for p in range(width // 128):
        cols = slice(p * 128, (p + 1) * 128)
        q_ref[:, cols] = (turn(proj[:, cols], cos_tab, sin_low, sin_high) * SCALE).astype(bf16)


def first_call(x, gains, offs, w_qkv, b_qkv, tab, group):
    tokens, width = x.shape
    operands = (x, gains, offs, w_qkv, b_qkv.reshape(1, -1), tab)
    shapes = [(tokens, width)] * 3 + [(group, tokens // group * 128)]
    return invoke(
        first_kernel,
        operands,
        (),
        grid=(1,),
        in_specs=[full_spec(v.shape) for v in operands],
        out_specs=[full_spec(v) for v in shapes],
        out_shape=[jax.ShapeDtypeStruct(v, bf16) for v in shapes],
        name="first",
        us=3,
    )


def mlp_fwd_kernel(nm_ref, up_ref, bup_ref, down_ref, y_ref, act_ref, slope_ref):
    lifted = dot_nn(nm_ref[...], up_ref[0]) + bup_ref[...]
    active, slope = gelu_parts(lifted)
    active = active.astype(bf16)
    act_ref[...] = active
    slope_ref[...] = slope.astype(bf16)

    @pl.when(pl.program_id(0) == 0)
    def _():
        y_ref[...] = jnp.zeros_like(y_ref)

    y_ref[...] += dot_nn(active, down_ref[0])


def mlp_fwd_call(nm, w_up, b_up, w_down, layer):
    tokens, width = nm.shape
    hidden = w_up.shape[2]
    return invoke(
        mlp_fwd_kernel,
        (nm, w_up, b_up[layer : layer + 1], w_down),
        (),
        grid=(hidden // TILE,),
        in_specs=[
            full_spec((tokens, width)),
            pl.BlockSpec((1, width, TILE), lambda t: (layer, 0, t)),
            pl.BlockSpec((1, TILE), lambda t: (0, t)),
            pl.BlockSpec((1, TILE, width), lambda t: (layer, t, 0)),
        ],
        out_specs=[
            full_spec((tokens, width)),
            pl.BlockSpec((tokens, TILE), lambda t: (0, t)),
            pl.BlockSpec((tokens, TILE), lambda t: (0, t)),
        ],
        out_shape=[
            jax.ShapeDtypeStruct((tokens, width), f32),
            jax.ShapeDtypeStruct((tokens, hidden), bf16),
            jax.ShapeDtypeStruct((tokens, hidden), bf16),
        ],
        name="mlp_fwd",
        us=10,
    )


def mlp_grads(active, slope, nm, nm_turned, grad, up, down, start, refs):
    grad_norm_ref, rows_ref, bias_ref = refs
    grad_lifted = (dot_nt(grad, down) * slope).astype(bf16)
    bias_ref[...] = jnp.sum(grad_lifted.astype(f32), axis=0, keepdims=True)

    @pl.when(pl.program_id(0) == 0)
    def _():
        grad_norm_ref[...] = jnp.zeros_like(grad_norm_ref) if start is None else start[...]
        nm_turned[...] = nm.T

    grad_norm_ref[...] += dot_nt(grad_lifted, up)
    grad_down = dot_tn(active, grad).astype(bf16)
    grad_up = dot_nn(nm_turned[...], grad_lifted).astype(bf16)
    for j in range(2):
        rows = slice(j * QUARTER, (j + 1) * QUARTER)
        rows_ref[0, 2 * j * QUARTER : (2 * j + 1) * QUARTER] = grad_down[rows]
        rows_ref[0, (2 * j + 1) * QUARTER : (2 * j + 2) * QUARTER] = grad_up[rows]


def mlp_both_kernel(more, core_ref, nm_ref, g_ref, up_ref, bup_ref, down_ref, *refs):
    y_start, grad_start = refs[:2] if more else (None, None)
    y_ref, *outs, nm_turned = refs[2:] if more else refs
    nm, up, down = nm_ref[...], up_ref[0], down_ref[0]
    active, slope = gelu_parts(dot_nn(nm, up) + bup_ref[...])
    active = active.astype(bf16)

    @pl.when(pl.program_id(0) == 0)
    def _():
        y_ref[...] = y_start[...] if more else jnp.zeros_like(y_ref)

    y_ref[...] += dot_nn(active, down)
    mlp_grads(active, slope, nm, nm_turned, g_ref[...], up, down, grad_start, outs)


def mlp_back_kernel(more, core_ref, nm_ref, g_ref, up_ref, down_ref, act_ref, slope_ref, *refs):
    grad_start = refs[0] if more else None
    *outs, nm_turned = refs[1:] if more else refs
    slope = slope_ref[...].astype(f32)
    mlp_grads(
        act_ref[...], slope, nm_ref[...], nm_turned, g_ref[...], up_ref[0], down_ref[0], grad_start, outs
    )


def mlp_back_call(core, nm, grad, w_up, w_down, layer, b_up=None, kept=None, before=None, deps=()):
    tokens, width = nm.shape
    hidden = w_up.shape[2]
    half = hidden // TILE // 2
    other = before is None

    def tile(t, core_ref):
        c = core_ref[0]
        return (1 - c if other else c) * half + t

    whole = full_spec((tokens, width))
    whole_shape = jax.ShapeDtypeStruct((tokens, width), f32)
    up_spec = pl.BlockSpec((1, width, TILE), lambda t, c: (layer, 0, tile(t, c)))
    down_spec = pl.BlockSpec((1, TILE, width), lambda t, c: (layer, tile(t, c), 0))
    cols_spec = pl.BlockSpec((tokens, TILE), lambda t, c: (0, tile(t, c)))
    both = kept is None
    if both:
        bias_spec = pl.BlockSpec((1, TILE), lambda t, c: (0, tile(t, c)))
        in_specs = [whole, whole, up_spec, bias_spec, down_spec]
        operands = (nm, grad, w_up, b_up[layer : layer + 1], w_down)
    else:
        in_specs = [whole, whole, up_spec, down_spec, cols_spec, cols_spec]
        operands = (nm, grad, w_up, w_down) + kept
    before = tuple(before or ())
    count = 2 if both else 1
    return invoke(
        partial(mlp_both_kernel if both else mlp_back_kernel, not other),
        operands + before,
        deps,
        scalars=(core,),
        grid=(half,),
        in_specs=in_specs + [whole] * len(before),
        out_specs=[whole] * count
        + [
            pl.BlockSpec((1, 2 * TILE, width), lambda t, c: (t, 0, 0)),
            pl.BlockSpec((1, TILE), lambda t, c: (0, t)),
        ],
        out_shape=[whole_shape] * count
        + [
            jax.ShapeDtypeStruct((half, 2 * TILE, width), bf16),
            jax.ShapeDtypeStruct((1, hidden // 2), f32),
        ],
        scratch=[pltpu.VMEM((width, tokens), bf16)],
        name="mlp_both" if both else "mlp_back",
        us=40 if both else (12 if other else 150),
    )


def spread_kv(pieces, order_ref, k0, k1, turned, forward):
    at = 0
    for ref in pieces:
        for p in range(ref.shape[0]):
            kv = ref[p].astype(f32)
            rows = kv.shape[0]
            swapped = pltpu.roll(kv, 64, 1)
            low_half = lax.broadcasted_iota(jnp.int32, kv.shape, 1) < 64
            zero = jnp.zeros_like(kv)
            block = order_ref[1 + at]
            place = pl.ds(pl.multiple_of(block * rows, rows), rows)
            k0[place] = jnp.where(low_half, kv, zero).astype(bf16)
            k1[place] = jnp.where(low_half, zero, swapped).astype(bf16)
            if forward:
                t0, t1 = turned
                rest = jnp.ones((64, rows), f32)
                part = kv.T[64:]
            else:
                v0, v1, t0, t1 = turned
                v0[place] = jnp.where(low_half, swapped, zero).astype(bf16)
                v1[place] = jnp.where(low_half, zero, kv).astype(bf16)
                rest = jnp.zeros((64, rows), f32)
                part = kv.T[:64]
            t0[block] = jnp.concatenate([part, rest], axis=0).astype(bf16)
            t1[block] = jnp.concatenate([rest, part], axis=0).astype(bf16)
            at += 1


def block_rows(index):
    return pl.ds(pl.multiple_of(index * KB, KB), KB)


def turned_block(ref, index):
    return jnp.concatenate([ref[2 * index], ref[2 * index + 1]], axis=1)


def visible(shape, first, start, group):
    key = lax.broadcasted_iota(jnp.int32, shape, 0)
    token = lax.broadcasted_iota(jnp.int32, shape, 1) % group
    return key - token <= first - start


def attend_kernel(count, first_ref, q_ref, *refs):
    pieces, (o_ref, lse_ref, k0, k1, t0, t1) = refs[:count], refs[count:]
    first = first_ref[0]
    group, width = q_ref.shape
    spread_kv(pieces, first_ref, k0, k1, (t0, t1), True)
    q6 = pairs_down(q_ref[...])
    full = first // KB

    def block(kb, carry):
        done = []
        for keys, vals, (top, summed) in zip((k0, k1), (t0, t1), carry or (2 * ((None, None),))):
            scores = dot_nt(keys[block_rows(kb), :], q6)
            if carry is None:
                scores = jnp.where(
                    visible(scores.shape, first, full * KB, group), scores, NEGATIVE
                )
            new_top = jnp.max(scores, axis=0, keepdims=True)
            if carry is not None:
                new_top = jnp.maximum(top, new_top)
            weights = jnp.exp(scores - new_top).astype(bf16)
            part = dot_nn(turned_block(vals, kb), weights)
            if carry is not None:
                part = part + summed * jnp.exp(top - new_top)
            done.append((new_top, part))
        return tuple(done)

    (top0, sum0), (top1, sum1) = lax.fori_loop(0, full, block, block(full, None))
    total0, total1 = sum0[64:65], sum1[0:1]
    both = jnp.concatenate([sum0[:64] / total0, sum1[64:] / total1], axis=0).T.astype(bf16)
    for p in range(width // 128):
        o_ref[:, p * 128 : (p + 1) * 128] = both[p * group : (p + 1) * group]
    shape = lse_ref.shape[2:]
    lse_ref[0, 0] = jnp.broadcast_to(top0 + jnp.log(total0), shape)
    lse_ref[0, 1] = jnp.broadcast_to(top1 + jnp.log(total1), shape)


def piece_specs(kv):
    return [pl.BlockSpec(v.shape[:2] + (128,), lambda s, f: (0, 0, s)) for v in kv]


def attend_call(first, q, kv, deps=()):
    tokens, width = q.shape
    length = sum(v.shape[0] for v in kv) * kv[0].shape[1]
    seqs = kv[0].shape[2] // 128
    group = tokens // seqs
    rows = group * width // 128
    return invoke(
        partial(attend_kernel, len(kv)),
        (q,) + kv,
        deps,
        scalars=(first,),
        grid=(seqs,),
        in_specs=[pl.BlockSpec((group, width), lambda s, f: (s, 0))] + piece_specs(kv),
        out_specs=[
            pl.BlockSpec((group, width), lambda s, f: (s, 0)),
            pl.BlockSpec((1, 2, 8, rows), lambda s, f: (s, 0, 0, 0)),
        ],
        scratch=[pltpu.VMEM((length, 128), bf16)] * 2
        + [pltpu.VMEM((length // 128, 128, 128), bf16)] * 2,
        out_shape=[
            jax.ShapeDtypeStruct((tokens, width), bf16),
            jax.ShapeDtypeStruct((seqs, 2, 8, rows), f32),
        ],
        name="attend",
        us=60,
    )


def attend_back_kernel(count, has_start, unread, first_ref, q_ref, *refs):
    pieces, refs = refs[:count], refs[count:]
    ins = 5 if has_start else 4
    refs = refs[:ins] + refs[ins + unread :]
    if has_start:
        o_ref, do_ref, lse_ref, tab_ref, start_ref, dq_out, low_ref, k0, k1, v0, v1, t0, t1, dq_ref, dkv_ref = refs
        dkv_ref[...] = start_ref[...]
    else:
        o_ref, do_ref, lse_ref, tab_ref, dq_out, dkv_ref, k0, k1, v0, v1, t0, t1, dq_ref = refs
        dkv_ref[...] = jnp.zeros_like(dkv_ref)
    first = first_ref[0]
    group = q_ref.shape[0]
    spread_kv(pieces, first_ref, k0, k1, (v0, v1, t0, t1), False)
    q6 = pairs_down(q_ref[...])
    do6 = pairs_down(do_ref[...])
    deltas = (do6.astype(f32) * pairs_down(o_ref[...]).astype(f32)).T
    halves = (
        (k0, v0, lse_ref[0, 0, 0:1], jnp.sum(deltas[:64], axis=0, keepdims=True)),
        (k1, v1, lse_ref[0, 1, 0:1], jnp.sum(deltas[64:], axis=0, keepdims=True)),
    )
    dq_ref[...] = jnp.zeros_like(dq_ref)
    full = first // KB
    low_half = lax.broadcasted_iota(jnp.int32, (KB, 128), 1) < 64

    def block(kb, masked):
        rows = block_rows(kb)
        grads, keys, vals = [], [], []
        for k, v, lse, delta in halves:
            probs = jnp.exp(dot_nt(k[rows, :], q6) - lse)
            if masked:
                probs = jnp.where(visible(probs.shape, first, full * KB, group), probs, 0.0)
            grad_probs = dot_nt(v[rows, :], do6)
            grad_scores = (probs * (grad_probs - delta)).astype(bf16)
            grads.append(grad_scores)
            keys.append(dot_nn(grad_scores, q6))
            vals.append(dot_nn(probs.astype(bf16), do6))
        dkv_ref[rows, :] += jnp.where(low_half, keys[0], vals[1]) + pltpu.roll(
            jnp.where(low_half, vals[0], keys[1]), 64, 1
        )
        turned = jnp.concatenate([turned_block(t0, kb), turned_block(t1, kb)], axis=1)
        dq_ref[...] += dot_nn(turned, jnp.concatenate(grads, axis=0))

    block(full, True)

    def step(kb, carry):
        block(kb, False)
        return carry

    lax.fori_loop(0, full, step, 0)
    if has_start:
        low_ref[...] = dkv_ref[...].astype(bf16)
    cos_tab, sin_low, sin_high = tab_ref[0], -tab_ref[1], -tab_ref[2]
    dq = dq_ref[...].T * SCALE
    for p in range(q_ref.shape[1] // 128):
        part = dq[p * group : (p + 1) * group]
        dq_out[:, p * 128 : (p + 1) * 128] = turn(part, cos_tab, sin_low, sin_high).astype(bf16)


def attend_back_call(first, q, kv, attended, grad, lse, tab, part, start=None, before=(), deps=()):
    tokens, width = q.shape
    length = sum(v.shape[0] for v in kv) * kv[0].shape[1]
    seqs = kv[0].shape[2] // 128
    group = tokens // seqs
    rows = group * width // 128
    count = seqs if part is None else seqs // 2
    at = (part or 0) * count
    tok_spec = pl.BlockSpec((group, width), lambda s, f: (at + s, 0))
    len_spec = pl.BlockSpec((length, 128), lambda s, f: (0, at + s))
    in_specs = [
        tok_spec,
        *[pl.BlockSpec(v.shape[:2] + (128,), lambda s, f: (0, 0, at + s)) for v in kv],
        tok_spec,
        tok_spec,
        pl.BlockSpec((1, 2, 8, rows), lambda s, f: (at + s, 0, 0, 0)),
        pl.BlockSpec((3, group, 128), lambda s, f: (0, at + s, 0)),
    ]
    operands = [q, *kv, attended, grad, lse, tab]
    if start is not None:
        in_specs.append(len_spec)
        operands.append(start)
    return invoke(
        partial(attend_back_kernel, len(kv), start is not None, len(before)),
        operands + list(before),
        deps,
        scalars=(first,),
        grid=(count,),
        in_specs=in_specs + [pl.BlockSpec(memory_space=pl.ANY)] * len(before),
        out_specs=[tok_spec, len_spec],
        scratch=[pltpu.VMEM((length, 128), bf16)] * 4
        + [pltpu.VMEM((length // 128, 128, 128), bf16)] * 2
        + [pltpu.VMEM((128, rows), f32)]
        + ([] if start is None else [pltpu.VMEM((length, 128), f32)]),
        out_shape=[
            jax.ShapeDtypeStruct((tokens, width), bf16),
            jax.ShapeDtypeStruct((length, seqs * 128), f32 if start is None else bf16),
        ],
        aliases={1 + len(operands) + i: i for i in range(len(before))},
        name="attend_back",
        us=45,
    )


def back_kernel(g_ref, w_ref, out_ref):
    out_ref[...] = dot_nt(g_ref[...], w_ref[0]).astype(bf16)


def back_call(grad, w_out, layer, deps=()):
    tokens, width = grad.shape
    return invoke(
        back_kernel,
        (grad, w_out),
        deps,
        grid=(1,),
        in_specs=[full_spec((tokens, width)), layer_spec((width, width), layer)],
        out_specs=full_spec((tokens, width)),
        out_shape=jax.ShapeDtypeStruct((tokens, width), bf16),
        name="back",
    )


def middle_kernel(
    att_ref, x_ref, y_ref, wo_ref, bias_ref, gain_ref, off_ref, wq_ref, bq_ref, tab_ref,
    x2_ref, na_ref, nm_ref, q_ref,
):
    second = (
        x_ref[...].astype(f32) + dot_nn(att_ref[...], wo_ref[0]) + y_ref[...] + bias_ref[...]
    ).astype(bf16)
    x2_ref[...] = second
    unit = unit_rows(second.astype(f32))[0]
    norm_a = (unit * gain_ref[0:1] + off_ref[0:1]).astype(bf16)
    na_ref[...] = norm_a
    nm_ref[...] = (unit * gain_ref[1:2] + off_ref[1:2]).astype(bf16)
    proj = dot_nn(norm_a, wq_ref[...]) + bq_ref[...]
    cos_tab, sin_low, sin_high = tab_ref[0], tab_ref[1], tab_ref[2]
    for p in range(proj.shape[1] // 128):
        cols = slice(p * 128, (p + 1) * 128)
        q_ref[:, cols] = (turn(proj[:, cols], cos_tab, sin_low, sin_high) * SCALE).astype(bf16)


def middle_call(att, x, y, w_out, bias, gains, offs, w_q2, b_q2, tab):
    tokens, width = x.shape
    operands = (att, x, y, w_out, bias, gains, offs, w_q2, b_q2.reshape(1, -1), tab)
    specs = [full_spec(v.shape) for v in operands]
    specs[3] = layer_spec((width, width), 0)
    return invoke(
        middle_kernel,
        operands,
        (),
        grid=(1,),
        in_specs=specs,
        out_specs=[full_spec((tokens, width))] * 4,
        out_shape=[jax.ShapeDtypeStruct((tokens, width), bf16)] * 4,
        name="middle",
        us=5,
    )


def norm_back(values, grad_a, grad_m, gain_ref, small_ref, row):
    unit, inverse = unit_rows(values)
    small_ref[row : row + 1] = jnp.sum(grad_a * unit, axis=0, keepdims=True)
    small_ref[row + 1 : row + 2] = jnp.sum(grad_m * unit, axis=0, keepdims=True)
    small_ref[row + 2 : row + 3] = jnp.sum(grad_a, axis=0, keepdims=True)
    small_ref[row + 3 : row + 4] = jnp.sum(grad_m, axis=0, keepdims=True)
    grad_unit = grad_a * gain_ref[0:1] + grad_m * gain_ref[1:2]
    return inverse * (
        grad_unit
        - jnp.mean(grad_unit, axis=-1, keepdims=True)
        - unit * jnp.mean(grad_unit * unit, axis=-1, keepdims=True)
    )


def by_core(core, send_ref, keep_ref, put):
    @pl.when(core == 0)
    def _():
        put(keep_ref, send_ref)

    @pl.when(core != 0)
    def _():
        put(send_ref, keep_ref)


def turn_kernel(
    x2_ref, y_ref, att2_ref, att1_ref, g_ref, na_ref, dq_ref, dnm_ref, wo1_ref, wo2_ref, wq_ref, bias_ref, gain_ref,
    hidden_ref, grads_ref, g1_ref, do1_ref, small_ref,
):
    width = x2_ref.shape[1]
    second = x2_ref[...].astype(f32)
    att2, grad, dq = att2_ref[...], g_ref[...], dq_ref[...]
    wide = grad.astype(f32)
    small_ref[...] = jnp.zeros_like(small_ref)
    grad_a = dot_nt(dq, wq_ref[...])
    g1 = (norm_back(second, grad_a, dnm_ref[...], gain_ref, small_ref, 0) + wide).astype(bf16)
    g1_ref[...] = g1
    do1_ref[...] = dot_nt(g1, wo1_ref[0]).astype(bf16)
    small_ref[4:5] = jnp.sum(wide, axis=0, keepdims=True)
    small_ref[5:6] = jnp.sum(dq.astype(f32), axis=0, keepdims=True)
    small_ref[6:7] = jnp.sum(g1.astype(f32), axis=0, keepdims=True)
    grads_ref[0:width] = dot_tn(att2, grad).astype(bf16)
    grads_ref[width : 2 * width] = dot_tn(na_ref[...], dq).astype(bf16)
    grads_ref[2 * width : 3 * width] = dot_tn(att1_ref[...], g1).astype(bf16)
    hidden_ref[...] = (second + dot_nn(att2, wo2_ref[0]) + y_ref[...] + bias_ref[...]).astype(bf16)


def turn_call(x2, y2, att2, att1, g, na2, dq2, dnm2, w_out, w_q2, bias, gains, deps=()):
    tokens, width = x2.shape
    operands = (x2, y2, att2, att1, g, na2, dq2, dnm2, w_out, w_out, w_q2, bias, gains)
    specs = [full_spec(v.shape) for v in operands]
    specs[8] = layer_spec((width, width), 0)
    specs[9] = layer_spec((width, width), 1)
    tok = full_spec((tokens, width))
    tok_shape = jax.ShapeDtypeStruct((tokens, width), bf16)
    return invoke(
        turn_kernel,
        operands,
        deps,
        grid=(1,),
        in_specs=specs,
        out_specs=[tok, full_spec((3 * width, width)), tok, tok, full_spec((8, width))],
        out_shape=[
            tok_shape,
            jax.ShapeDtypeStruct((3 * width, width), bf16),
            tok_shape,
            tok_shape,
            jax.ShapeDtypeStruct((8, width), f32),
        ],
        name="turn",
        us=60,
    )


def last_kernel(
    core_ref, x_ref, g1_ref, na_ref, dq_ref, dkv_ref, dnm_ref, w_ref, gain_ref, tab_ref, small2_ref, bup1_ref, bup2_ref,
    early_ref, grad_ref, send_ref, keep_ref, small_ref,
):
    tokens, width = x_ref.shape
    group = dkv_ref.shape[0]
    dkv = jnp.concatenate(
        [dkv_ref[:, s * 128 : (s + 1) * 128] for s in range(tokens // group)], axis=0
    ).astype(f32)
    low_half = lax.broadcasted_iota(jnp.int32, dkv.shape, 1) < 64
    dkv = jnp.where(low_half, turn(dkv, tab_ref[0], -tab_ref[1], -tab_ref[2]), dkv).astype(bf16)
    dq, norm_a = dq_ref[...], na_ref[...]
    small_ref[...] = jnp.zeros_like(small_ref)
    small_ref[4:5] = jnp.sum(dq.astype(f32), axis=0, keepdims=True)
    small_ref[5:6, 0:128] = jnp.sum(dkv.astype(f32), axis=0, keepdims=True)
    grad_a = dot_nt(dq, w_ref[:, :width]) + dot_nt(dkv, w_ref[:, width:])
    grad_ref[...] = g1_ref[...].astype(f32) + norm_back(
        x_ref[...].astype(f32), grad_a, dnm_ref[...], gain_ref, small_ref, 0
    )
    q1 = dot_tn(norm_a, dq).astype(bf16)
    kv = dot_tn(dkv, norm_a).astype(bf16)
    smalls = [small_ref[...], small2_ref[...], bup1_ref[...], bup2_ref[...]]
    smalls.append(jnp.zeros((EXTRA - 128 - sum(v.shape[0] for v in smalls), width), f32))
    smalls = jnp.concatenate(smalls, axis=0).astype(bf16)

    def put(one, two):
        one[: 2 * width] = early_ref[: 2 * width]
        one[2 * width : 2 * width + 128] = kv
        one[2 * width + 128 :] = smalls
        two[:width] = early_ref[2 * width :]
        two[width : 2 * width] = q1
        two[2 * width :] = jnp.zeros((EXTRA, width), bf16)

    by_core(core_ref[0], send_ref, keep_ref, put)


def last_call(core, x, g1, na1, dq1, dkv, dnm1, w_qkv, gains, tab, small2, bup1, bup2, early, deps=()):
    tokens, width = x.shape
    operands = (x, g1, na1, dq1, dkv, dnm1, w_qkv, gains, tab, small2, bup1, bup2, early)
    out_shape = [
        jax.ShapeDtypeStruct((tokens, width), f32),
        jax.ShapeDtypeStruct((2 * width + EXTRA, width), bf16),
        jax.ShapeDtypeStruct((2 * width + EXTRA, width), bf16),
    ]
    return invoke(
        last_kernel,
        operands,
        deps,
        scalars=(core,),
        grid=(1,),
        in_specs=[full_spec(v.shape) for v in operands],
        out_specs=[full_spec(v.shape) for v in out_shape],
        out_shape=out_shape,
        scratch=[pltpu.VMEM((8, width), f32)],
        name="last",
        us=10,
    )


PAIR = [(0, 1), (1, 0)]


def swap(values, axis):
    return lax.ppermute(values, axis, PAIR)


def add_low(first, *rest):
    total = first.astype(f32)
    for value in rest:
        total = total + value.astype(f32)
    return total.astype(bf16)


def pick(values, index):
    return lax.dynamic_index_in_dim(values, index, 0, keepdims=False)


def square():
    return lax.axis_size("b0") == 2 and lax.axis_size("b1") == 2 and lax.axis_size(Z) == 4


def turns(values_at):
    size = lax.axis_size(Z)
    return [
        lax.ppermute(values_at(k), Z, [(i, (i + k) % size) for i in range(size)])
        for k in range(1, size)
    ]


def reduce_offloaded(part):
    part = lax.psum_scatter(part, B, scatter_dimension=0, tiled=True)
    return lax.psum_scatter(part, Z, scatter_dimension=0, tiled=True)


def gather_offloaded(part):
    return lax.all_gather(part, (C,) + B + (Z,), axis=0, tiled=True)


def combine(groups, where, deps, grid=(1,), name="combine", us=2, vmem=50):
    terms = [t for sums, *_ in groups for parts in sums for t in parts]

    def kernel(where_ref, *refs):
        ins, outs = iter(refs[: len(terms)]), refs[len(terms) :]
        for (sums, *_), out_ref in zip(groups, outs):
            for i, parts in enumerate(sums):
                total = next(ins)[...].astype(f32)
                for _ in parts[1:]:
                    total = total + next(ins)[...].astype(f32)
                if len(sums) == 1:
                    out_ref[...] = total.reshape(out_ref.shape).astype(bf16)
                else:
                    out_ref[i] = total.reshape(out_ref.shape[1:]).astype(bf16)

    return invoke(
        kernel,
        [t[0] for t in terms],
        deps,
        scalars=(where,),
        grid=grid,
        in_specs=[pl.BlockSpec(t[1], t[2]) for t in terms],
        out_specs=[pl.BlockSpec(g[1], g[2]) for g in groups],
        out_shape=[jax.ShapeDtypeStruct(g[3], bf16) for g in groups],
        name=name,
        us=us,
        vmem=vmem,
    )


def sum_cores(keep, got, where, deps=(), us=20):
    width = keep.shape[-1]
    keep, got = (v.reshape(2, 2, 2, -1, width) for v in (keep, got))
    quarter = keep.shape[3]
    half = quarter // 2
    maps = (
        lambda i, j, w: (i, 1 - w[1], 0, j, 0),
        lambda i, j, w: (i, w[1], 0, j, 0),
        lambda i, j, w: (1 - w[0], i, 1, j, 0),
        lambda i, j, w: (w[0], i, 1, j, 0),
    )
    block = (1, 1, 1, half, width)
    groups = [
        (
            [[(keep, block, m), (got, block, m)]],
            (1, half, width),
            lambda i, j, w: (i, j, 0),
            (2, quarter, width),
        )
        for m in maps
    ]
    return combine(groups, where, deps, grid=(2, 2), name="sum_cores", us=us)


def sum_first(one, one_got, two, two_got, where, deps=(), us=30):
    _, quarter, width = one.shape
    half = quarter // 2
    groups = []
    for values, got, m in (
        (one, one_got, lambda j, w: (1 - w[0], j, 0)),
        (one, one_got, lambda j, w: (w[0], j, 0)),
        (two, two_got, lambda j, w: (1 - w[1], j, 0)),
        (two, two_got, lambda j, w: (w[1], j, 0)),
    ):
        block = (1, half, width)
        groups.append(
            ([[(values, block, m), (got, block, m)]], block, lambda j, w: (0, j, 0), (1, quarter, width))
        )
    return combine(groups, where, deps, grid=(2,), name="sum_first", us=us)


def sum_second(one, one_got, two, two_got, where, deps=(), us=100):
    width = one.shape[-1]
    one, one_got, two, two_got = (v.reshape(4, -1, width) for v in (one, one_got, two, two_got))
    block = (1,) + one.shape[1:]
    groups = []
    for k in range(4):
        m = lambda i, w, k=k: (lax.rem(w[2] + k, 4), 0, 0)
        groups.append(
            (
                [[(a, block, m), (b, block, m)] for a, b in ((one, one_got), (two, two_got))],
                (2,) + one.shape[1:],
                lambda i, w: (0, 0, 0),
                (2,) + one.shape[1:],
            )
        )
    return combine(groups, where, deps, name="sum_second", us=us)


def sum_third(parts, where, deps=(), us=10):
    shape = parts[0].shape
    m = lambda i, w: (0, 0, 0)
    return combine([([[(p, shape, m) for p in parts]], shape, m, shape)], where, deps, name="sum_third", us=us)[0]


def join(parts, leads, where, deps=()):
    shape = parts[0].shape[1:]
    groups = [
        (
            [[(p, (1,) + shape, lambda i, w, a=a: (a,) + (0,) * len(shape))] for p in parts],
            (len(parts),) + shape,
            lambda i, w: (0,) * (len(shape) + 1),
            (len(parts),) + shape,
        )
        for a in leads
    ]
    return combine(groups, where, deps, name="join")


def gather_blocks(both):
    return lax.all_gather(both, (C,) + B + (Z,), axis=0, tiled=False)


def relay(values, where, deps):
    block = (values[0].shape[0] // 2, values[0].shape[1])
    m = lambda i, w: (i, 0)
    groups = [([[(v, block, m)]], block, m, v.shape) for v in values]
    return combine(groups, where, deps, grid=(2,), name="relay")


def place_kernel(count, quarter, where_ref, *refs):
    ins, out_ref = refs[:count], refs[-1]
    step = pl.program_id(0)
    z = where_ref[2 * count]
    unit = quarter // 4
    for a in range(count):

        @pl.when(step // 2 == a)
        def _():
            for k in range(4):
                rows = pl.ds(pl.multiple_of(lax.rem(z - k + 4, 4) * unit, 16), unit)
                out_ref[0, rows] = ins[a][k * unit : (k + 1) * unit].astype(f32)


def place_relative(parts, out_map, out_shape, before, deps=()):
    values = [v for v, _ in parts]
    count, width = len(parts), values[0].shape[1]
    quarter = values[0].shape[0] // 2
    where = jnp.stack([m for _, marks in parts for m in marks] + [lax.axis_index(Z)])
    return invoke(
        partial(place_kernel, count, quarter),
        values + [before],
        deps,
        scalars=(where.astype(jnp.int32),),
        grid=(2 * count,),
        in_specs=[
            pl.BlockSpec((quarter, width), lambda i, w, a=a: (jnp.clip(i - 2 * a, 0, 1), 0))
            for a in range(count)
        ]
        + [pl.BlockSpec(memory_space=pl.ANY)],
        out_specs=pl.BlockSpec((1, quarter, width), lambda i, w: out_map(w[i])),
        out_shape=jax.ShapeDtypeStruct(out_shape, f32),
        aliases={1 + count: 0},
        name="place",
        us=2,
    )


def spread_kernel(z_first, in_ref, *refs):
    down_ref, up_ref = refs[-2:]
    unit = QUARTER // 4
    for z in range(4):
        rows = slice(z * unit, (z + 1) * unit)
        down_ref[0, rows] = (in_ref[0, z, 0] if z_first else in_ref[0, 0, z]).astype(f32)
        up_ref[0, rows] = (in_ref[0, z, 1] if z_first else in_ref[0, 1, z]).astype(f32)


def spread_turned_kernel(where_ref, in_ref, down_ref, up_ref):
    unit = QUARTER // 4
    for k in range(4):
        rows = pl.ds(pl.multiple_of(lax.rem(where_ref[2] - k + 4, 4) * unit, 16), unit)
        down_ref[0, rows] = in_ref[0, k, 0].astype(f32)
        up_ref[0, rows] = in_ref[0, k, 1].astype(f32)


def place_gathered(blocks, layer, where, deps=()):
    unit, width = blocks.shape[-2:]
    hidden = blocks.size // width // 2
    return invoke(
        spread_turned_kernel,
        (blocks,),
        deps,
        scalars=(where,),
        grid=(8,),
        in_specs=[
            pl.BlockSpec((1, 4, 2, unit, width), lambda i, w: (i % 4 * 2 + i // 4, 0, 0, 0, 0))
        ],
        out_specs=[
            pl.BlockSpec((1, QUARTER, width), lambda i, w: (layer, i, 0)),
            pl.BlockSpec((1, QUARTER, TILE), lambda i, w: (layer, i % 2, i // 2)),
        ],
        out_shape=[
            jax.ShapeDtypeStruct((2, hidden, width), f32),
            jax.ShapeDtypeStruct((2, width, hidden), f32),
        ],
        name="spread",
        us=2,
    )


def place_ordered(rows, layer, before=None, z_first=False, deps=()):
    width = rows.shape[-1]
    hidden = rows.size // width // 2
    inner = (4, 2) if z_first else (2, 4)
    rows = rows.reshape((hidden // QUARTER,) + inner + (QUARTER // 4, width))
    return invoke(
        partial(spread_kernel, z_first),
        [rows] + list(before or ()),
        deps,
        grid=(hidden // QUARTER,),
        in_specs=[pl.BlockSpec((1,) + rows.shape[1:], lambda i: (i, 0, 0, 0, 0))]
        + [pl.BlockSpec(memory_space=pl.ANY)] * len(before or ()),
        out_specs=[
            pl.BlockSpec((1, QUARTER, width), lambda i: (layer, i, 0)),
            pl.BlockSpec((1, QUARTER, TILE), lambda i: (layer, i % 2, i // 2)),
        ],
        out_shape=[
            jax.ShapeDtypeStruct((2, hidden, width), f32),
            jax.ShapeDtypeStruct((2, width, hidden), f32),
        ],
        aliases={1: 0, 2: 1} if before else {},
        name="spread",
        us=2,
    )


def finish_kernel(in_ref, out_ref, q2_ref, qkv_ref, small_ref, flat):
    width = out_ref.shape[2]
    size = in_ref.shape[2]
    for w in range(8):
        for two in range(2):
            for z in range(4):
                at = ((w * 2 + two) * 4 + z) * size
                flat[at : at + size] = in_ref[w * 4 + z, two].astype(f32)
    half = flat.shape[0] // 2
    out_ref[1] = flat[:width]
    q2_ref[...] = flat[width : 2 * width]
    out_ref[0] = flat[half : half + width]
    qkv_ref[:, :width] = flat[half + width : half + 2 * width]
    qkv_ref[:, width:] = flat[2 * width : 2 * width + 128].T
    small_ref[...] = flat[2 * width + 128 : half]


def finish_call(blocks):
    width = blocks.shape[-1]
    rows = blocks.size // width
    shapes = [(2, width, width), (width, width), (width, width + 128), (EXTRA - 128, width)]
    return invoke(
        finish_kernel,
        (blocks,),
        (),
        grid=(1,),
        in_specs=[full_spec(blocks.shape)],
        out_specs=[full_spec(v) for v in shapes],
        out_shape=[jax.ShapeDtypeStruct(v, f32) for v in shapes],
        scratch=[pltpu.VMEM((rows, width), f32)],
        name="finish",
        us=6,
    )


def rotary_tables(positions):
    half_rot = ROT // 2
    inverse = BASE ** (-(jnp.arange(half_rot, dtype=f32) * 2.0 / ROT))
    angles = positions.astype(f32).reshape(-1, 1) * inverse
    cos, sin = jnp.cos(angles), jnp.sin(angles)
    zero = jnp.zeros_like(sin)
    rest = jnp.zeros((cos.shape[0], 64 - ROT), f32)
    head = [
        jnp.concatenate([cos, cos, rest + 1.0], axis=-1),
        jnp.concatenate([-sin, zero, rest], axis=-1),
        jnp.concatenate([zero, sin, rest], axis=-1),
    ]
    return jnp.stack([jnp.concatenate([h, h], axis=-1) for h in head])


def local(
    hidden_in,
    positions,
    cotangent,
    norm_gains,
    norm_biases,
    w_qkv,
    b_qkv,
    w_q2,
    b_q2,
    w_out,
    w_up,
    b_up,
    w_down,
    out_bias,
):
    seqs, group, width = hidden_in.shape
    tokens = seqs * group
    hidden = w_up.shape[2]
    y, x, z, core = (lax.axis_index(a) for a in ("b0", "b1", Z, C))
    core_row = core.reshape(1).astype(jnp.int32)
    where = jnp.stack([y, x, z, core]).astype(jnp.int32)
    direct = square()
    x1 = hidden_in.reshape(tokens, width)
    g2 = cotangent.reshape(tokens, width)
    tab = rotary_tables(positions)

    na1, nm1, q1, kv_own = first_call(x1, norm_gains[0], norm_biases[0], w_qkv, b_qkv, tab, group)
    if direct:
        got = turns(lambda k: kv_own)
        y1, act1, slope1 = mlp_fwd_call(nm1, w_up, b_up, w_down, 0)
        mine = join([v[None] for v in (kv_own, *got)], (0,), where, (y1,))[0]
        theirs = swap(mine, C)
        kv = (mine, theirs)
        back = (z - jnp.arange(4)) % 4 * 2
        order = jnp.concatenate([back + core, back + 1 - core])
        do2 = back_call(g2, w_out, 1, (mine,))
    else:
        kv = (lax.all_gather(kv_own, (Z, C), axis=0, tiled=False),)
        order = jnp.arange(kv[0].shape[0])
        y1, act1, slope1 = mlp_fwd_call(nm1, w_up, b_up, w_down, 0)
        do2 = back_call(g2, w_out, 1)
    first = jnp.concatenate([((z * 2 + core) * group).reshape(1), order]).astype(jnp.int32)
    att1, lse1 = attend_call(first, q1, kv, (do2,))
    x2, na2, nm2, q2 = middle_call(
        att1, x1, y1, w_out, out_bias[0:1], norm_gains[1], norm_biases[1], w_q2, b_q2, tab
    )
    y2, dnm2, send, bup_send = mlp_back_call(core_row, nm2, g2, w_up, w_down, 1, b_up=b_up)
    got = swap(send.reshape(hidden, width), C)
    y2, dnm2, keep, bup_keep = mlp_back_call(
        core_row, nm2, g2, w_up, w_down, 1, b_up=b_up, before=(y2, dnm2)
    )
    keep = keep.reshape(hidden, width)

    def in_order(own, other):
        both = jnp.concatenate([own, other], axis=0)
        return jnp.where(core == 0, both, jnp.concatenate([other, own], axis=0)).reshape(-1, width)

    bup2 = in_order(bup_keep, bup_send)

    def swaps(one, two, axes):
        return swap(one, axes[0]), swap(two, axes[1])

    wait = ()
    if direct:
        one_send, one, two_send, two = sum_cores(keep, got, where)
        one_got, two_got = swaps(one_send, two_send, ("b1", "b0"))
        wait = (one,)
    else:
        mlp2 = add_low(keep, got)
    att2, lse2 = attend_call(first, q2, kv, wait)
    back2 = attend_back_call(first, q2, kv, att2, do2, lse2, tab, 0)
    if direct:
        one_send, one, two_send, two = sum_first(one, one_got, two, two_got, where, (back2[0],))
        one_got, two_got = swaps(one_send, two_send, ("b0", "b1"))
        wait = (one,)
    dq2, dkv2 = attend_back_call(first, q2, kv, att2, do2, lse2, tab, 1, before=back2, deps=wait)
    if direct:
        parts = sum_second(one, one_got, two, two_got, where, (dq2,))
        ahead = turns(lambda k: parts[k])
        wait = (parts[0],)
    hidden_out, early, g1, do1, small2 = turn_call(
        x2, y2, att2, att1, g2, na2, dq2, dnm2, w_out, w_q2, out_bias[1:2], norm_gains[1], deps=wait
    )
    dnm1, send, bup_send = mlp_back_call(
        core_row, nm1, g1, w_up, w_down, 0, kept=(act1, slope1)
    )
    got = swap(send.reshape(hidden, width), C)
    wait = ()
    if direct:
        mlp2 = sum_third([parts[0]] + ahead, where, (dnm1,))
        wait = (mlp2,)
        ahead = turns(lambda k: mlp2)
    dnm1, keep, bup_keep = mlp_back_call(
        core_row, nm1, g1, w_up, w_down, 0, kept=(act1, slope1), before=(dnm1,), deps=wait
    )
    keep = keep.reshape(hidden, width)
    bup1 = in_order(bup_keep, bup_send)
    if direct:
        one_send, one, two_send, two = sum_cores(keep, got, where)
        one_got, two_got = swaps(one_send, two_send, ("b1", "b0"))
        mlp2 = join([v[None] for v in (mlp2, *ahead)], (0,), where, (one,))[0]
        wait = (mlp2,)
        mlp2 = lax.all_gather(mlp2, B + (C,), axis=0, tiled=False)
    dq1, dkv1 = attend_back_call(
        first, q1, kv, att1, do1, lse1, tab, None, dkv2, deps=wait + (dnm1,)
    )
    if direct:
        one_send, one, two_send, two = sum_first(one, one_got, two, two_got, where, (dq1,))
        one_got, two_got = swaps(one_send, two_send, ("b0", "b1"))
    low = dkv1.astype(bf16)
    if direct:
        low = low.reshape(4, 2, group, -1)
        at = lambda c: lax.dynamic_index_in_dim(low, c, 1, keepdims=False)
        dkv_got = swap(at(1 - core), C)
        block = (1,) + low.shape[2:]
        dkv_parts = combine(
            [
                (
                    [
                        [
                            (
                                low.reshape((8,) + low.shape[2:]),
                                block,
                                lambda i, w, k=k: (lax.rem(w[2] + k, 4) * 2 + w[3], 0, 0),
                            ),
                            (dkv_got, block, lambda i, w, k=k: (lax.rem(w[2] + k, 4), 0, 0)),
                        ]
                    ],
                    block,
                    lambda i, w: (0, 0, 0),
                    block,
                )
                for k in range(4)
            ],
            where,
            (one,),
            name="sum_kv",
        )
        dkv_got = turns(lambda k: dkv_parts[k])
        dkv = sum_third([dkv_parts[0]] + dkv_got, where)[0]
        parts = sum_second(one, one_got, two, two_got, where, (dkv,))
        ahead = turns(lambda k: parts[k])
        wait = (parts[0],)
    else:
        dkv = lax.psum_scatter(low, (Z, C), scatter_dimension=0, tiled=True)
        mlp1 = add_low(keep, got)
        wait = ()
    grad_input, late_send, late = last_call(
        core_row, x1, g1, na1, dq1, dkv, dnm1, w_qkv, norm_gains[0], tab, small2, bup1, bup2, early, deps=wait
    )
    late_got = swap(late_send, C)

    if direct:
        both = sum_third([parts[0]] + ahead, where, (grad_input,), us=400)
        ahead = turns(lambda k: both)
        l1_send, l1, l2_send, l2 = sum_cores(late, late_got, where, (both,), us=1)
        l1_got, l2_got = swaps(l1_send, l2_send, ("b1", "b0"))
        l1_send, l1, l2_send, l2 = sum_first(l1, l1_got, l2, l2_got, where, us=1)
        l1_got, l2_got = swaps(l1_send, l2_send, ("b0", "b1"))
        one, two = join([both] + ahead, (0, 1), where, (l1,))
        one_got, two_got = swaps(one, two, ("b0", "b1"))
        parts = sum_second(l1, l1_got, l2, l2_got, where, (one,), us=1)
        late_ahead = turns(lambda k: parts[k])
        late = sum_third([parts[0]] + late_ahead, where, (mlp2,))
        outs = gather_blocks(late)
        one_near, two_near = (
            join([v[None], g[None]], (0,), where, (late,))[0].reshape(-1, width)
            for v, g in ((one, one_got), (two, two_got))
        )
        one_far, two_far = swaps(one_near, two_near, ("b1", "b0"))
        one_near_got, two_near_got = swap(one_near, C), swap(two_near, C)
        grad_down, grad_up = place_gathered(mlp2, 1, where, (one_near, two_near))
        mark = lambda c, v, u: c * 4 + v * 2 + u
        down_map = lambda w: (0, w, 0)
        up_map = lambda w: (0, w % 2, w // 2)

        def down_marks(c, far):
            u = 1 - x if far else x
            return (mark(c, y, u), mark(c, 1 - y, u))

        def up_marks(c, far):
            v = 1 - y if far else y
            return (mark(c, v, x), mark(c, v, 1 - x))

        def put(down, up, one, two, far, cores):
            down = place_relative(
                [(o, down_marks(c, far)) for o, c in zip(one, cores)], down_map, down.shape, down
            )
            up = place_relative(
                [(t, up_marks(c, far)) for t, c in zip(two, cores)], up_map, up.shape, up
            )
            return down, up

        near_one, near_two = (one_near, one_near_got), (two_near, two_near_got)
        grad_down, grad_up = put(grad_down, grad_up, near_one, near_two, False, (core, 1 - core))
        one_far, two_far = relay((one_far, two_far), where, (grad_down, grad_up))
        one_far_got, two_far_got = swap(one_far, C), swap(two_far, C)
        grad_down, grad_up = put(grad_down, grad_up, (one_far,), (two_far,), True, (core,))
        grad_down, grad_up = put(
            grad_down, grad_up, (one_far_got,), (two_far_got,), True, (1 - core,)
        )
    else:
        mlp2 = gather_offloaded(reduce_offloaded(mlp2))
        placed = place_ordered(mlp2, 1)
        grad_down, grad_up = place_ordered(gather_offloaded(reduce_offloaded(mlp1)), 0, placed)
        outs = gather_offloaded(reduce_offloaded(add_low(late, late_got)))
        outs = outs.reshape(8, 2, 4, -1, width).transpose(0, 2, 1, 3, 4).reshape(32, 2, -1, width)
    grad_out, grad_q2, grad_qkv, small = finish_call(outs)
    one, two = small[0:8], small[8:16]
    ups = hidden // width
    grad_up_bias = jnp.stack([small[16 : 16 + ups].reshape(-1), small[16 + ups : 16 + 2 * ups].reshape(-1)])
    grad_gains = jnp.stack([one[0:2], two[0:2]])
    grad_biases = jnp.stack([one[2:4], two[2:4]])
    grad_qkv_bias = jnp.concatenate([one[4], one[5, :128]])
    grad_out_bias = jnp.stack([two[6], two[4]])
    return (
        hidden_out.reshape(seqs, group, width),
        grad_input.reshape(seqs, group, width),
        grad_gains,
        grad_biases,
        grad_qkv,
        grad_qkv_bias,
        grad_q2,
        two[5],
        grad_out,
        grad_up,
        grad_up_bias,
        grad_down,
        grad_out_bias,
    )


def solution(mesh):
    batch, seq = mesh.shape["batch"], mesh.shape["seq"]
    fine = jax.sharding.Mesh(
        mesh.devices.reshape(2, batch // 2, seq // 2, 2), ("b0", "b1", "z", "c")
    )
    rows = P(B, (Z, C), None)
    return jax.shard_map(
        local,
        mesh=fine,
        in_specs=(rows, P(B, (Z, C)), rows) + (P(),) * 11,
        out_specs=(rows, rows) + (P(),) * 11,
        check_vma=False,
    )
```
